128 devices in a mesh: gx: 8 (over y, z_lo), gy: 16 (over z_hi, x, core).
Axes of the slice: x: 4, y: 4, z: 4 (z_hi: 2, z_lo: 2; z = z_hi * 2 + z_lo), core: 2. Of those that a mesh axis runs over, the one named last changes fastest.
Arguments:
- velocity: float32 [3, 96, 448, 1024], P(None, 'gx', 'gy'), may hold values from -12 to 12
- viscosity: float32 [96, 448, 1024], P('gx', 'gy'), may hold values from 0.5 to 4
- cells: int32 [3, 131072], P(None, ('gx', 'gy')), may hold values from 0 to 1023, as said below
- offsets: float32 [3, 131072], P(None, ('gx', 'gy')), may hold values from 0 to 1
- forces: float32 [3, 131072], P(None, ('gx', 'gy')), may hold values from -48 to 48
- owners: int32 [131072, 1], P(('gx', 'gy')), may hold values from 0 to 127; in each aligned block of 1024 rows (0 to 1023, 1024 to 2047, ...) at most 16 rows name the same one
Outputs:
- new_velocity: float32 [3, 96, 448, 1024], P(None, 'gx', 'gy')
- marker_velocity: float32 [3, 131072], P(None, ('gx', 'gy'))
The draws below stay inside these ranges and needn't reach their ends.
Inputs may be any that keep to these rules, and one draw needn't show every extreme that they name: cells[0] lies below 12, cells[1] below 28, cells[2] below 1024. `owners`: among one device's 1024 markers at most 16 have the same owner, and in every draw some owner is named exactly 16 times by one device's markers.
All inputs are finite; a program needn't handle non-finite values.
Results may differ from the reference program's by a relative error of at most 0.000096.
Values sent between devices are 32-bit elements; how exact they have to be, the bound alone decides.
No kernel may reach another device: no remote copies, remote signals or barrier semaphores. Data moves between devices by JAX's collectives and lax.ppermute only.
A program may use at most 128 MiB of HBM per device.

```python
import math
import jax
import jax.numpy as jnp
import numpy as np

CX = 12
CY = 28
NZ = 1024
M_DEV = 1024
SWEEPS = 3
NX = 96
NY = 448
MARKERS = 131072
CAP = 16
N_GY = 16
DEVICES = 128


def draw_cells(key, part):
    upper = jnp.array([[CX], [CY], [NZ]], jnp.int32)
    return jax.random.randint(key, (3, MARKERS), 0, upper, dtype=jnp.int32)


def block_levels(own_key, extent, cuts, smallest, largest):
    loudness, own = 1.0, jax.random.fold_in(own_key, 6)
    for axis_at, blocks in cuts:
        draws = jnp.exp(jax.random.uniform(jax.random.fold_in(own, axis_at), (blocks,), jnp.float32, smallest / len(cuts), largest / len(cuts)))
        loudness = loudness * jnp.repeat(draws, extent[axis_at] // blocks).reshape([-1 if axis == axis_at else 1 for axis in range(len(extent))])
    return loudness


def assign_block(key, own, number, rows, amount, top, bound, skew):
    order = jax.random.permutation(key, amount)
    heavy_load, ordinary = portions_of(amount, rows * top, bound, skew, True), portions_of(amount, rows * top, bound, skew, False)
    places = jnp.arange(amount)

    def named(tallies, turn):
        used = int((tallies > 0).sum())
        fixed = max(1, used // 4)
        moved = fixed + (places - fixed + turn * (used - fixed)) % max(1, amount - fixed)
        return jnp.zeros((amount,), jnp.int32).at[order[jnp.where(places < fixed, places, moved)]].set(jnp.asarray(tallies, jnp.int32))

    tallies = jnp.where(number % 4 == 0, named(heavy_load, number // 4), named(ordinary, number - number // 4 - 1))
    mixed = jax.random.permutation(jax.random.fold_in(own, 3), amount)
    donor, taker = mixed[0:amount // 2 * 2:2], mixed[1:amount // 2 * 2:2]
    margin = jnp.minimum(tallies[donor] - 1, bound - tallies[taker]) // 2
    margin = jnp.where((donor == order[0]) | (taker == order[0]) | (tallies[taker] == 0), 0, jnp.maximum(margin, 0))
    moved = jax.random.randint(jax.random.fold_in(own, 4), (amount // 2,), 0, 1 << 20) % (margin + 1)
    tallies = tallies.at[donor].add(-moved).at[taker].add(moved)
    labels = jnp.searchsorted(jnp.cumsum(tallies), jnp.arange(rows * top), side="right").astype(jnp.int32)
    grid = labels.reshape(top, rows).T
    grid = grid[jax.random.permutation(jax.random.fold_in(own, 1), rows)]
    turn = jax.random.randint(jax.random.fold_in(own, 2), (rows, 1), 0, top)
    return jnp.take_along_axis(grid, (jnp.arange(top)[None, :] + turn) % top, axis=1)


def portions_of(count, total, limit, slope, full):
    weights = [(1 << 20) // math.isqrt(grade ** slope) + 1 for grade in range(1, count + 1)]
    largest = limit if full else min(limit, max(-(-total // count), total * weights[0] // sum(weights)))
    least = 1 if total - largest >= count - 1 else 0
    counts, rest = [largest] + [least] * (count - 1), total - largest - least * (count - 1)
    while rest > 0:
        free = [i for i in range(1, count) if counts[i] < largest] or [i for i in range(1, count) if counts[i] < limit]
        whole, left = sum([weights[i] for i in free]), rest
        for i in free:
            more = min(limit - counts[i], max(1, left * weights[i] // whole), rest)
            counts[i] = counts[i] + more
            rest = rest - more
    return np.array(counts)


def bell_draw(key, shape, spread, reach, cuts=(), kind=jnp.bfloat16):
    level = block_levels(key, shape, cuts, -0.22, 0.18) if cuts else 1.0
    drawn = jax.random.normal(key, shape, jnp.float32) * spread * level
    return jnp.minimum(jnp.maximum(drawn, -reach), reach).astype(kind)


def setup_inputs(seed: int = 0) -> dict:
    key_of = jax.random.split(jax.random.key(seed), 7)
    velocity = bell_draw(key_of[0], (3, NX, NY, NZ), 2.0, 12.0, ((1, 8), (2, 16)), jnp.float32)
    viscosity = jnp.clip(jnp.exp(math.log(4.0) - 2.0794415 * jax.random.uniform(key_of[1], (NX, NY, NZ), jnp.float32) ** block_levels(key_of[1], (NX, NY, NZ), ((0, 8), (1, 16)), -0.2, 0.2)), 0.5, 4.0)
    cells = draw_cells(jax.random.fold_in(key_of[6], 71), 0)
    offsets = jnp.clip(1.0 * jax.random.uniform(key_of[3], (3, MARKERS), jnp.float32) ** block_levels(key_of[3], (3, MARKERS), ((1, 128),), -0.2, 0.2), 0.0, 1.0)
    forces = bell_draw(key_of[4], (3, MARKERS), 8.0, 48.0, ((1, 128),), jnp.float32)
    owners_keys = jax.random.split(jax.random.fold_in(key_of[5], 1), MARKERS // M_DEV)
    owners_turns = jax.random.permutation(jax.random.fold_in(key_of[5], 3), MARKERS // M_DEV)
    owners = jax.vmap(lambda own, number: assign_block(jax.random.fold_in(key_of[5], 2), own, number, M_DEV, DEVICES, 1, CAP, 2))(owners_keys, owners_turns).reshape((MARKERS, 1))
    return dict(velocity=velocity, viscosity=viscosity, cells=cells, offsets=offsets, forces=forces, owners=owners)


def kernel_weights(frac):
    root = jnp.sqrt(1.0 + 4.0 * frac - 4.0 * frac * frac)
    return jnp.stack([(3.0 - 2.0 * frac - root) / 8.0, (3.0 - 2.0 * frac + root) / 8.0, (1.0 + 2.0 * frac + root) / 8.0, (1.0 + 2.0 * frac - root) / 8.0])

def reference(velocity, viscosity, cells, offsets, forces, owners):
    owner = owners[:, 0]
    base_x = owner // N_GY * CX + cells[0]
    base_y = owner % N_GY * CY + cells[1]
    base_z = cells[2]
    weight_x = kernel_weights(offsets[0])
    weight_y = kernel_weights(offsets[1])
    weight_z = kernel_weights(offsets[2])
    flat = jnp.zeros((3, NX * NY * NZ), jnp.float32)
    entries = []
    for i in range(4):
        for j in range(4):
            for k in range(4):
                index = (((base_x - 1 + i) % NX * NY + (base_y - 1 + j) % NY) * NZ + (base_z - 1 + k) % NZ).astype(jnp.int32)
                weight = weight_x[i] * weight_y[j] * weight_z[k]
                entries.append((index, weight))
                flat = flat.at[:, index].add(forces * weight[None, :])
    rhs = velocity + flat.reshape(3, NX, NY, NZ)
    field = rhs
    for sweep in range(SWEEPS):
        beside_all = jnp.roll(field, -1, 1) + jnp.roll(field, 1, 1)
        beside_all = beside_all + jnp.roll(field, -1, 2) + jnp.roll(field, 1, 2)
        beside_all = beside_all + jnp.roll(field, -1, 3) + jnp.roll(field, 1, 3)
        field = (rhs + viscosity * beside_all) / (1.0 + 6.0 * viscosity)
    values = field.reshape(3, NX * NY * NZ)
    speeds = jnp.zeros((3, owner.shape[0]), jnp.float32)
    for index, weight in entries:
        speeds = speeds + values[:, index] * weight[None, :]
    return (field, speeds)
```

```python
import functools

import jax
import jax.numpy as jnp
from jax import lax
from jax.experimental import pallas as pl
from jax.experimental.pallas import tpu as pltpu
from jax.sharding import PartitionSpec as P

F32 = jnp.float32
BF16 = jnp.bfloat16
I32 = jnp.int32
LIMIT = 60 * 1024 * 1024
CAP = 16
HALO = 3
PAD = 8
YE = 40


def split3(x):
    hi = x.astype(BF16).astype(F32)
    rest = x - hi
    mid = rest.astype(BF16).astype(F32)
    return hi, mid, rest - mid


def split2(x):
    hi = x.astype(BF16)
    return hi, (x - hi.astype(F32)).astype(BF16)


def nn(a, b):
    return lax.dot_general(a, b, (((1,), (0,)), ((), ())), preferred_element_type=F32)


def nt(a, b):
    return lax.dot_general(a, b, (((1,), (1,)), ((), ())), preferred_element_type=F32)


def tn(a, b):
    return lax.dot_general(a, b, (((0,), (0,)), ((), ())), preferred_element_type=F32)


def iota(shape, dim):
    return lax.broadcasted_iota(I32, shape, dim)


def vmem():
    return pl.BlockSpec(memory_space=pltpu.VMEM)


def smem():
    return pl.BlockSpec(memory_space=pltpu.SMEM)


def params():
    return pltpu.CompilerParams(vmem_limit_bytes=LIMIT)


def cost(flops, size):
    return pl.CostEstimate(flops=flops, bytes_accessed=size, transcendentals=0)


def pack_kernel(owner_ref, cells_ref, offsets_ref, forces_ref, out_ref, rank_ref):
    markers = owner_ref.shape[1]
    devices = out_ref.shape[0]
    owner = owner_ref[...]
    before = (iota((128, 128), 0) < iota((128, 128), 1)).astype(BF16)
    running = jnp.zeros((devices, 1), F32)
    ranks = []
    hots = []
    for g in range(markers // 128):
        hot = (iota((devices, 128), 0) == owner[:, g * 128 : (g + 1) * 128]).astype(F32)
        within = nn(hot.astype(BF16), before)
        ranks.append(jnp.sum(hot * (within + running), axis=0, keepdims=True))
        running = running + jnp.sum(hot, axis=1, keepdims=True)
        hots.append(hot.astype(BF16))
    rank = jnp.concatenate(ranks, axis=1).astype(I32)
    rank_ref[...] = rank
    onehot = jnp.concatenate(hots, axis=1)
    payload = jnp.concatenate(
        [
            cells_ref[...].astype(F32),
            offsets_ref[...],
            forces_ref[...],
            jnp.ones((1, markers), F32),
            jnp.zeros((6, markers), F32),
        ],
        axis=0,
    )
    parts = split3(payload)
    total = None
    for part in parts:
        rows = jnp.concatenate([jnp.where(rank == k, part, 0.0) for k in range(CAP)], axis=0)
        term = nt(onehot, rows.astype(BF16))
        total = term if total is None else total + term
    out_ref[...] = total


def pack(owner_row, cells, offsets, forces, devices):
    markers = owner_row.shape[1]
    return pl.pallas_call(
        pack_kernel,
        out_shape=(
            jax.ShapeDtypeStruct((devices, CAP * 16), F32),
            jax.ShapeDtypeStruct((1, markers), I32),
        ),
        in_specs=[vmem()] * 4,
        out_specs=(vmem(), vmem()),
        compiler_params=params(),
        cost_estimate=cost(4 * 10**8, 300_000),
        name="pack",
    )(owner_row, cells, offsets, forces)


def place_block(flat, start, count):
    return (flat == start + iota((count, flat.shape[1]), 0)).astype(F32).astype(BF16)


def sort_kernel(depth, rec_ref, list_ref, rank_ref, keys, pieces):
    devices = rec_ref.shape[0]
    slots = devices * CAP
    rec = rec_ref[...]
    flipped = rec.T
    empty = float(depth * 4096)

    def key_of(z, valid, index):
        low = jnp.where(z < 0.5, float(depth - 1), z - 1.0)
        return jnp.where(valid > 0.5, low * float(slots), empty) + index

    rows = []
    lane = iota((devices, 128), 1)
    for k in range(CAP):
        at = k * 16
        column = key_of(
            rec[:, at + 2 : at + 3],
            rec[:, at + 9 : at + 10],
            (iota((devices, 1), 0) + k * devices).astype(F32),
        )
        keys[k] = jnp.broadcast_to(column, (devices, devices))
        rows.append(
            key_of(
                flipped[at + 2 : at + 3, :],
                flipped[at + 9 : at + 10, :],
                (iota((1, devices), 1) + k * devices).astype(F32),
            )
        )
        half = rec[:, (k // 8) * 128 : (k // 8 + 1) * 128]
        turned = half if k % 8 == 0 else pltpu.roll(half, 128 - (k % 8) * 16, 1)
        hi, mid, lo = split3(turned)
        joined = jnp.where(
            lane < 16,
            hi,
            jnp.where(
                lane < 32, pltpu.roll(mid, 16, 1), jnp.where(lane < 48, pltpu.roll(lo, 32, 1), 0.0)
            ),
        )
        pieces[k * devices : (k + 1) * devices, :] = joined.astype(BF16)
    ranks = []
    for k in range(CAP):
        row = rows[k]

        def count(other, acc):
            return acc + jnp.where(keys[other] < row, 1.0, 0.0)

        acc = lax.fori_loop(0, CAP, count, jnp.zeros((devices, devices), F32))
        ranks.append(jnp.sum(acc, axis=0, keepdims=True).astype(I32))
    rank_ref[...] = jnp.concatenate(ranks, axis=0)
    flat = jnp.concatenate(ranks, axis=1)
    block = 256
    for b in range(slots // block):
        moved = nn(place_block(flat, b * block, block), pieces[...]).T
        rows = moved[0:16] + moved[16:32] + moved[32:48]
        z = rows[2:3]
        low = jnp.where(z < 0.5, float(depth - 1), z - 1.0)
        list_ref[:, b * block : (b + 1) * block] = jnp.where(
            iota((16, block), 0) == 2, low, rows
        )
    lanes = iota((1, 128), 1)
    meta = jnp.zeros((1, 128), F32)
    chunks = jnp.zeros((1, 1), F32)
    for c in range(slots // 128):
        low = list_ref[2:3, c * 128 : (c + 1) * 128]
        valid = list_ref[9:10, c * 128 : (c + 1) * 128] > 0.5
        first = jnp.min(
            jnp.where(valid, jnp.floor(low / 128.0), 1000.0), axis=1, keepdims=True
        )
        last = jnp.max(
            jnp.where(valid, jnp.floor((low + 3.0) / 128.0), -1.0), axis=1, keepdims=True
        )
        number = jnp.maximum(last - first + 1.0, 0.0)
        chunks = chunks + jnp.where(number > 0.5, 1.0, 0.0)
        meta = meta + jnp.where(lanes == c, first, 0.0) + jnp.where(lanes == 16 + c, number, 0.0)
    meta = meta + jnp.where(lanes == 32, chunks, 0.0)
    list_ref[10:11, 0:128] = meta


def sort(received, depth):
    devices = received.shape[0]
    slots = devices * CAP
    return pl.pallas_call(
        functools.partial(sort_kernel, depth),
        out_shape=(
            jax.ShapeDtypeStruct((16, slots), F32),
            jax.ShapeDtypeStruct((CAP, devices), I32),
        ),
        in_specs=[vmem()],
        out_specs=(vmem(), vmem()),
        scratch_shapes=[
            pltpu.VMEM((CAP, devices, devices), F32),
            pltpu.VMEM((slots, 128), BF16),
        ],
        compiler_params=params(),
        cost_estimate=cost(2 * 10**9, 300_000),
        name="sort",
    )(received)


def bump(frac):
    root = jnp.sqrt(1.0 + 4.0 * frac - 4.0 * frac * frac)
    return (
        (3.0 - 2.0 * frac - root) / 8.0,
        (3.0 - 2.0 * frac + root) / 8.0,
        (1.0 + 2.0 * frac + root) / 8.0,
        (1.0 + 2.0 * frac - root) / 8.0,
    )


def tent(first, weights, count, modulus=None):
    rows = iota((count, 128), 0)
    table = jnp.zeros((count, 128), F32)
    for i in range(4):
        table = table + jnp.where(rows == first + i, weights[i], 0.0)
    return table


def planar_of(ref, at, lanes, shift_x, rows_x, shift_y, rows_y):
    part = ref[at, :, lanes]
    x = part[0:1].astype(I32) + shift_x
    y = part[1:2].astype(I32) + shift_y
    table_x = tent(x, bump(part[3:4]), -(-rows_x // 8) * 8)
    table_y = tent(y, bump(part[4:5]), rows_y)
    planar = jnp.concatenate([table_x[r : r + 1] * table_y for r in range(rows_x)], axis=0)
    return part, planar


def window_of(low, weights, window, depth):
    rows = iota((128, 128), 0) + window * 128
    table = jnp.zeros((128, 128), F32)
    for i in range(4):
        target = jnp.bitwise_and(low + i, depth - 1)
        table = table + jnp.where(rows == target, weights[i], 0.0)
    return table


def spread_kernel(size_x, size_y, meta, mid_ref, low_ref, high_ref, out_ref):
    depth = out_ref.shape[3]
    windows = depth // 128

    def clear(e, carry):
        for c in range(3):
            out_ref[c, e] = jnp.zeros((YE, depth), F32)
        return carry

    lax.fori_loop(0, size_x + 2 * HALO, clear, 0)
    rows_of = {-1: (0, 6), 0: (2, 16), 1: (14, 4)}
    cols_of = {-1: (0, 16), 0: (0, YE), 1: (32, 8)}
    for dy, ref in ((0, mid_ref), (-1, low_ref), (1, high_ref)):
        for dx in (-1, 0, 1):
            index = (dy + 1) * 3 + dx + 1
            e0, rows = rows_of[dx]
            s0, cols = cols_of[dy]

            def chunk_step(chunk, carry):
                lanes = pl.ds(pl.multiple_of(chunk * 128, 128), 128)
                part, planar = planar_of(
                    ref,
                    dx + 1,
                    lanes,
                    HALO - 1 + size_x * dx - e0,
                    rows,
                    PAD - 1 + size_y * dy - s0,
                    cols,
                )
                hi, lo = split2(planar)
                left = jnp.concatenate([hi, lo, hi, lo], axis=1)
                low = part[2:3].astype(I32)
                weights = bump(part[5:6])
                first = meta[index, chunk]

                def window_step(turn, inner):
                    window = jnp.bitwise_and(first + turn, windows - 1)
                    table = window_of(low, weights, window, depth)
                    pushed = jnp.concatenate([table * part[6 + c : 7 + c] for c in range(3)], axis=0)
                    big, small = split2(pushed)
                    right = jnp.concatenate([big, big, small, small], axis=1)
                    sums = nt(left, right)
                    at = pl.ds(pl.multiple_of(window * 128, 128), 128)
                    for c in range(3):
                        for r in range(rows):
                            out_ref[c, e0 + r, s0 : s0 + cols, at] += sums[
                                r * cols : (r + 1) * cols, c * 128 : (c + 1) * 128
                            ]
                    return inner

                lax.fori_loop(0, meta[index, 16 + chunk], window_step, 0)
                return carry

            lax.fori_loop(0, meta[index, 32], chunk_step, 0)


def spread(meta, mid, low, high, size_x, size_y, depth):
    return pl.pallas_call(
        functools.partial(spread_kernel, size_x, size_y),
        out_shape=jax.ShapeDtypeStruct((3, size_x + 2 * HALO, YE, depth), F32),
        in_specs=[smem(), vmem(), vmem(), vmem()],
        out_specs=vmem(),
        compiler_params=params(),
        cost_estimate=cost(10**10, 10**7),
        name="spread",
    )(meta, mid, low, high)


def faces_kernel(vel_ref, visc_ref, x_up, x_down, y_up, y_down):
    size_x, size_y = visc_ref.shape[0], visc_ref.shape[1]
    for l in range(HALO):
        for c in range(3):
            r = c * HALO + l
            x_up[r * size_y : (r + 1) * size_y, :] = vel_ref[c, size_x - HALO + l]
            x_down[r * size_y : (r + 1) * size_y, :] = vel_ref[c, l]
    for l in range(HALO - 1):
        r = 3 * HALO + l
        x_up[r * size_y : (r + 1) * size_y, :] = visc_ref[size_x - HALO + 1 + l]
        x_down[r * size_y : (r + 1) * size_y, :] = visc_ref[l]
    for x in range(size_x):
        for c in range(3):
            r = (c * size_x + x) * HALO
            y_up[r : r + HALO, :] = vel_ref[c, x, size_y - HALO : size_y, :]
            y_down[r : r + HALO, :] = vel_ref[c, x, 0:HALO, :]
        r = 3 * size_x * HALO + x * (HALO - 1)
        y_up[r : r + HALO - 1, :] = visc_ref[x, size_y - HALO + 1 : size_y, :]
        y_down[r : r + HALO - 1, :] = visc_ref[x, 0 : HALO - 1, :]


X_LAYERS = 4 * HALO - 1


def face_rows(size_x, size_y):
    rows_x = X_LAYERS * size_y
    rows_y = 3 * size_x * HALO + size_x * (HALO - 1)
    return -(-rows_x // 8) * 8, -(-rows_y // 8) * 8


def faces(velocity, viscosity):
    size_x, size_y, depth = viscosity.shape
    rows_x, rows_y = face_rows(size_x, size_y)
    shape_x = jax.ShapeDtypeStruct((rows_x, depth), F32)
    shape_y = jax.ShapeDtypeStruct((rows_y, depth), F32)
    return pl.pallas_call(
        faces_kernel,
        out_shape=(shape_x, shape_x, shape_y, shape_y),
        in_specs=[vmem(), vmem()],
        out_specs=(vmem(),) * 4,
        compiler_params=params(),
        cost_estimate=cost(10**6, 10**7),
        name="faces",
    )(velocity, viscosity)


def corners_kernel(size_y, low_ref, high_ref, up, down):
    for side, ref in ((0, low_ref), (1, high_ref)):
        for r in range(X_LAYERS):
            at = (side * X_LAYERS + r) * HALO
            up[at : at + HALO, :] = ref[(r + 1) * size_y - HALO : (r + 1) * size_y, :]
            down[at : at + HALO, :] = ref[r * size_y : r * size_y + HALO, :]


def corners(low, high, size_y):
    rows = -(-2 * X_LAYERS * HALO // 8) * 8
    shape = jax.ShapeDtypeStruct((rows, low.shape[1]), F32)
    return pl.pallas_call(
        functools.partial(corners_kernel, size_y),
        out_shape=(shape, shape),
        in_specs=[vmem(), vmem()],
        out_specs=(vmem(), vmem()),
        compiler_params=params(),
        cost_estimate=cost(10**6, 3 * 10**6),
        name="corners",
    )(low, high)


def solve_kernel(
    sweeps,
    meta,
    spread_ref,
    vel_ref,
    visc_ref,
    x_low,
    x_high,
    y_low,
    y_high,
    c_low,
    c_high,
    mid_ref,
    low_ref,
    high_ref,
    new_ref,
    part_mid,
    part_low,
    part_high,
    rhs,
    scaled,
    field,
    ratio,
):
    size_x, size_y, depth = visc_ref.shape
    ext = size_x + 2 * HALO
    own = slice(PAD, PAD + size_y)
    below = slice(PAD - HALO, PAD)
    above = slice(PAD + size_y, PAD + size_y + HALO)

    def clear(e, carry):
        ratio[e] = jnp.zeros((YE, depth), F32)
        return carry

    lax.fori_loop(0, ext - 2, clear, 0)
    base = 3 * size_x * HALO
    thin = HALO - 1
    for x in range(size_x):
        e = x + HALO - 1
        ratio[e, own, :] = visc_ref[x]
        ratio[e, PAD - thin : PAD, :] = y_low[base + x * thin : base + (x + 1) * thin, :]
        ratio[e, PAD + size_y : PAD + size_y + thin, :] = y_high[
            base + x * thin : base + (x + 1) * thin, :
        ]
    for side, ref in ((0, x_low), (1, x_high)):
        for l in range(thin):
            e = l if side == 0 else size_x + HALO - 1 + l
            r = 3 * HALO + l
            at = (side * X_LAYERS + r) * HALO
            ratio[e, own, :] = ref[r * size_y : (r + 1) * size_y, :]
            ratio[e, below, :] = c_low[at : at + HALO, :]
            ratio[e, above, :] = c_high[at : at + HALO, :]

    def clear_rhs(e, carry):
        for c in range(3):
            rhs[c, e] = jnp.zeros((YE, depth), F32)
        return carry

    lax.fori_loop(0, ext, clear_rhs, 0)
    for c in range(3):
        for x in range(size_x):
            e = x + HALO
            r = (c * size_x + x) * HALO
            rhs[c, e, own, :] = vel_ref[c, x]
            rhs[c, e, below, :] = y_low[r : r + HALO, :]
            rhs[c, e, above, :] = y_high[r : r + HALO, :]
        for side, ref in ((0, x_low), (1, x_high)):
            for l in range(HALO):
                e = l if side == 0 else size_x + HALO + l
                r = c * HALO + l
                at = (side * X_LAYERS + r) * HALO
                rhs[c, e, own, :] = ref[r * size_y : (r + 1) * size_y, :]
                rhs[c, e, below, :] = c_low[at : at + HALO, :]
                rhs[c, e, above, :] = c_high[at : at + HALO, :]

    def edge(e, carry):
        for c in range(3):
            rhs[c, e] = rhs[c, e] + spread_ref[c, e]
        return carry

    edge(0, 0)
    edge(ext - 1, 0)

    def scale(e, carry):
        for s in range(YE // 8):
            rows = slice(s * 8, s * 8 + 8)
            nu = ratio[e - 1, rows, :]
            inverse = 1.0 / (1.0 + 6.0 * nu)
            ratio[e - 1, rows, :] = nu * inverse
            for c in range(3):
                value = rhs[c, e, rows, :] + spread_ref[c, e, rows, :]
                rhs[c, e, rows, :] = value
                scaled[c, e - 1, rows, :] = value * inverse
        return carry

    lax.fori_loop(1, ext - 1, scale, 0)

    def sweep(source, offset, target, target_offset, first, last, write):
        def row(e, carry):
            for c in range(3):
                here = source[c, e - offset]
                beside = source[c, e + 1 - offset] + source[c, e - 1 - offset]
                beside = beside + pltpu.roll(here, YE - 1, 0) + pltpu.roll(here, 1, 0)
                beside = beside + pltpu.roll(here, depth - 1, 1) + pltpu.roll(here, 1, 1)
                value = scaled[c, e - 1] + ratio[e - 1] * beside
                if write:
                    value = jnp.where(iota((YE, depth), 0) < PAD + size_y, value, 0.0)
                target[c, e - target_offset] = value
                if write:
                    new_ref[c, e - HALO] = value[own]
            return carry

        lax.fori_loop(first, last, row, 0)

    sweep(rhs, 0, field, 1, 1, ext - 1, False)
    sweep(field, 1, rhs, 0, 2, ext - 2, False)
    sweep(rhs, 0, field, 1, 3, ext - 3, True)

    rows_of = {-1: (0, 2), 0: (0, size_x), 1: (size_x - 2, 2)}
    cols_of = {-1: (8, 8), 0: (8, 32), 1: (32, 8)}
    windows = depth // 128
    for dy, ref, part_ref in (
        (0, mid_ref, part_mid),
        (-1, low_ref, part_low),
        (1, high_ref, part_high),
    ):
        part_ref[...] = jnp.zeros(part_ref.shape, F32)
        for dx in (-1, 0, 1):
            index = (dy + 1) * 3 + dx + 1
            e0, rows = rows_of[dx]
            s0, cols = cols_of[dy]

            def chunk_step(chunk, carry):
                lanes = pl.ds(pl.multiple_of(chunk * 128, 128), 128)
                part, planar = planar_of(
                    ref, dx + 1, lanes, size_x * dx - 1 - e0, rows, PAD - 1 + size_y * dy - s0, cols
                )
                right = jnp.concatenate(split2(planar), axis=1)
                low = part[2:3].astype(I32)
                weights = bump(part[5:6])
                first = meta[index, chunk]

                def window_step(turn, sums):
                    window = jnp.bitwise_and(first + turn, windows - 1)
                    table = window_of(low, weights, window, depth)
                    at = pl.ds(pl.multiple_of(window * 128, 128), 128)
                    new = []
                    for c in range(3):
                        values = jnp.concatenate(
                            [
                                field[c, e0 + HALO - 1 + r, s0 : s0 + cols, at]
                                for r in range(rows)
                            ],
                            axis=0,
                        )
                        big, small = split2(values)
                        got = tn(big, right) + tn(small, right)
                        got = got[:, 0:128] + got[:, 128:256]
                        new.append(sums[c] + jnp.sum(got * table, axis=0, keepdims=True))
                    return tuple(new)

                start = tuple(jnp.zeros((1, 128), F32) for _ in range(3))
                sums = lax.fori_loop(0, meta[index, 16 + chunk], window_step, start)
                for c in range(3):
                    at = (dx + 1) * 3 + c
                    part_ref[at : at + 1, lanes] = sums[c]
                return carry

            lax.fori_loop(0, meta[index, 32], chunk_step, 0)


def solve(sweeps, meta, spread_ext, velocity, viscosity, halos, lists):
    size_x, size_y, depth = viscosity.shape
    ext = size_x + 2 * HALO
    slots = lists[0].shape[2]
    partial = jax.ShapeDtypeStruct((9, slots), F32)
    return pl.pallas_call(
        functools.partial(solve_kernel, sweeps),
        out_shape=(jax.ShapeDtypeStruct(velocity.shape, F32), partial, partial, partial),
        in_specs=[smem()] + [vmem()] * 12,
        out_specs=(vmem(),) * 4,
        scratch_shapes=[
            pltpu.VMEM((3, ext, YE, depth), F32),
            pltpu.VMEM((3, ext - 2, YE, depth), F32),
            pltpu.VMEM((3, ext - 2, YE, depth), F32),
            pltpu.VMEM((ext - 2, YE, depth), F32),
        ],
        compiler_params=params(),
        cost_estimate=cost(10**10, 2 * 10**7),
        name="solve",
    )(meta, spread_ext, velocity, viscosity, *halos, *lists)


def unsort_kernel(total_ref, rank_ref, out_ref):
    devices = out_ref.shape[0]
    slots = total_ref.shape[1]
    flat = jnp.concatenate([rank_ref[k : k + 1, :] for k in range(CAP)], axis=1)
    block = 256
    sums = jnp.zeros((32, slots), F32)
    for b in range(slots // block):
        values = total_ref[:, b * block : (b + 1) * block]
        parts = jnp.concatenate([*split3(values), jnp.zeros_like(values)], axis=0)
        sums = sums + nn(parts.astype(BF16), place_block(flat, b * block, block))
    rows = sums[0:8] + sums[8:16] + sums[16:24]
    turned = jnp.concatenate(
        [rows[:, k * devices : (k + 1) * devices] for k in range(CAP)], axis=0
    )
    out_ref[...] = turned.T


def unsort(total, rank):
    devices = rank.shape[1]
    return pl.pallas_call(
        unsort_kernel,
        out_shape=jax.ShapeDtypeStruct((devices, CAP * 8), F32),
        in_specs=[vmem(), vmem()],
        out_specs=vmem(),
        compiler_params=params(),
        cost_estimate=cost(10**9, 300_000),
        name="unsort",
    )(total, rank)


def unpack_kernel(owner_ref, rank_ref, back_ref, out_ref):
    markers = owner_ref.shape[1]
    devices = back_ref.shape[0]
    onehot = (iota((devices, markers), 0) == owner_ref[...]).astype(F32).astype(BF16)
    rank = rank_ref[...]
    turned = back_ref[...].T
    picked = None
    for part in split3(turned):
        term = nn(part.astype(BF16), onehot)
        picked = term if picked is None else picked + term
    total = jnp.zeros((8, markers), F32)
    for k in range(CAP):
        total = total + jnp.where(rank == k, picked[k * 8 : (k + 1) * 8], 0.0)
    out_ref[...] = total[0:3]


def unpack(owner_row, rank, back):
    markers = owner_row.shape[1]
    return pl.pallas_call(
        unpack_kernel,
        out_shape=jax.ShapeDtypeStruct((3, markers), F32),
        in_specs=[vmem()] * 3,
        out_specs=vmem(),
        compiler_params=params(),
        cost_estimate=cost(10**8, 100_000),
        name="unpack",
    )(owner_row, rank, back)


def shift_up(x, axis):
    count = lax.axis_size(axis)
    return lax.ppermute(x, axis, [(i, (i + 1) % count) for i in range(count)])


def shift_down(x, axis):
    count = lax.axis_size(axis)
    return lax.ppermute(x, axis, [((i + 1) % count, i) for i in range(count)])


def shards(velocity, viscosity, cells, offsets, forces, owners):
    devices = lax.axis_size("gx") * lax.axis_size("gy")
    size_x, size_y, depth = viscosity.shape
    markers = owners.shape[0]
    owner_row = owners.reshape(1, markers)
    both = ("gx", "gy")

    x_up, x_down, y_up, y_down = faces(velocity, viscosity)
    x_low = shift_up(x_up, "gx")
    x_high = shift_down(x_down, "gx")
    y_low = shift_up(y_up, "gy")
    y_high = shift_down(y_down, "gy")

    outgoing, rank = pack(owner_row, cells, offsets, forces, devices)
    received = lax.all_to_all(outgoing, both, split_axis=0, concat_axis=0, tiled=True)
    markers_list, order = sort(received, depth)
    list_low = shift_up(markers_list, "gx")
    list_high = shift_down(markers_list, "gx")
    mid = jnp.stack([list_low, markers_list, list_high])
    low = shift_up(mid, "gy")
    high = shift_down(mid, "gy")
    meta = jnp.concatenate([part[:, 10, 0:64] for part in (low, mid, high)], axis=0).astype(I32)
    spread_ext = spread(meta, mid, low, high, size_x, size_y, depth)

    c_up, c_down = corners(x_low, x_high, size_y)
    c_low = shift_up(c_up, "gy")
    c_high = shift_down(c_down, "gy")
    halos = (x_low, x_high, y_low, y_high, c_low, c_high)
    field, part_mid, part_low, part_high = solve(
        3, meta, spread_ext, velocity, viscosity, halos, (mid, low, high)
    )
    part = part_mid + shift_down(part_low, "gy") + shift_up(part_high, "gy")
    total = part[3:6] + shift_down(part[0:3], "gx") + shift_up(part[6:9], "gx")
    total = jnp.pad(total, ((0, 5), (0, 0)))
    back = unsort(total, order)
    back = lax.all_to_all(back, both, split_axis=0, concat_axis=0, tiled=True)
    return (field, unpack(owner_row, rank, back))


def solution(mesh):
    in_specs = (
        P(None, "gx", "gy", None),
        P("gx", "gy", None),
        P(None, ("gx", "gy")),
        P(None, ("gx", "gy")),
        P(None, ("gx", "gy")),
        P(("gx", "gy"), None),
    )
    out_specs = (P(None, "gx", "gy", None), P(None, ("gx", "gy")))
    return jax.shard_map(shards, mesh=mesh, in_specs=in_specs, out_specs=out_specs, check_vma=False)
```

```python
import functools

import jax
import jax.numpy as jnp
from jax import lax
from jax.experimental import pallas as pl
from jax.experimental.pallas import tpu as pltpu
from jax.sharding import PartitionSpec as P

F32 = jnp.float32
BF16 = jnp.bfloat16
I32 = jnp.int32
LIMIT = 60 * 1024 * 1024
CAP = 16
HALO = 3
PAD = 8
YE = 40
VISITS = 16
STEP = 256


def split3(x):
    hi = x.astype(BF16).astype(F32)
    rest = x - hi
    mid = rest.astype(BF16).astype(F32)
    return hi, mid, rest - mid


def split2(x):
    hi = x.astype(BF16)
    return hi, (x - hi.astype(F32)).astype(BF16)


def nn(a, b):
    return lax.dot_general(a, b, (((1,), (0,)), ((), ())), preferred_element_type=F32)


def nt(a, b):
    return lax.dot_general(a, b, (((1,), (1,)), ((), ())), preferred_element_type=F32)


def tn(a, b):
    return lax.dot_general(a, b, (((0,), (0,)), ((), ())), preferred_element_type=F32)


def iota(shape, dim):
    return lax.broadcasted_iota(I32, shape, dim)


def vmem():
    return pl.BlockSpec(memory_space=pltpu.VMEM)


def smem():
    return pl.BlockSpec(memory_space=pltpu.SMEM)


def params():
    return pltpu.CompilerParams(vmem_limit_bytes=LIMIT)


def cost(flops, size):
    return pl.CostEstimate(flops=flops, bytes_accessed=size, transcendentals=0)


def pack_kernel(owner_ref, cells_ref, offsets_ref, forces_ref, out_ref, rank_ref):
    markers = owner_ref.shape[1]
    devices = out_ref.shape[0]
    owner = owner_ref[...]
    before = (iota((128, 128), 0) < iota((128, 128), 1)).astype(BF16)
    running = jnp.zeros((devices, 1), F32)
    ranks = []
    hots = []
    for g in range(markers // 128):
        hot = (iota((devices, 128), 0) == owner[:, g * 128 : (g + 1) * 128]).astype(F32)
        within = nn(hot.astype(BF16), before)
        ranks.append(jnp.sum(hot * (within + running), axis=0, keepdims=True))
        running = running + jnp.sum(hot, axis=1, keepdims=True)
        hots.append(hot.astype(BF16))
    rank = jnp.concatenate(ranks, axis=1).astype(I32)
    rank_ref[...] = rank
    onehot = jnp.concatenate(hots, axis=1)
    payload = jnp.concatenate(
        [
            cells_ref[...].astype(F32),
            offsets_ref[...],
            forces_ref[...],
            jnp.ones((1, markers), F32),
            jnp.zeros((6, markers), F32),
        ],
        axis=0,
    )
    parts = split3(payload)
    total = None
    for part in parts:
        rows = jnp.concatenate([jnp.where(rank == k, part, 0.0) for k in range(CAP)], axis=0)
        term = nt(onehot, rows.astype(BF16))
        total = term if total is None else total + term
    out_ref[...] = total


def pack(owner_row, cells, offsets, forces, devices):
    markers = owner_row.shape[1]
    return pl.pallas_call(
        pack_kernel,
        out_shape=(
            jax.ShapeDtypeStruct((devices, CAP * 16), F32),
            jax.ShapeDtypeStruct((1, markers), I32),
        ),
        in_specs=[vmem()] * 4,
        out_specs=(vmem(), vmem()),
        compiler_params=params(),
        cost_estimate=cost(4 * 10**8, 300_000),
        name="pack",
    )(owner_row, cells, offsets, forces)


def place_block(flat, start, count):
    return (flat == start + iota((count, flat.shape[1]), 0)).astype(F32).astype(BF16)


def sort_kernel(depth, rec_ref, list_ref, rank_ref, keys, pieces):
    devices = rec_ref.shape[0]
    slots = devices * CAP
    rec = rec_ref[...]
    flipped = rec.T
    empty = float(depth * 4096)

    def key_of(z, valid, index):
        low = jnp.where(z < 0.5, float(depth - 1), z - 1.0)
        return jnp.where(valid > 0.5, low * float(slots), empty) + index

    rows = []
    lane = iota((devices, 128), 1)
    for k in range(CAP):
        at = k * 16
        column = key_of(
            rec[:, at + 2 : at + 3],
            rec[:, at + 9 : at + 10],
            (iota((devices, 1), 0) + k * devices).astype(F32),
        )
        keys[k] = jnp.broadcast_to(column, (devices, devices))
        rows.append(
            key_of(
                flipped[at + 2 : at + 3, :],
                flipped[at + 9 : at + 10, :],
                (iota((1, devices), 1) + k * devices).astype(F32),
            )
        )
        half = rec[:, (k // 8) * 128 : (k // 8 + 1) * 128]
        turned = half if k % 8 == 0 else pltpu.roll(half, 128 - (k % 8) * 16, 1)
        hi, mid, lo = split3(turned)
        joined = jnp.where(
            lane < 16,
            hi,
            jnp.where(
                lane < 32, pltpu.roll(mid, 16, 1), jnp.where(lane < 48, pltpu.roll(lo, 32, 1), 0.0)
            ),
        )
        pieces[k * devices : (k + 1) * devices, :] = joined.astype(BF16)
    ranks = []
    for k in range(CAP):
        row = rows[k]

        def count(other, acc):
            return acc + jnp.where(keys[other] < row, 1.0, 0.0)

        acc = lax.fori_loop(0, CAP, count, jnp.zeros((devices, devices), F32))
        ranks.append(jnp.sum(acc, axis=0, keepdims=True).astype(I32))
    rank_ref[...] = jnp.concatenate(ranks, axis=0)
    flat = jnp.concatenate(ranks, axis=1)
    block = 256
    for b in range(slots // block):
        moved = nn(place_block(flat, b * block, block), pieces[...]).T
        rows = moved[0:16] + moved[16:32] + moved[32:48]
        z = rows[2:3]
        low = jnp.where(z < 0.5, float(depth - 1), z - 1.0)
        list_ref[:, b * block : (b + 1) * block] = jnp.where(
            iota((16, block), 0) == 2, low, rows
        )
    low = jnp.where(list_ref[9:10, :] > 0.5, list_ref[2:3, :], float(4 * depth))
    visit = (iota((VISITS, slots), 0) * 128).astype(F32)
    diagonal = iota((VISITS, 128), 0) == iota((VISITS, 128), 1)

    def count_below(bound):
        column = jnp.sum(jnp.where(low < bound, 1.0, 0.0), axis=1, keepdims=True)
        return jnp.sum(jnp.where(diagonal, column, 0.0), axis=0, keepdims=True)

    first = count_below(visit - 3.0)
    last = count_below(visit + 128.0)
    chunk = jnp.minimum(jnp.floor(first / 128.0), float(slots // 128 - 2))
    steps = jnp.where(last > first, jnp.floor((last - chunk * 128.0 + 255.0) / 256.0), 0.0)
    meta = jnp.where(iota((1, 128), 1) < VISITS, chunk, pltpu.roll(steps, VISITS, 1))
    list_ref[10:11, 0:128] = meta


def sort(received, depth):
    devices = received.shape[0]
    slots = devices * CAP
    return pl.pallas_call(
        functools.partial(sort_kernel, depth),
        out_shape=(
            jax.ShapeDtypeStruct((16, slots), F32),
            jax.ShapeDtypeStruct((CAP, devices), I32),
        ),
        in_specs=[vmem()],
        out_specs=(vmem(), vmem()),
        scratch_shapes=[
            pltpu.VMEM((CAP, devices, devices), F32),
            pltpu.VMEM((slots, 128), BF16),
        ],
        compiler_params=params(),
        cost_estimate=cost(2 * 10**9, 300_000),
        name="sort",
    )(received)


def bump(frac):
    root = jnp.sqrt(1.0 + 4.0 * frac - 4.0 * frac * frac)
    return (
        (3.0 - 2.0 * frac - root) / 8.0,
        (3.0 - 2.0 * frac + root) / 8.0,
        (1.0 + 2.0 * frac + root) / 8.0,
        (1.0 + 2.0 * frac - root) / 8.0,
    )


def tent(first, weights, count, modulus=None):
    rows = iota((count, first.shape[1]), 0)
    table = 0.0
    for i in range(4):
        target = first + i
        if modulus is not None:
            target = jnp.bitwise_and(target, modulus - 1)
        table = jnp.where(rows == target, weights[i], table)
    return table


def markers_of(meta, index, visit, step, ref, at):
    slots = ref.shape[2]
    wanted = meta[index, visit] + 2 * step
    chunk = jnp.minimum(wanted, slots // 128 - 2)
    lanes = pl.ds(pl.multiple_of(chunk * 128, 128), STEP)
    part = ref[at, :, lanes]
    live = jnp.logical_and(
        iota((1, STEP), 1) >= (wanted - chunk) * 128, step < meta[index, VISITS + visit]
    )
    return part, lanes, live


def window_of(part, live, window, depth):
    weights = [jnp.where(live, w, 0.0) for w in bump(part[5:6])]
    return tent(part[2:3].astype(I32) - window * 128, weights, 128, depth)


def plane_of(part, shift_x, rows_x, shift_y, rows_y):
    table_x = tent(part[0:1].astype(I32) + shift_x, bump(part[3:4]), -(-rows_x // 8) * 8)
    table_y = tent(part[1:2].astype(I32) + shift_y, bump(part[4:5]), rows_y)
    return table_x, table_y


def run_lists(one, refs, meta, visit):
    for dy, ref in zip((0, -1, 1), refs):
        for dx in (0, -1, 1):
            one(dy, dx, ref, 0)

    @pl.when(most_steps(meta, visit) > 1)
    def _():
        for dy, ref in zip((0, -1, 1), refs):
            for dx in (0, -1, 1):

                def later(step, carry, dy=dy, dx=dx, ref=ref):
                    one(dy, dx, ref, step)
                    return carry

                lax.fori_loop(1, meta[(dy + 1) * 3 + dx + 1, VISITS + visit], later, 0)


def most_steps(meta, visit):
    most = meta[0, VISITS + visit]
    for index in range(1, 9):
        most = jnp.maximum(most, meta[index, VISITS + visit])
    return most


def spread_kernel(size_x, size_y, meta, mid_ref, low_ref, high_ref, out_ref):
    depth = out_ref.shape[3]
    windows = depth // 128

    def clear(e, carry):
        for c in range(3):
            out_ref[c, e] = jnp.zeros((YE, depth), F32)
        return carry

    lax.fori_loop(0, size_x + 2 * HALO, clear, 0)
    rows_of = {-1: (0, 5), 0: (2, size_x + 3), 1: (size_x + 2, 4)}
    cols_of = {-1: (PAD - 3, 8), 0: (PAD - 1, 32), 1: (32, 8)}

    def visit_step(visit, carry):
        window = jnp.bitwise_and(visit, windows - 1)
        at = pl.ds(pl.multiple_of(window * 128, 128), 128)

        def one(dy, dx, ref, step):
            index = (dy + 1) * 3 + dx + 1
            e0, rows = rows_of[dx]
            s0, cols = cols_of[dy]
            part, _, live = markers_of(meta, index, visit, step, ref, dx + 1)
            both = jnp.concatenate(split2(window_of(part, live, window, depth).T), axis=1)
            right = jnp.concatenate([both, both], axis=0)
            table_x, table_y = plane_of(
                part, HALO - 1 + size_x * dx - e0, rows, PAD - 1 + size_y * dy - s0, cols
            )
            for c in range(3):
                pushed = table_y * part[6 + c : 7 + c]
                planar = jnp.concatenate(
                    [table_x[r : r + 1] * pushed for r in range(rows)], axis=0
                )
                sums = nn(jnp.concatenate(split2(planar), axis=1), right)
                sums = sums[:, 0:128] + sums[:, 128:256]
                for r in range(rows):
                    out_ref[c, e0 + r, s0 : s0 + cols, at] += sums[r * cols : (r + 1) * cols]

        run_lists(one, (mid_ref, low_ref, high_ref), meta, visit)
        return carry

    lax.fori_loop(0, windows + 1, visit_step, 0)


def spread(meta, mid, low, high, size_x, size_y, depth):
    return pl.pallas_call(
        functools.partial(spread_kernel, size_x, size_y),
        out_shape=jax.ShapeDtypeStruct((3, size_x + 2 * HALO, YE, depth), F32),
        in_specs=[smem(), vmem(), vmem(), vmem()],
        out_specs=vmem(),
        compiler_params=params(),
        cost_estimate=cost(10**10, 10**7),
        name="spread",
    )(meta, mid, low, high)


def faces_kernel(vel_ref, visc_ref, x_up, x_down, x_up_late, x_down_late, y_up, y_down):
    size_x, size_y = visc_ref.shape[0], visc_ref.shape[1]
    for r in range(X_LAYERS):
        up, down = (x_up, x_down) if r < X_EARLY else (x_up_late, x_down_late)
        at = r if r < X_EARLY else r - X_EARLY
        rows = slice(at * size_y, (at + 1) * size_y)
        c, l = r // HALO, r % HALO
        if c < 3:
            up[rows, :] = vel_ref[c, size_x - HALO + l]
            down[rows, :] = vel_ref[c, l]
        else:
            up[rows, :] = visc_ref[size_x - HALO + 1 + l]
            down[rows, :] = visc_ref[l]
    for x in range(size_x):
        for c in range(3):
            r = (c * size_x + x) * HALO
            y_up[r : r + HALO, :] = vel_ref[c, x, size_y - HALO : size_y, :]
            y_down[r : r + HALO, :] = vel_ref[c, x, 0:HALO, :]
        r = 3 * size_x * HALO + x * (HALO - 1)
        y_up[r : r + HALO - 1, :] = visc_ref[x, size_y - HALO + 1 : size_y, :]
        y_down[r : r + HALO - 1, :] = visc_ref[x, 0 : HALO - 1, :]


def layer_of(early, late, r, size_y):
    if r < X_EARLY:
        return early, r * size_y
    return late, (r - X_EARLY) * size_y


X_LAYERS = 4 * HALO - 1
X_EARLY = 6
WAIT = True


def face_rows(size_x, size_y):
    rows_y = 3 * size_x * HALO + size_x * (HALO - 1)
    return tuple(-(-rows // 8) * 8 for rows in (X_EARLY * size_y, (X_LAYERS - X_EARLY) * size_y, rows_y))


def faces(velocity, viscosity):
    size_x, size_y, depth = viscosity.shape
    shapes = [jax.ShapeDtypeStruct((rows, depth), F32) for rows in face_rows(size_x, size_y)]
    return pl.pallas_call(
        faces_kernel,
        out_shape=[shape for shape in shapes for _ in range(2)],
        in_specs=[vmem(), vmem()],
        out_specs=[vmem()] * 6,
        compiler_params=params(),
        cost_estimate=cost(10**6, 10**7),
        name="faces",
    )(velocity, viscosity)


def corners_kernel(size_y, low_early, high_early, low_late, high_late, up, down):
    for side, early, late in ((0, low_early, low_late), (1, high_early, high_late)):
        for r in range(X_LAYERS):
            at = (side * X_LAYERS + r) * HALO
            ref, row = layer_of(early, late, r, size_y)
            up[at : at + HALO, :] = ref[row + size_y - HALO : row + size_y, :]
            down[at : at + HALO, :] = ref[row : row + HALO, :]


def corners(x_halos, size_y):
    rows = -(-2 * X_LAYERS * HALO // 8) * 8
    shape = jax.ShapeDtypeStruct((rows, x_halos[0].shape[1]), F32)
    return pl.pallas_call(
        functools.partial(corners_kernel, size_y),
        out_shape=(shape, shape),
        in_specs=[vmem()] * 4,
        out_specs=(vmem(), vmem()),
        compiler_params=params(),
        cost_estimate=cost(10**6, 3 * 10**6),
        name="corners",
    )(*x_halos)


def solve_kernel(
    sweeps,
    meta,
    spread_ref,
    vel_ref,
    visc_ref,
    x_low,
    x_high,
    x_low_late,
    x_high_late,
    y_low,
    y_high,
    c_low,
    c_high,
    mid_ref,
    low_ref,
    high_ref,
    new_ref,
    part_mid,
    part_low,
    part_high,
    rhs,
    scaled,
    field,
    ratio,
):
    size_x, size_y, depth = visc_ref.shape
    ext = size_x + 2 * HALO
    own = slice(PAD, PAD + size_y)
    below = slice(PAD - HALO, PAD)
    above = slice(PAD + size_y, PAD + size_y + HALO)

    def clear(e, carry):
        ratio[e] = jnp.zeros((YE, depth), F32)
        return carry

    lax.fori_loop(0, ext - 2, clear, 0)
    base = 3 * size_x * HALO
    thin = HALO - 1
    for x in range(size_x):
        e = x + HALO - 1
        ratio[e, own, :] = visc_ref[x]
        ratio[e, PAD - thin : PAD, :] = y_low[base + x * thin : base + (x + 1) * thin, :]
        ratio[e, PAD + size_y : PAD + size_y + thin, :] = y_high[
            base + x * thin : base + (x + 1) * thin, :
        ]
    for side, early, late in ((0, x_low, x_low_late), (1, x_high, x_high_late)):
        for l in range(thin):
            e = l if side == 0 else size_x + HALO - 1 + l
            r = 3 * HALO + l
            at = (side * X_LAYERS + r) * HALO
            ref, row = layer_of(early, late, r, size_y)
            ratio[e, own, :] = ref[row : row + size_y, :]
            ratio[e, below, :] = c_low[at : at + HALO, :]
            ratio[e, above, :] = c_high[at : at + HALO, :]

    def clear_rhs(e, carry):
        for c in range(3):
            rhs[c, e] = jnp.zeros((YE, depth), F32)
        return carry

    lax.fori_loop(0, ext, clear_rhs, 0)
    for c in range(3):
        for x in range(size_x):
            e = x + HALO
            r = (c * size_x + x) * HALO
            rhs[c, e, own, :] = vel_ref[c, x]
            rhs[c, e, below, :] = y_low[r : r + HALO, :]
            rhs[c, e, above, :] = y_high[r : r + HALO, :]
        for side, early, late in ((0, x_low, x_low_late), (1, x_high, x_high_late)):
            for l in range(HALO):
                e = l if side == 0 else size_x + HALO + l
                r = c * HALO + l
                at = (side * X_LAYERS + r) * HALO
                ref, row = layer_of(early, late, r, size_y)
                rhs[c, e, own, :] = ref[row : row + size_y, :]
                rhs[c, e, below, :] = c_low[at : at + HALO, :]
                rhs[c, e, above, :] = c_high[at : at + HALO, :]

    def edge(e, carry):
        for c in range(3):
            rhs[c, e] = rhs[c, e] + spread_ref[c, e]
        return carry

    edge(0, 0)
    edge(ext - 1, 0)

    def scale(e, carry):
        for s in range(YE // 8):
            rows = slice(s * 8, s * 8 + 8)
            nu = ratio[e - 1, rows, :]
            inverse = 1.0 / (1.0 + 6.0 * nu)
            ratio[e - 1, rows, :] = nu * inverse
            for c in range(3):
                value = rhs[c, e, rows, :] + spread_ref[c, e, rows, :]
                rhs[c, e, rows, :] = value
                scaled[c, e - 1, rows, :] = value * inverse
        return carry

    lax.fori_loop(1, ext - 1, scale, 0)

    def sweep(source, offset, target, target_offset, first, last, write):
        def row(e, carry):
            for c in range(3):
                here = source[c, e - offset]
                beside = source[c, e + 1 - offset] + source[c, e - 1 - offset]
                beside = beside + pltpu.roll(here, YE - 1, 0) + pltpu.roll(here, 1, 0)
                beside = beside + pltpu.roll(here, depth - 1, 1) + pltpu.roll(here, 1, 1)
                value = scaled[c, e - 1] + ratio[e - 1] * beside
                if write:
                    value = jnp.where(iota((YE, depth), 0) < PAD + size_y, value, 0.0)
                target[c, e - target_offset] = value
                if write:
                    new_ref[c, e - HALO] = value[own]
            return carry

        lax.fori_loop(first, last, row, 0)

    sweep(rhs, 0, field, 1, 1, ext - 1, False)
    sweep(field, 1, rhs, 0, 2, ext - 2, False)
    sweep(rhs, 0, field, 1, 3, ext - 3, True)

    rows_of = {-1: (0, 2), 0: (0, size_x), 1: (size_x - 1, 1)}
    cols_of = {-1: (8, 8), 0: (8, 32), 1: (32, 8)}
    windows = depth // 128
    parts = {0: part_mid, -1: part_low, 1: part_high}
    for part_ref in (part_mid, part_low, part_high):
        part_ref[...] = jnp.zeros(part_ref.shape, F32)

    def visit_step(visit, carry):
        window = jnp.bitwise_and(visit, windows - 1)
        at = pl.ds(pl.multiple_of(window * 128, 128), 128)

        def one(dy, dx, ref, step):
            part_ref = parts[dy]
            index = (dy + 1) * 3 + dx + 1
            e0, rows = rows_of[dx]
            s0, cols = cols_of[dy]
            part, lanes, live = markers_of(meta, index, visit, step, ref, dx + 1)
            both = jnp.concatenate(split2(window_of(part, live, window, depth)), axis=1)
            right = jnp.concatenate([both, both], axis=0)
            table_x, table_y = plane_of(
                part, size_x * dx - 1 - e0, rows, PAD - 1 + size_y * dy - s0, cols
            )
            for c in range(3):
                values = jnp.concatenate(
                    [field[c, e0 + HALO - 1 + r, s0 : s0 + cols, at] for r in range(rows)], axis=0
                )
                sums = nn(jnp.concatenate(split2(values), axis=1), right)
                sums = sums[:, 0:STEP] + sums[:, STEP : 2 * STEP]
                mixed = jnp.zeros((cols, STEP), F32)
                for r in range(rows):
                    mixed = mixed + table_x[r : r + 1] * sums[r * cols : (r + 1) * cols]
                row = (dx + 1) * 3 + c
                part_ref[row : row + 1, lanes] += jnp.sum(mixed * table_y, axis=0, keepdims=True)

        run_lists(one, (mid_ref, low_ref, high_ref), meta, visit)
        return carry

    lax.fori_loop(0, windows + 1, visit_step, 0)


def solve(sweeps, meta, spread_ext, velocity, viscosity, halos, lists):
    size_x, size_y, depth = viscosity.shape
    ext = size_x + 2 * HALO
    slots = lists[0].shape[2]
    partial = jax.ShapeDtypeStruct((9, slots), F32)
    return pl.pallas_call(
        functools.partial(solve_kernel, sweeps),
        out_shape=(jax.ShapeDtypeStruct(velocity.shape, F32), partial, partial, partial),
        in_specs=[smem()] + [vmem()] * 14,
        out_specs=(vmem(),) * 4,
        scratch_shapes=[
            pltpu.VMEM((3, ext, YE, depth), F32),
            pltpu.VMEM((3, ext - 2, YE, depth), F32),
            pltpu.VMEM((3, ext - 2, YE, depth), F32),
            pltpu.VMEM((ext - 2, YE, depth), F32),
        ],
        compiler_params=params(),
        cost_estimate=cost(10**10, 2 * 10**7),
        name="solve",
    )(meta, spread_ext, velocity, viscosity, *halos, *lists)


def unsort_kernel(total_ref, rank_ref, out_ref):
    devices = out_ref.shape[0]
    slots = total_ref.shape[1]
    flat = jnp.concatenate([rank_ref[k : k + 1, :] for k in range(CAP)], axis=1)
    block = 256
    sums = jnp.zeros((32, slots), F32)
    for b in range(slots // block):
        values = total_ref[:, b * block : (b + 1) * block]
        parts = jnp.concatenate([*split3(values), jnp.zeros_like(values)], axis=0)
        sums = sums + nn(parts.astype(BF16), place_block(flat, b * block, block))
    rows = sums[0:8] + sums[8:16] + sums[16:24]
    turned = jnp.concatenate(
        [rows[:, k * devices : (k + 1) * devices] for k in range(CAP)], axis=0
    )
    out_ref[...] = turned.T


def unsort(total, rank):
    devices = rank.shape[1]
    return pl.pallas_call(
        unsort_kernel,
        out_shape=jax.ShapeDtypeStruct((devices, CAP * 8), F32),
        in_specs=[vmem(), vmem()],
        out_specs=vmem(),
        compiler_params=params(),
        cost_estimate=cost(10**9, 300_000),
        name="unsort",
    )(total, rank)


def unpack_kernel(owner_ref, rank_ref, back_ref, out_ref):
    markers = owner_ref.shape[1]
    devices = back_ref.shape[0]
    onehot = (iota((devices, markers), 0) == owner_ref[...]).astype(F32).astype(BF16)
    rank = rank_ref[...]
    turned = back_ref[...].T
    picked = None
    for part in split3(turned):
        term = nn(part.astype(BF16), onehot)
        picked = term if picked is None else picked + term
    total = jnp.zeros((8, markers), F32)
    for k in range(CAP):
        total = total + jnp.where(rank == k, picked[k * 8 : (k + 1) * 8], 0.0)
    out_ref[...] = total[0:3]


def unpack(owner_row, rank, back):
    markers = owner_row.shape[1]
    return pl.pallas_call(
        unpack_kernel,
        out_shape=jax.ShapeDtypeStruct((3, markers), F32),
        in_specs=[vmem()] * 3,
        out_specs=vmem(),
        compiler_params=params(),
        cost_estimate=cost(10**8, 100_000),
        name="unpack",
    )(owner_row, rank, back)


def shift_up(x, axis):
    count = lax.axis_size(axis)
    return lax.ppermute(x, axis, [(i, (i + 1) % count) for i in range(count)])


def shift_down(x, axis):
    count = lax.axis_size(axis)
    return lax.ppermute(x, axis, [((i + 1) % count, i) for i in range(count)])


def shards(velocity, viscosity, cells, offsets, forces, owners):
    devices = lax.axis_size("gx") * lax.axis_size("gy")
    size_x, size_y, depth = viscosity.shape
    markers = owners.shape[0]
    owner_row = owners.reshape(1, markers)
    both = ("gx", "gy")

    x_up, x_down, x_up_late, x_down_late, y_up, y_down = faces(velocity, viscosity)
    x_low = shift_up(x_up, "gx")
    x_high = shift_down(x_down, "gx")
    owner_row, x_up_late = lax.optimization_barrier((owner_row, x_up_late))
    outgoing, rank = pack(owner_row, cells, offsets, forces, devices)
    received = lax.all_to_all(outgoing, both, split_axis=0, concat_axis=0, tiled=True)
    markers_list, order = sort(received, depth)
    markers_list, x_low, x_high = lax.optimization_barrier((markers_list, x_low, x_high))
    list_low = shift_up(markers_list, "gx")
    list_high = shift_down(markers_list, "gx")
    mid = jnp.stack([list_low, markers_list, list_high])
    mid, x_up_late, x_down_late, y_up, y_down = lax.optimization_barrier(
        (mid, x_up_late, x_down_late, y_up, y_down)
    )
    low = shift_up(mid, "gy")
    high = shift_down(mid, "gy")
    x_low_late = shift_up(x_up_late, "gx")
    x_high_late = shift_down(x_down_late, "gx")
    y_low = shift_up(y_up, "gy")
    y_high = shift_down(y_down, "gy")
    meta = jnp.concatenate([part[:, 10, 0:64] for part in (low, mid, high)], axis=0).astype(I32)
    spread_ext = spread(meta, mid, low, high, size_x, size_y, depth)

    x_halos = (x_low, x_high, x_low_late, x_high_late)
    x_halos = lax.optimization_barrier((*x_halos, spread_ext))[:4] if WAIT else x_halos
    c_up, c_down = corners(x_halos, size_y)
    c_low = shift_up(c_up, "gy")
    c_high = shift_down(c_down, "gy")
    halos = (*x_halos, y_low, y_high, c_low, c_high)
    field, part_mid, part_low, part_high = solve(
        3, meta, spread_ext, velocity, viscosity, halos, (mid, low, high)
    )
    part = part_mid + shift_down(part_low, "gy") + shift_up(part_high, "gy")
    total = part[3:6] + shift_down(part[0:3], "gx") + shift_up(part[6:9], "gx")
    total = jnp.pad(total, ((0, 5), (0, 0)))
    back = unsort(total, order)
    back = lax.all_to_all(back, both, split_axis=0, concat_axis=0, tiled=True)
    return (field, unpack(owner_row, rank, back))


def solution(mesh):
    in_specs = (
        P(None, "gx", "gy", None),
        P("gx", "gy", None),
        P(None, ("gx", "gy")),
        P(None, ("gx", "gy")),
        P(None, ("gx", "gy")),
        P(("gx", "gy"), None),
    )
    out_specs = (P(None, "gx", "gy", None), P(None, ("gx", "gy")))
    return jax.shard_map(shards, mesh=mesh, in_specs=in_specs, out_specs=out_specs, check_vma=False)
```

```python
import functools

import jax
import jax.numpy as jnp
from jax import lax
from jax.experimental import pallas as pl
from jax.experimental.pallas import tpu as pltpu
from jax.sharding import PartitionSpec as P

F32 = jnp.float32
BF16 = jnp.bfloat16
I32 = jnp.int32
LIMIT = 60 * 1024 * 1024
CAP = 16
HALO = 3
PAD = 8
YE = 40
VISITS = 16
STEP = 256


def split3(x):
    hi = x.astype(BF16).astype(F32)
    rest = x - hi
    mid = rest.astype(BF16).astype(F32)
    return hi, mid, rest - mid


def split2(x):
    hi = x.astype(BF16)
    return hi, (x - hi.astype(F32)).astype(BF16)


def nn(a, b):
    return lax.dot_general(a, b, (((1,), (0,)), ((), ())), preferred_element_type=F32)


def nt(a, b):
    return lax.dot_general(a, b, (((1,), (1,)), ((), ())), preferred_element_type=F32)


def tn(a, b):
    return lax.dot_general(a, b, (((0,), (0,)), ((), ())), preferred_element_type=F32)


def iota(shape, dim):
    return lax.broadcasted_iota(I32, shape, dim)


def vmem():
    return pl.BlockSpec(memory_space=pltpu.VMEM)


def smem():
    return pl.BlockSpec(memory_space=pltpu.SMEM)


def params():
    return pltpu.CompilerParams(vmem_limit_bytes=LIMIT)


def cost(flops, size):
    return pl.CostEstimate(flops=flops, bytes_accessed=size, transcendentals=0)


def pack_kernel(owner_ref, cells_ref, offsets_ref, forces_ref, out_ref, rank_ref):
    markers = owner_ref.shape[1]
    devices = out_ref.shape[0]
    owner = owner_ref[...]
    before = (iota((128, 128), 0) < iota((128, 128), 1)).astype(BF16)
    running = jnp.zeros((devices, 1), F32)
    ranks = []
    hots = []
    for g in range(markers // 128):
        hot = (iota((devices, 128), 0) == owner[:, g * 128 : (g + 1) * 128]).astype(F32)
        within = nn(hot.astype(BF16), before)
        ranks.append(jnp.sum(hot * (within + running), axis=0, keepdims=True))
        running = running + jnp.sum(hot, axis=1, keepdims=True)
        hots.append(hot.astype(BF16))
    rank = jnp.concatenate(ranks, axis=1).astype(I32)
    rank_ref[...] = rank
    onehot = jnp.concatenate(hots, axis=1)
    payload = jnp.concatenate(
        [
            cells_ref[...].astype(F32),
            offsets_ref[...],
            forces_ref[...],
            jnp.ones((1, markers), F32),
            jnp.zeros((6, markers), F32),
        ],
        axis=0,
    )
    parts = split3(payload)
    total = None
    for part in parts:
        rows = jnp.concatenate([jnp.where(rank == k, part, 0.0) for k in range(CAP)], axis=0)
        term = nt(onehot, rows.astype(BF16))
        total = term if total is None else total + term
    out_ref[...] = total


def pack(owner_row, cells, offsets, forces, devices):
    markers = owner_row.shape[1]
    return pl.pallas_call(
        pack_kernel,
        out_shape=(
            jax.ShapeDtypeStruct((devices, CAP * 16), F32),
            jax.ShapeDtypeStruct((1, markers), I32),
        ),
        in_specs=[vmem()] * 4,
        out_specs=(vmem(), vmem()),
        compiler_params=params(),
        cost_estimate=cost(4 * 10**8, 300_000),
        name="pack",
    )(owner_row, cells, offsets, forces)


def place_block(flat, start, count):
    return (flat == start + iota((count, flat.shape[1]), 0)).astype(F32).astype(BF16)


def sort_kernel(depth, rec_ref, list_ref, rank_ref, keys, pieces):
    devices = rec_ref.shape[0]
    slots = devices * CAP
    rec = rec_ref[...]
    flipped = rec.T
    empty = float(depth * 4096)

    def key_of(z, valid, index):
        low = jnp.where(z < 0.5, float(depth - 1), z - 1.0)
        return jnp.where(valid > 0.5, low * float(slots), empty) + index

    rows = []
    lane = iota((devices, 128), 1)
    for k in range(CAP):
        at = k * 16
        column = key_of(
            rec[:, at + 2 : at + 3],
            rec[:, at + 9 : at + 10],
            (iota((devices, 1), 0) + k * devices).astype(F32),
        )
        keys[k] = jnp.broadcast_to(column, (devices, devices))
        rows.append(
            key_of(
                flipped[at + 2 : at + 3, :],
                flipped[at + 9 : at + 10, :],
                (iota((1, devices), 1) + k * devices).astype(F32),
            )
        )
        half = rec[:, (k // 8) * 128 : (k // 8 + 1) * 128]
        turned = half if k % 8 == 0 else pltpu.roll(half, 128 - (k % 8) * 16, 1)
        hi, mid, lo = split3(turned)
        joined = jnp.where(
            lane < 16,
            hi,
            jnp.where(
                lane < 32, pltpu.roll(mid, 16, 1), jnp.where(lane < 48, pltpu.roll(lo, 32, 1), 0.0)
            ),
        )
        pieces[k * devices : (k + 1) * devices, :] = joined.astype(BF16)
    ranks = []
    for k in range(CAP):
        row = rows[k]

        def count(other, acc):
            return acc + jnp.where(keys[other] < row, 1.0, 0.0)

        acc = lax.fori_loop(0, CAP, count, jnp.zeros((devices, devices), F32))
        ranks.append(jnp.sum(acc, axis=0, keepdims=True).astype(I32))
    rank_ref[...] = jnp.concatenate(ranks, axis=0)
    flat = jnp.concatenate(ranks, axis=1)
    block = 256
    for b in range(slots // block):
        moved = nn(place_block(flat, b * block, block), pieces[...]).T
        rows = moved[0:16] + moved[16:32] + moved[32:48]
        z = rows[2:3]
        low = jnp.where(z < 0.5, float(depth - 1), z - 1.0)
        list_ref[:, b * block : (b + 1) * block] = jnp.where(
            iota((16, block), 0) == 2, low, rows
        )
    low = jnp.where(list_ref[9:10, :] > 0.5, list_ref[2:3, :], float(4 * depth))
    visit = (iota((VISITS, slots), 0) * 128).astype(F32)
    diagonal = iota((VISITS, 128), 0) == iota((VISITS, 128), 1)

    def count_below(bound):
        column = jnp.sum(jnp.where(low < bound, 1.0, 0.0), axis=1, keepdims=True)
        return jnp.sum(jnp.where(diagonal, column, 0.0), axis=0, keepdims=True)

    first = count_below(visit - 3.0)
    last = count_below(visit + 128.0)
    meta = jnp.where(iota((1, 128), 1) < VISITS, first, pltpu.roll(last, VISITS, 1))
    list_ref[10:11, 0:128] = meta


def sort(received, depth):
    devices = received.shape[0]
    slots = devices * CAP
    return pl.pallas_call(
        functools.partial(sort_kernel, depth),
        out_shape=(
            jax.ShapeDtypeStruct((16, slots), F32),
            jax.ShapeDtypeStruct((CAP, devices), I32),
        ),
        in_specs=[vmem()],
        out_specs=(vmem(), vmem()),
        scratch_shapes=[
            pltpu.VMEM((CAP, devices, devices), F32),
            pltpu.VMEM((slots, 128), BF16),
        ],
        compiler_params=params(),
        cost_estimate=cost(2 * 10**9, 300_000),
        name="sort",
    )(received)


def bump(frac):
    root = jnp.sqrt(1.0 + 4.0 * frac - 4.0 * frac * frac)
    return (
        (3.0 - 2.0 * frac - root) / 8.0,
        (3.0 - 2.0 * frac + root) / 8.0,
        (1.0 + 2.0 * frac + root) / 8.0,
        (1.0 + 2.0 * frac - root) / 8.0,
    )


def tent(first, weights, count, modulus=None):
    rows = iota((count, first.shape[1]), 0)
    table = 0.0
    for i in range(4):
        target = first + i
        if modulus is not None:
            target = jnp.bitwise_and(target, modulus - 1)
        table = jnp.where(rows == target, weights[i], table)
    return table


def markers_of(meta, index, visit, step, ref, at):
    slots = ref.shape[2]
    width = STEP + 128
    start = meta[index, visit] + STEP * step
    chunk = jnp.minimum(lax.shift_right_logical(start, 7), slots // 128 - width // 128)
    ahead = start - chunk * 128
    lanes = pl.ds(pl.multiple_of(chunk * 128, 128), width)
    part = pltpu.roll(ref[at, :, lanes], jnp.where(ahead == 0, 0, width - ahead), 1)[:, 0:STEP]
    live = iota((1, STEP), 1) < meta[index, VISITS + visit] - start
    return part, lanes, ahead, live


def window_of(part, live, window, depth):
    weights = [jnp.where(live, w, 0.0) for w in bump(part[5:6])]
    return tent(part[2:3].astype(I32) - window * 128, weights, 128, depth)


def plane_of(part, shift_x, rows_x, shift_y, rows_y):
    table_x = tent(part[0:1].astype(I32) + shift_x, bump(part[3:4]), -(-rows_x // 8) * 8)
    table_y = tent(part[1:2].astype(I32) + shift_y, bump(part[4:5]), rows_y)
    return table_x, table_y


def run_lists(one, lists, meta, visit):
    def length(dy, dx):
        index = (dy + 1) * 3 + dx + 1
        return meta[index, VISITS + visit] - meta[index, visit]

    most = 0
    for dy, dx, ref in lists:
        one(dy, dx, ref, 0)
        most = jnp.maximum(most, length(dy, dx))

    @pl.when(most > STEP)
    def _():
        for dy, dx, ref in lists:

            def later(step, carry, dy=dy, dx=dx, ref=ref):
                one(dy, dx, ref, step)
                return carry

            steps = lax.shift_right_logical(length(dy, dx) + STEP - 1, 8)
            lax.fori_loop(1, steps, later, 0)


def spread_lists(size_x, size_y, meta, lists, outs, first_row):
    depth = next(iter(outs.values())).shape[3]
    windows = depth // 128
    rows_of = {-1: (0, 5), 0: (2, size_x + 3), 1: (size_x + 2, 4)}

    def clear(e, carry):
        for out_ref in outs.values():
            for c in range(3):
                out_ref[c, e] = jnp.zeros(out_ref.shape[2:], F32)
        return carry

    lax.fori_loop(0, size_x + 2 * HALO, clear, 0)

    def visit_step(visit, carry):
        window = jnp.bitwise_and(visit, windows - 1)
        at = pl.ds(pl.multiple_of(window * 128, 128), 128)

        def one(dy, dx, ref, step):
            out_ref = outs[dy]
            index = (dy + 1) * 3 + dx + 1
            e0, rows = rows_of[dx]
            s0, cols, base = first_row[dy]
            part, _, _, live = markers_of(meta, index, visit, step, ref, dx + 1)
            both = jnp.concatenate(split2(window_of(part, live, window, depth).T), axis=1)
            right = jnp.concatenate([both, both], axis=0)
            table_x, table_y = plane_of(
                part, HALO - 1 + size_x * dx - e0, rows, PAD - 1 + size_y * dy - s0, cols
            )
            for c in range(3):
                pushed = table_y * part[6 + c : 7 + c]
                planar = jnp.concatenate(
                    [table_x[r : r + 1] * pushed for r in range(rows)], axis=0
                )
                sums = nn(jnp.concatenate(split2(planar), axis=1), right)
                sums = sums[:, 0:128] + sums[:, 128:256]
                for r in range(rows):
                    out_ref[c, e0 + r, base : base + cols, at] += sums[r * cols : (r + 1) * cols]

        run_lists(one, lists, meta, visit)
        return carry

    lax.fori_loop(0, windows + 1, visit_step, 0)


ROWS_MID = {0: (PAD - 1, 32, PAD - 1)}
ROWS_SIDE = {-1: (PAD - 3, 8, 0), 1: (32, 8, 0)}


def spread_mid_kernel(size_x, size_y, meta, mid_ref, out_ref):
    lists = [(0, dx, mid_ref) for dx in (0, -1, 1)]
    spread_lists(size_x, size_y, meta, lists, {0: out_ref}, ROWS_MID)


def spread_side_kernel(size_x, size_y, meta, low_ref, high_ref, out_low, out_high):
    lists = [(dy, dx, ref) for dy, ref in ((-1, low_ref), (1, high_ref)) for dx in (0, -1, 1)]
    outs = {-1: out_low, 1: out_high}
    spread_lists(size_x, size_y, meta, lists, outs, ROWS_SIDE)


def spread_mid(meta, mid, size_x, size_y, depth):
    return pl.pallas_call(
        functools.partial(spread_mid_kernel, size_x, size_y),
        out_shape=jax.ShapeDtypeStruct((3, size_x + 2 * HALO, YE, depth), F32),
        in_specs=[smem(), vmem()],
        out_specs=vmem(),
        compiler_params=params(),
        cost_estimate=cost(10**10, 10**7),
        name="spread_mid",
    )(meta, mid)


def spread_side(meta, low, high, size_x, size_y, depth):
    shape = jax.ShapeDtypeStruct((3, size_x + 2 * HALO, 8, depth), F32)
    return pl.pallas_call(
        functools.partial(spread_side_kernel, size_x, size_y),
        out_shape=(shape, shape),
        in_specs=[smem(), vmem(), vmem()],
        out_specs=(vmem(), vmem()),
        compiler_params=params(),
        cost_estimate=cost(10**10, 10**7),
        name="spread_side",
    )(meta, low, high)


def faces_kernel(vel_ref, visc_ref, x_up, x_down, y_up, y_down, x_up_late, x_down_late):
    size_x, size_y = visc_ref.shape[0], visc_ref.shape[1]
    for r in range(X_LAYERS):
        up, down = (x_up, x_down) if r < X_EARLY else (x_up_late, x_down_late)
        at = r if r < X_EARLY else r - X_EARLY
        rows = slice(at * size_y, (at + 1) * size_y)
        c, l = r // HALO, r % HALO
        if c < 3:
            up[rows, :] = vel_ref[c, size_x - HALO + l]
            down[rows, :] = vel_ref[c, l]
        else:
            up[rows, :] = visc_ref[size_x - HALO + 1 + l]
            down[rows, :] = visc_ref[l]
    for x in range(size_x):
        for c in range(3):
            r = (c * size_x + x) * HALO
            y_up[r : r + HALO, :] = vel_ref[c, x, size_y - HALO : size_y, :]
            y_down[r : r + HALO, :] = vel_ref[c, x, 0:HALO, :]
        r = 3 * size_x * HALO + x * (HALO - 1)
        y_up[r : r + HALO - 1, :] = visc_ref[x, size_y - HALO + 1 : size_y, :]
        y_down[r : r + HALO - 1, :] = visc_ref[x, 0 : HALO - 1, :]


def layer_of(early, late, r, size_y):
    if r < X_EARLY:
        return early, r * size_y
    return late, (r - X_EARLY) * size_y


X_LAYERS = 4 * HALO - 1
X_EARLY = 6


def face_rows(size_x, size_y):
    rows_y = 3 * size_x * HALO + size_x * (HALO - 1)
    rows = (X_EARLY * size_y, rows_y, (X_LAYERS - X_EARLY) * size_y)
    return tuple(-(-number // 8) * 8 for number in rows)


def faces(velocity, viscosity):
    size_x, size_y, depth = viscosity.shape
    shapes = [jax.ShapeDtypeStruct((rows, depth), F32) for rows in face_rows(size_x, size_y)]
    return pl.pallas_call(
        faces_kernel,
        out_shape=[shape for shape in shapes for _ in range(2)],
        in_specs=[vmem(), vmem()],
        out_specs=[vmem()] * 6,
        compiler_params=params(),
        cost_estimate=cost(10**6, 10**7),
        name="faces",
    )(velocity, viscosity)


def late_kernel(size_x, up_ref, down_ref, y_low, y_high, up, down):
    thick = up_ref.shape[0]
    up[0:thick, :] = up_ref[...]
    down[0:thick, :] = down_ref[...]
    base = 3 * size_x * HALO
    thin = HALO - 1
    for r in range(X_LAYERS):
        c, l = r // HALO, r % HALO
        for side, ref in ((0, y_low), (1, y_high)):
            for out, x in (
                (up, size_x - HALO + l + (1 if c == 3 else 0)),
                (down, l),
            ):
                at = thick + (r * 2 + side) * HALO
                if c < 3:
                    row = (c * size_x + x) * HALO
                    out[at : at + HALO, :] = ref[row : row + HALO, :]
                else:
                    row = base + x * thin
                    skip = 1 - side
                    out[at + skip : at + skip + thin, :] = ref[row : row + thin, :]


def late_faces(up, down, y_low, y_high, size_x):
    thick = up.shape[0]
    rows = thick + -(-2 * X_LAYERS * HALO // 8) * 8
    shape = jax.ShapeDtypeStruct((rows, up.shape[1]), F32)
    return pl.pallas_call(
        functools.partial(late_kernel, size_x),
        out_shape=(shape, shape),
        in_specs=[vmem()] * 4,
        out_specs=(vmem(), vmem()),
        compiler_params=params(),
        cost_estimate=cost(10**6, 4 * 10**6),
        name="late_faces",
    )(up, down, y_low, y_high)


def solve_kernel(
    sweeps,
    meta,
    spread_ref,
    side_low,
    side_high,
    vel_ref,
    visc_ref,
    x_low,
    x_high,
    x_low_late,
    x_high_late,
    y_low,
    y_high,
    mid_ref,
    low_ref,
    high_ref,
    new_ref,
    part_mid,
    part_low,
    part_high,
    rhs,
    scaled,
    field,
    ratio,
    gathered,
):
    size_x, size_y, depth = visc_ref.shape
    ext = size_x + 2 * HALO
    own = slice(PAD, PAD + size_y)
    below = slice(PAD - HALO, PAD)
    above = slice(PAD + size_y, PAD + size_y + HALO)
    tiles = [slice(s, s + 8) for s in range(0, YE, 8)]
    thick = -(-(X_LAYERS - X_EARLY) * size_y // 8) * 8

    def clear(e, carry):
        for c in range(3):
            rhs[c, e, tiles[0]] = jnp.zeros((8, depth), F32)
            rhs[c, e, tiles[4]] = jnp.zeros((8, depth), F32)
        return carry

    lax.fori_loop(0, ext, clear, 0)

    def clear_ratio(e, carry):
        ratio[e, tiles[0]] = jnp.zeros((8, depth), F32)
        ratio[e, tiles[4]] = jnp.zeros((8, depth), F32)
        return carry

    lax.fori_loop(0, ext - 2, clear_ratio, 0)

    base = 3 * size_x * HALO
    thin = HALO - 1
    for x in range(size_x):
        e = x + HALO - 1
        ratio[e, own, :] = visc_ref[x]
        ratio[e, PAD - thin : PAD, :] = y_low[base + x * thin : base + (x + 1) * thin, :]
        ratio[e, PAD + size_y : PAD + size_y + thin, :] = y_high[
            base + x * thin : base + (x + 1) * thin, :
        ]
        for c in range(3):
            r = (c * size_x + x) * HALO
            rhs[c, x + HALO, own, :] = vel_ref[c, x]
            rhs[c, x + HALO, below, :] = y_low[r : r + HALO, :]
            rhs[c, x + HALO, above, :] = y_high[r : r + HALO, :]
    for side, early, late in ((0, x_low, x_low_late), (1, x_high, x_high_late)):
        for r in range(X_LAYERS):
            c, l = r // HALO, r % HALO
            ref, row = layer_of(early, late, r, size_y)
            at = thick + 2 * r * HALO
            skip = 1 if c == 3 else 0
            if c < 3:
                target = rhs.at[c, l if side == 0 else size_x + HALO + l]
            else:
                target = ratio.at[l if side == 0 else size_x + HALO - 1 + l]
            target[own, :] = ref[row : row + size_y, :]
            target[PAD - HALO + skip : PAD, :] = late[at + skip : at + HALO, :]
            at = at + HALO
            end = HALO - skip
            target[PAD + size_y : PAD + size_y + end, :] = late[at : at + end, :]

    rows8 = iota((8, depth), 0)

    def total(c, e, s):
        value = rhs[c, e, tiles[s], :] + spread_ref[c, e, tiles[s], :]
        if s < 2:
            turned = pltpu.roll(side_low[c, e], PAD - 3, 0)
            keep = rows8 >= PAD - 3 if s == 0 else rows8 < PAD - 3
            value = value + jnp.where(keep, turned, 0.0)
        if s == 4:
            value = value + side_high[c, e]
        return value

    for e in (0, ext - 1):
        for c in range(3):
            for s in range(5):
                rhs[c, e, tiles[s], :] = total(c, e, s)

    def scale(e, carry):
        for s in range(5):
            nu = ratio[e - 1, tiles[s], :]
            inverse = 1.0 / (1.0 + 6.0 * nu)
            ratio[e - 1, tiles[s], :] = nu * inverse
            for c in range(3):
                value = total(c, e, s)
                rhs[c, e, tiles[s], :] = value
                scaled[c, e - 1, tiles[s], :] = value * inverse
        return carry

    lax.fori_loop(1, ext - 1, scale, 0)

    def sweep(source, offset, target, target_offset, first, last, write):
        def row(e, carry):
            for s in range(1 if write else 0, 5):
                factor = ratio[e - 1, tiles[s], :]
                for c in range(3):
                    here = source[c, e - offset, tiles[s], :]
                    beside = source[c, e + 1 - offset, tiles[s], :]
                    beside = beside + source[c, e - 1 - offset, tiles[s], :]
                    if s < 4:
                        beside = beside + source[c, e - offset, s * 8 + 1 : s * 8 + 9, :]
                    else:
                        beside = beside + pltpu.roll(here, 7, 0)
                    if s > 0:
                        beside = beside + source[c, e - offset, s * 8 - 1 : s * 8 + 7, :]
                    else:
                        beside = beside + pltpu.roll(here, 1, 0)
                    beside = beside + pltpu.roll(here, depth - 1, 1) + pltpu.roll(here, 1, 1)
                    value = scaled[c, e - 1, tiles[s], :] + factor * beside
                    if write and s == 4:
                        new_ref[c, e - HALO, 24:size_y, :] = value[0 : size_y - 24]
                        value = jnp.where(rows8 < size_y - 24, value, 0.0)
                    elif write:
                        new_ref[c, e - HALO, (s - 1) * 8 : s * 8, :] = value
                    target[c, e - target_offset, tiles[s], :] = value
            return carry

        lax.fori_loop(first, last, row, 0)

    sweep(rhs, 0, field, 1, 1, ext - 1, False)
    sweep(field, 1, rhs, 0, 2, ext - 2, False)
    sweep(rhs, 0, field, 1, 3, ext - 3, True)

    rows_of = {-1: (0, 2), 0: (0, size_x), 1: (size_x - 1, 1)}
    cols_of = {-1: (8, 8), 0: (8, 32), 1: (32, 8)}
    windows = depth // 128
    gathered[...] = jnp.zeros(gathered.shape, F32)

    def visit_step(visit, carry):
        window = jnp.bitwise_and(visit, windows - 1)
        at = pl.ds(pl.multiple_of(window * 128, 128), 128)

        def one(dy, dx, ref, step):
            index = (dy + 1) * 3 + dx + 1
            e0, rows = rows_of[dx]
            s0, cols = cols_of[dy]
            part, lanes, ahead, live = markers_of(meta, index, visit, step, ref, dx + 1)
            both = jnp.concatenate(split2(window_of(part, live, window, depth)), axis=1)
            right = jnp.concatenate([both, both], axis=0)
            table_x, table_y = plane_of(
                part, size_x * dx - 1 - e0, rows, PAD - 1 + size_y * dy - s0, cols
            )
            found = []
            for c in range(3):
                values = jnp.concatenate(
                    [field[c, e0 + HALO - 1 + r, s0 : s0 + cols, at] for r in range(rows)], axis=0
                )
                sums = nn(jnp.concatenate(split2(values), axis=1), right)
                sums = sums[:, 0:STEP] + sums[:, STEP : 2 * STEP]
                mixed = jnp.zeros((cols, STEP), F32)
                for r in range(rows):
                    mixed = mixed + table_x[r : r + 1] * sums[r * cols : (r + 1) * cols]
                total = jnp.sum(mixed * table_y, axis=0, keepdims=True)
                found.append(jnp.where(live, total, 0.0))
            found = jnp.concatenate([*found, jnp.zeros((5, STEP), F32)], axis=0)
            found = jnp.concatenate([found, jnp.zeros((8, 128), F32)], axis=1)
            gathered[index, :, lanes] += pltpu.roll(found, ahead, 1)

        lists = [
            (dy, dx, ref)
            for dy, ref in ((0, mid_ref), (-1, low_ref), (1, high_ref))
            for dx in (0, -1, 1)
        ]
        run_lists(one, lists, meta, visit)
        return carry

    lax.fori_loop(0, windows + 1, visit_step, 0)
    for dy, part_ref in ((-1, part_low), (0, part_mid), (1, part_high)):
        for dx in range(3):
            part_ref[dx * 3 : dx * 3 + 3, :] = gathered[(dy + 1) * 3 + dx, 0:3, :]


def solve(sweeps, meta, spreads, velocity, viscosity, halos, lists):
    size_x, size_y, depth = viscosity.shape
    ext = size_x + 2 * HALO
    slots = lists[0].shape[2]
    partial = jax.ShapeDtypeStruct((9, slots), F32)
    return pl.pallas_call(
        functools.partial(solve_kernel, sweeps),
        out_shape=(jax.ShapeDtypeStruct(velocity.shape, F32), partial, partial, partial),
        in_specs=[smem()] + [vmem()] * 14,
        out_specs=(vmem(),) * 4,
        scratch_shapes=[
            pltpu.VMEM((3, ext, YE, depth), F32),
            pltpu.VMEM((3, ext - 2, YE, depth), F32),
            pltpu.VMEM((3, ext - 2, YE, depth), F32),
            pltpu.VMEM((ext - 2, YE, depth), F32),
            pltpu.VMEM((9, 8, slots), F32),
        ],
        compiler_params=params(),
        cost_estimate=cost(10**10, 2 * 10**7),
        name="solve",
    )(meta, *spreads, velocity, viscosity, *halos, *lists)


def unsort_kernel(total_ref, rank_ref, out_ref):
    devices = out_ref.shape[0]
    slots = total_ref.shape[1]
    flat = jnp.concatenate([rank_ref[k : k + 1, :] for k in range(CAP)], axis=1)
    block = 256
    sums = jnp.zeros((32, slots), F32)
    for b in range(slots // block):
        values = total_ref[:, b * block : (b + 1) * block]
        parts = jnp.concatenate([*split3(values), jnp.zeros_like(values)], axis=0)
        sums = sums + nn(parts.astype(BF16), place_block(flat, b * block, block))
    rows = sums[0:8] + sums[8:16] + sums[16:24]
    turned = jnp.concatenate(
        [rows[:, k * devices : (k + 1) * devices] for k in range(CAP)], axis=0
    )
    out_ref[...] = turned.T


def unsort(total, rank):
    devices = rank.shape[1]
    return pl.pallas_call(
        unsort_kernel,
        out_shape=jax.ShapeDtypeStruct((devices, CAP * 8), F32),
        in_specs=[vmem(), vmem()],
        out_specs=vmem(),
        compiler_params=params(),
        cost_estimate=cost(10**9, 300_000),
        name="unsort",
    )(total, rank)


def unpack_kernel(owner_ref, rank_ref, back_ref, out_ref):
    markers = owner_ref.shape[1]
    devices = back_ref.shape[0]
    onehot = (iota((devices, markers), 0) == owner_ref[...]).astype(F32).astype(BF16)
    rank = rank_ref[...]
    turned = back_ref[...].T
    picked = None
    for part in split3(turned):
        term = nn(part.astype(BF16), onehot)
        picked = term if picked is None else picked + term
    total = jnp.zeros((8, markers), F32)
    for k in range(CAP):
        total = total + jnp.where(rank == k, picked[k * 8 : (k + 1) * 8], 0.0)
    out_ref[...] = total[0:3]


def unpack(owner_row, rank, back):
    markers = owner_row.shape[1]
    return pl.pallas_call(
        unpack_kernel,
        out_shape=jax.ShapeDtypeStruct((3, markers), F32),
        in_specs=[vmem()] * 3,
        out_specs=vmem(),
        compiler_params=params(),
        cost_estimate=cost(10**8, 100_000),
        name="unpack",
    )(owner_row, rank, back)


def shift_up(x, axis):
    count = lax.axis_size(axis)
    return lax.ppermute(x, axis, [(i, (i + 1) % count) for i in range(count)])


def shift_down(x, axis):
    count = lax.axis_size(axis)
    return lax.ppermute(x, axis, [((i + 1) % count, i) for i in range(count)])


def shards(velocity, viscosity, cells, offsets, forces, owners):
    devices = lax.axis_size("gx") * lax.axis_size("gy")
    size_x, size_y, depth = viscosity.shape
    markers = owners.shape[0]
    owner_row = owners.reshape(1, markers)
    both = ("gx", "gy")

    x_up, x_down, y_up, y_down, x_up_late, x_down_late = faces(velocity, viscosity)
    x_low = shift_up(x_up, "gx")
    x_high = shift_down(x_down, "gx")
    y_low = shift_up(y_up, "gy")
    y_high = shift_down(y_down, "gy")
    owner_row, x_up_late = lax.optimization_barrier((owner_row, x_up_late))
    outgoing, rank = pack(owner_row, cells, offsets, forces, devices)
    received = lax.all_to_all(outgoing, both, split_axis=0, concat_axis=0, tiled=True)
    markers_list, order = sort(received, depth)
    markers_list, x_low, x_high, y_low, y_high = lax.optimization_barrier(
        (markers_list, x_low, x_high, y_low, y_high)
    )
    list_low = shift_up(markers_list, "gx")
    list_high = shift_down(markers_list, "gx")
    x_up_late, x_down_late = late_faces(x_up_late, x_down_late, y_low, y_high, size_x)
    mid = jnp.stack([list_low, markers_list, list_high])
    mid, x_up_late, x_down_late = lax.optimization_barrier((mid, x_up_late, x_down_late))
    x_low_late = shift_up(x_up_late, "gx")
    x_high_late = shift_down(x_down_late, "gx")
    low = shift_up(mid, "gy")
    high = shift_down(mid, "gy")
    halos = (x_low, x_high, x_low_late, x_high_late, y_low, y_high)
    meta_mid = mid[:, 10, 0:64].astype(I32)
    meta_mid = jnp.pad(meta_mid, ((3, 3), (0, 0)))
    spread_own = spread_mid(meta_mid, mid, size_x, size_y, depth)
    low, high, spread_own = lax.optimization_barrier((low, high, spread_own))
    meta = jnp.concatenate([part[:, 10, 0:64] for part in (low, mid, high)], axis=0).astype(I32)
    spreads = (spread_own, *spread_side(meta, low, high, size_x, size_y, depth))
    halos, spreads = lax.optimization_barrier((halos, spreads))
    field, part_mid, part_low, part_high = solve(
        3, meta, spreads, velocity, viscosity, halos, (mid, low, high)
    )
    part = part_mid + shift_down(part_low, "gy") + shift_up(part_high, "gy")
    total = part[3:6] + shift_down(part[0:3], "gx") + shift_up(part[6:9], "gx")
    total = jnp.pad(total, ((0, 5), (0, 0)))
    back = unsort(total, order)
    back = lax.all_to_all(back, both, split_axis=0, concat_axis=0, tiled=True)
    return (field, unpack(owner_row, rank, back))


def solution(mesh):
    in_specs = (
        P(None, "gx", "gy", None),
        P("gx", "gy", None),
        P(None, ("gx", "gy")),
        P(None, ("gx", "gy")),
        P(None, ("gx", "gy")),
        P(("gx", "gy"), None),
    )
    out_specs = (P(None, "gx", "gy", None), P(None, ("gx", "gy")))
    return jax.shard_map(shards, mesh=mesh, in_specs=in_specs, out_specs=out_specs, check_vma=False)
```

```python
import functools

import jax
import jax.numpy as jnp
from jax import lax
from jax.experimental import pallas as pl
from jax.experimental.pallas import tpu as pltpu
from jax.sharding import PartitionSpec as P

F32 = jnp.float32
BF16 = jnp.bfloat16
I32 = jnp.int32
LIMIT = 60 * 1024 * 1024
CAP = 16
HALO = 3
PAD = 8
YE = 40
VISITS = 16
STEP = 256


def split3(x):
    hi = x.astype(BF16).astype(F32)
    rest = x - hi
    mid = rest.astype(BF16).astype(F32)
    return hi, mid, rest - mid


def split2(x):
    hi = x.astype(BF16)
    return hi, (x - hi.astype(F32)).astype(BF16)


def nn(a, b):
    return lax.dot_general(a, b, (((1,), (0,)), ((), ())), preferred_element_type=F32)


def nt(a, b):
    return lax.dot_general(a, b, (((1,), (1,)), ((), ())), preferred_element_type=F32)


def tn(a, b):
    return lax.dot_general(a, b, (((0,), (0,)), ((), ())), preferred_element_type=F32)


def iota(shape, dim):
    return lax.broadcasted_iota(I32, shape, dim)


def vmem():
    return pl.BlockSpec(memory_space=pltpu.VMEM)


def smem():
    return pl.BlockSpec(memory_space=pltpu.SMEM)


def params():
    return pltpu.CompilerParams(vmem_limit_bytes=LIMIT)


def cost(flops, size):
    return pl.CostEstimate(flops=flops, bytes_accessed=size, transcendentals=0)


def pack_kernel(owner_ref, cells_ref, offsets_ref, forces_ref, out_ref, rank_ref):
    markers = owner_ref.shape[1]
    devices = out_ref.shape[0]
    owner = owner_ref[...]
    before = (iota((128, 128), 0) < iota((128, 128), 1)).astype(BF16)
    running = jnp.zeros((devices, 1), F32)
    ranks = []
    hots = []
    for g in range(markers // 128):
        hot = (iota((devices, 128), 0) == owner[:, g * 128 : (g + 1) * 128]).astype(F32)
        within = nn(hot.astype(BF16), before)
        ranks.append(jnp.sum(hot * (within + running), axis=0, keepdims=True))
        running = running + jnp.sum(hot, axis=1, keepdims=True)
        hots.append(hot.astype(BF16))
    rank = jnp.concatenate(ranks, axis=1).astype(I32)
    rank_ref[...] = rank
    onehot = jnp.concatenate(hots, axis=1)
    payload = jnp.concatenate(
        [
            cells_ref[...].astype(F32),
            offsets_ref[...],
            forces_ref[...],
            jnp.ones((1, markers), F32),
            jnp.zeros((6, markers), F32),
        ],
        axis=0,
    )
    parts = split3(payload)
    total = None
    for part in parts:
        rows = jnp.concatenate([jnp.where(rank == k, part, 0.0) for k in range(CAP)], axis=0)
        term = nt(onehot, rows.astype(BF16))
        total = term if total is None else total + term
    out_ref[...] = total


def pack(owner_row, cells, offsets, forces, devices):
    markers = owner_row.shape[1]
    return pl.pallas_call(
        pack_kernel,
        out_shape=(
            jax.ShapeDtypeStruct((devices, CAP * 16), F32),
            jax.ShapeDtypeStruct((1, markers), I32),
        ),
        in_specs=[vmem()] * 4,
        out_specs=(vmem(), vmem()),
        compiler_params=params(),
        cost_estimate=cost(4 * 10**8, 300_000),
        name="pack",
    )(owner_row, cells, offsets, forces)


def place_block(flat, start, count):
    return (flat == start + iota((count, flat.shape[1]), 0)).astype(F32).astype(BF16)


def sort_kernel(depth, rec_ref, list_ref, rank_ref, keys, pieces):
    devices = rec_ref.shape[0]
    slots = devices * CAP
    rec = rec_ref[...]
    flipped = rec.T
    empty = float(depth * 4096)

    def key_of(z, valid, index):
        low = jnp.where(z < 0.5, float(depth - 1), z - 1.0)
        return jnp.where(valid > 0.5, low * float(slots), empty) + index

    rows = []
    lane = iota((devices, 128), 1)
    for k in range(CAP):
        at = k * 16
        column = key_of(
            rec[:, at + 2 : at + 3],
            rec[:, at + 9 : at + 10],
            (iota((devices, 1), 0) + k * devices).astype(F32),
        )
        keys[k] = jnp.broadcast_to(column, (devices, devices))
        rows.append(
            key_of(
                flipped[at + 2 : at + 3, :],
                flipped[at + 9 : at + 10, :],
                (iota((1, devices), 1) + k * devices).astype(F32),
            )
        )
        half = rec[:, (k // 8) * 128 : (k // 8 + 1) * 128]
        turned = half if k % 8 == 0 else pltpu.roll(half, 128 - (k % 8) * 16, 1)
        hi, mid, lo = split3(turned)
        joined = jnp.where(
            lane < 16,
            hi,
            jnp.where(
                lane < 32, pltpu.roll(mid, 16, 1), jnp.where(lane < 48, pltpu.roll(lo, 32, 1), 0.0)
            ),
        )
        pieces[k * devices : (k + 1) * devices, :] = joined.astype(BF16)
    ranks = []
    for k in range(CAP):
        row = rows[k]

        def count(other, acc):
            return acc + jnp.where(keys[other] < row, 1.0, 0.0)

        acc = lax.fori_loop(0, CAP, count, jnp.zeros((devices, devices), F32))
        ranks.append(jnp.sum(acc, axis=0, keepdims=True).astype(I32))
    rank_ref[...] = jnp.concatenate(ranks, axis=0)
    flat = jnp.concatenate(ranks, axis=1)
    block = 256
    for b in range(slots // block):
        moved = nn(place_block(flat, b * block, block), pieces[...]).T
        rows = moved[0:16] + moved[16:32] + moved[32:48]
        z = rows[2:3]
        low = jnp.where(z < 0.5, float(depth - 1), z - 1.0)
        list_ref[:, b * block : (b + 1) * block] = jnp.where(
            iota((16, block), 0) == 2, low, rows
        )
    low = jnp.where(list_ref[9:10, :] > 0.5, list_ref[2:3, :], float(4 * depth))
    visit = (iota((VISITS, slots), 0) * 128).astype(F32)
    diagonal = iota((VISITS, 128), 0) == iota((VISITS, 128), 1)

    def count_below(bound):
        column = jnp.sum(jnp.where(low < bound, 1.0, 0.0), axis=1, keepdims=True)
        return jnp.sum(jnp.where(diagonal, column, 0.0), axis=0, keepdims=True)

    first = count_below(visit - 3.0)
    last = count_below(visit + 128.0)
    meta = jnp.where(iota((1, 128), 1) < VISITS, first, pltpu.roll(last, VISITS, 1))
    list_ref[10:11, 0:128] = meta


def sort(received, depth):
    devices = received.shape[0]
    slots = devices * CAP
    return pl.pallas_call(
        functools.partial(sort_kernel, depth),
        out_shape=(
            jax.ShapeDtypeStruct((16, slots), F32),
            jax.ShapeDtypeStruct((CAP, devices), I32),
        ),
        in_specs=[vmem()],
        out_specs=(vmem(), vmem()),
        scratch_shapes=[
            pltpu.VMEM((CAP, devices, devices), F32),
            pltpu.VMEM((slots, 128), BF16),
        ],
        compiler_params=params(),
        cost_estimate=cost(2 * 10**9, 300_000),
        name="sort",
    )(received)


def bump(frac):
    root = jnp.sqrt(1.0 + 4.0 * frac - 4.0 * frac * frac)
    return (
        (3.0 - 2.0 * frac - root) / 8.0,
        (3.0 - 2.0 * frac + root) / 8.0,
        (1.0 + 2.0 * frac + root) / 8.0,
        (1.0 + 2.0 * frac - root) / 8.0,
    )


def tent(first, weights, count, modulus=None):
    rows = iota((count, first.shape[1]), 0)
    table = 0.0
    for i in range(4):
        target = first + i
        if modulus is not None:
            target = jnp.bitwise_and(target, modulus - 1)
        table = jnp.where(rows == target, weights[i], table)
    return table


def markers_of(meta, index, visit, step, ref, at):
    slots = ref.shape[2]
    width = STEP + 128
    start = meta[index, visit] + STEP * step
    chunk = jnp.minimum(lax.shift_right_logical(start, 7), slots // 128 - width // 128)
    ahead = start - chunk * 128
    lanes = pl.ds(pl.multiple_of(chunk * 128, 128), width)
    part = pltpu.roll(ref[at, :, lanes], jnp.where(ahead == 0, 0, width - ahead), 1)[:, 0:STEP]
    live = iota((1, STEP), 1) < meta[index, VISITS + visit] - start
    return part, lanes, ahead, live


def window_of(part, live, window, depth):
    weights = [jnp.where(live, w, 0.0) for w in bump(part[5:6])]
    return tent(part[2:3].astype(I32) - window * 128, weights, 128, depth)


def plane_of(part, shift_x, rows_x, shift_y, rows_y):
    table_x = tent(part[0:1].astype(I32) + shift_x, bump(part[3:4]), -(-rows_x // 8) * 8)
    table_y = tent(part[1:2].astype(I32) + shift_y, bump(part[4:5]), rows_y)
    return table_x, table_y


def run_lists(one, lists, meta, visit):
    def length(dy, dx):
        index = (dy + 1) * 3 + dx + 1
        return meta[index, VISITS + visit] - meta[index, visit]

    most = 0
    for dy, dx, ref in lists:
        one(dy, dx, ref, 0)
        most = jnp.maximum(most, length(dy, dx))

    @pl.when(most > STEP)
    def _():
        for dy, dx, ref in lists:

            def later(step, carry, dy=dy, dx=dx, ref=ref):
                one(dy, dx, ref, step)
                return carry

            steps = lax.shift_right_logical(length(dy, dx) + STEP - 1, 8)
            lax.fori_loop(1, steps, later, 0)


def spread_lists(size_x, size_y, meta, lists, outs, first_row):
    depth = next(iter(outs.values())).shape[3]
    windows = depth // 128
    rows_of = {-1: (0, 5), 0: (2, size_x + 3), 1: (size_x + 2, 4)}

    def clear(e, carry):
        for out_ref in outs.values():
            for c in range(3):
                out_ref[c, e] = jnp.zeros(out_ref.shape[2:], F32)
        return carry

    lax.fori_loop(0, size_x + 2 * HALO, clear, 0)

    def visit_step(visit, carry):
        window = jnp.bitwise_and(visit, windows - 1)
        at = pl.ds(pl.multiple_of(window * 128, 128), 128)

        def one(dy, dx, ref, step):
            out_ref = outs[dy]
            index = (dy + 1) * 3 + dx + 1
            e0, rows = rows_of[dx]
            s0, cols, base = first_row[dy]
            part, _, _, live = markers_of(meta, index, visit, step, ref, dx + 1)
            both = jnp.concatenate(split2(window_of(part, live, window, depth).T), axis=1)
            right = jnp.concatenate([both, both], axis=0)
            table_x, table_y = plane_of(
                part, HALO - 1 + size_x * dx - e0, rows, PAD - 1 + size_y * dy - s0, cols
            )
            for c in range(3):
                pushed = table_y * part[6 + c : 7 + c]
                planar = jnp.concatenate(
                    [table_x[r : r + 1] * pushed for r in range(rows)], axis=0
                )
                sums = nn(jnp.concatenate(split2(planar), axis=1), right)
                sums = sums[:, 0:128] + sums[:, 128:256]
                for r in range(rows):
                    out_ref[c, e0 + r, base : base + cols, at] += sums[r * cols : (r + 1) * cols]

        run_lists(one, lists, meta, visit)
        return carry

    lax.fori_loop(0, windows + 1, visit_step, 0)


ROWS_MID = {0: (PAD - 1, 32, PAD - 1)}
ROWS_SIDE = {-1: (PAD - 3, 8, 0), 1: (32, 8, 0)}


def spread_mid_kernel(size_x, size_y, meta, mid_ref, out_ref):
    lists = [(0, dx, mid_ref) for dx in (0, -1, 1)]
    spread_lists(size_x, size_y, meta, lists, {0: out_ref}, ROWS_MID)


def spread_side_kernel(size_x, size_y, meta, low_ref, high_ref, out_low, out_high):
    lists = [(dy, dx, ref) for dy, ref in ((-1, low_ref), (1, high_ref)) for dx in (0, -1, 1)]
    outs = {-1: out_low, 1: out_high}
    spread_lists(size_x, size_y, meta, lists, outs, ROWS_SIDE)


def spread_mid(meta, mid, size_x, size_y, depth):
    return pl.pallas_call(
        functools.partial(spread_mid_kernel, size_x, size_y),
        out_shape=jax.ShapeDtypeStruct((3, size_x + 2 * HALO, YE, depth), F32),
        in_specs=[smem(), vmem()],
        out_specs=vmem(),
        compiler_params=params(),
        cost_estimate=cost(10**10, 10**7),
        name="spread_mid",
    )(meta, mid)


def spread_side(meta, low, high, size_x, size_y, depth):
    shape = jax.ShapeDtypeStruct((3, size_x + 2 * HALO, 8, depth), F32)
    return pl.pallas_call(
        functools.partial(spread_side_kernel, size_x, size_y),
        out_shape=(shape, shape),
        in_specs=[smem(), vmem(), vmem()],
        out_specs=(vmem(), vmem()),
        compiler_params=params(),
        cost_estimate=cost(10**10, 10**7),
        name="spread_side",
    )(meta, low, high)


def faces_kernel(vel_ref, visc_ref, x_up, x_down, y_up, y_down, x_up_late, x_down_late):
    size_x, size_y = visc_ref.shape[0], visc_ref.shape[1]
    for r in range(X_LAYERS):
        up, down = (x_up, x_down) if r < X_EARLY else (x_up_late, x_down_late)
        at = r if r < X_EARLY else r - X_EARLY
        rows = slice(at * size_y, (at + 1) * size_y)
        c, l = r // HALO, r % HALO
        if c < 3:
            up[rows, :] = vel_ref[c, size_x - HALO + l]
            down[rows, :] = vel_ref[c, l]
        else:
            up[rows, :] = visc_ref[size_x - HALO + 1 + l]
            down[rows, :] = visc_ref[l]
    for x in range(size_x):
        for c in range(3):
            r = (c * size_x + x) * HALO
            y_up[r : r + HALO, :] = vel_ref[c, x, size_y - HALO : size_y, :]
            y_down[r : r + HALO, :] = vel_ref[c, x, 0:HALO, :]
        r = 3 * size_x * HALO + x * (HALO - 1)
        y_up[r : r + HALO - 1, :] = visc_ref[x, size_y - HALO + 1 : size_y, :]
        y_down[r : r + HALO - 1, :] = visc_ref[x, 0 : HALO - 1, :]


def layer_of(early, late, r, size_y):
    if r < X_EARLY:
        return early, r * size_y
    return late, (r - X_EARLY) * size_y


X_LAYERS = 4 * HALO - 1
X_EARLY = 2


def face_rows(size_x, size_y):
    rows_y = 3 * size_x * HALO + size_x * (HALO - 1)
    rows = (X_EARLY * size_y, rows_y, (X_LAYERS - X_EARLY) * size_y)
    return tuple(-(-number // 8) * 8 for number in rows)


def faces(velocity, viscosity):
    size_x, size_y, depth = viscosity.shape
    shapes = [jax.ShapeDtypeStruct((rows, depth), F32) for rows in face_rows(size_x, size_y)]
    return pl.pallas_call(
        faces_kernel,
        out_shape=[shape for shape in shapes for _ in range(2)],
        in_specs=[vmem(), vmem()],
        out_specs=[vmem()] * 6,
        compiler_params=params(),
        cost_estimate=cost(10**6, 10**7),
        name="faces",
    )(velocity, viscosity)


def corner_plan(up):
    plan, at = [], 0
    for r in range(X_LAYERS):
        c, l = r // HALO, r % HALO
        reach = HALO if c < 3 else HALO - 1
        away = reach - l if up else l + 1
        if reach > away:
            plan.append((r, reach - away, at))
            at += 2 * (reach - away)
    return plan, at


def late_kernel(size_x, up_ref, down_ref, y_low, y_high, up, down):
    thick = up_ref.shape[0]
    up[0:thick, :] = up_ref[...]
    down[0:thick, :] = down_ref[...]
    base = 3 * size_x * HALO
    thin = HALO - 1
    for out, is_up in ((up, True), (down, False)):
        for r, count, first in corner_plan(is_up)[0]:
            c, l = r // HALO, r % HALO
            x = l if not is_up else size_x - HALO + l + (1 if c == 3 else 0)
            deep, row = (HALO, (c * size_x + x) * HALO) if c < 3 else (thin, base + x * thin)
            at = thick + first
            out[at : at + count, :] = y_low[row + deep - count : row + deep, :]
            at = at + count
            out[at : at + count, :] = y_high[row : row + count, :]


def late_faces(up, down, y_low, y_high, size_x):
    thick = up.shape[0]
    rows = thick + -(-corner_plan(True)[1] // 8) * 8
    shape = jax.ShapeDtypeStruct((rows, up.shape[1]), F32)
    return pl.pallas_call(
        functools.partial(late_kernel, size_x),
        out_shape=(shape, shape),
        in_specs=[vmem()] * 4,
        out_specs=(vmem(), vmem()),
        compiler_params=params(),
        cost_estimate=cost(10**6, 4 * 10**6),
        name="late_faces",
    )(up, down, y_low, y_high)


def solve_kernel(
    sweeps,
    meta,
    spread_ref,
    side_low,
    side_high,
    vel_ref,
    visc_ref,
    x_low,
    x_high,
    x_low_late,
    x_high_late,
    y_low,
    y_high,
    low_ref,
    high_ref,
    new_ref,
    part_low,
    part_high,
    rhs,
    scaled,
    field,
    ratio,
    gathered,
):
    size_x, size_y, depth = visc_ref.shape
    ext = size_x + 2 * HALO
    own = slice(PAD, PAD + size_y)
    below = slice(PAD - HALO, PAD)
    above = slice(PAD + size_y, PAD + size_y + HALO)
    tiles = [slice(s, s + 8) for s in range(0, YE, 8)]
    thick = -(-(X_LAYERS - X_EARLY) * size_y // 8) * 8

    def clear(e, carry):
        for c in range(3):
            rhs[c, e, tiles[0]] = jnp.zeros((8, depth), F32)
            rhs[c, e, tiles[4]] = jnp.zeros((8, depth), F32)
        return carry

    lax.fori_loop(0, ext, clear, 0)

    def clear_ratio(e, carry):
        ratio[e, tiles[0]] = jnp.zeros((8, depth), F32)
        ratio[e, tiles[4]] = jnp.zeros((8, depth), F32)
        return carry

    lax.fori_loop(0, ext - 2, clear_ratio, 0)

    base = 3 * size_x * HALO
    thin = HALO - 1
    for x in range(size_x):
        e = x + HALO - 1
        ratio[e, own, :] = visc_ref[x]
        ratio[e, PAD - thin : PAD, :] = y_low[base + x * thin : base + (x + 1) * thin, :]
        ratio[e, PAD + size_y : PAD + size_y + thin, :] = y_high[
            base + x * thin : base + (x + 1) * thin, :
        ]
        for c in range(3):
            r = (c * size_x + x) * HALO
            rhs[c, x + HALO, own, :] = vel_ref[c, x]
            rhs[c, x + HALO, below, :] = y_low[r : r + HALO, :]
            rhs[c, x + HALO, above, :] = y_high[r : r + HALO, :]
    for side, early, late in ((0, x_low, x_low_late), (1, x_high, x_high_late)):
        for r in range(X_LAYERS):
            c, l = r // HALO, r % HALO
            ref, row = layer_of(early, late, r, size_y)
            if c < 3:
                target = rhs.at[c, l if side == 0 else size_x + HALO + l]
            else:
                target = ratio.at[l if side == 0 else size_x + HALO - 1 + l]
            target[own, :] = ref[row : row + size_y, :]
        for r, count, first in corner_plan(side == 0)[0]:
            c, l = r // HALO, r % HALO
            if c < 3:
                target = rhs.at[c, l if side == 0 else size_x + HALO + l]
            else:
                target = ratio.at[l if side == 0 else size_x + HALO - 1 + l]
            at = thick + first
            target[PAD - count : PAD, :] = late[at : at + count, :]
            at = at + count
            target[PAD + size_y : PAD + size_y + count, :] = late[at : at + count, :]

    rows8 = iota((8, depth), 0)

    def total(c, e, s):
        value = rhs[c, e, tiles[s], :] + spread_ref[c, e, tiles[s], :]
        if s < 2:
            turned = pltpu.roll(side_low[c, e], PAD - 3, 0)
            keep = rows8 >= PAD - 3 if s == 0 else rows8 < PAD - 3
            value = value + jnp.where(keep, turned, 0.0)
        if s == 4:
            value = value + side_high[c, e]
        return value

    for e in (0, ext - 1):
        for c in range(3):
            for s in range(5):
                rhs[c, e, tiles[s], :] = total(c, e, s)

    def scale(e, carry):
        for s in range(5):
            nu = ratio[e - 1, tiles[s], :]
            inverse = 1.0 / (1.0 + 6.0 * nu)
            ratio[e - 1, tiles[s], :] = nu * inverse
            for c in range(3):
                value = total(c, e, s)
                rhs[c, e, tiles[s], :] = value
                scaled[c, e - 1, tiles[s], :] = value * inverse
        return carry

    lax.fori_loop(1, ext - 1, scale, 0)

    def sweep(source, offset, target, target_offset, first, last, write):
        def row(e, carry):
            for s in range(1 if write else 0, 5):
                factor = ratio[e - 1, tiles[s], :]
                for c in range(3):
                    here = source[c, e - offset, tiles[s], :]
                    beside = source[c, e + 1 - offset, tiles[s], :]
                    beside = beside + source[c, e - 1 - offset, tiles[s], :]
                    if s < 4:
                        beside = beside + source[c, e - offset, s * 8 + 1 : s * 8 + 9, :]
                    else:
                        beside = beside + pltpu.roll(here, 7, 0)
                    if s > 0:
                        beside = beside + source[c, e - offset, s * 8 - 1 : s * 8 + 7, :]
                    else:
                        beside = beside + pltpu.roll(here, 1, 0)
                    beside = beside + pltpu.roll(here, depth - 1, 1) + pltpu.roll(here, 1, 1)
                    value = scaled[c, e - 1, tiles[s], :] + factor * beside
                    if not write:
                        target[c, e - target_offset, tiles[s], :] = value
                    elif s == 4:
                        target[c, e - target_offset, 24:size_y, :] = value[0 : size_y - 24]
                    else:
                        target[c, e - target_offset, (s - 1) * 8 : s * 8, :] = value
            return carry

        lax.fori_loop(first, last, row, 0)

    sweep(rhs, 0, field, 1, 1, ext - 1, False)
    sweep(field, 1, rhs, 0, 2, ext - 2, False)
    sweep(rhs, 0, new_ref, HALO, 3, ext - 3, True)

    gathered[...] = jnp.zeros(gathered.shape, F32)
    lists = [(dy, dx, ref) for dy, ref in ((-1, low_ref), (1, high_ref)) for dx in (0, -1, 1)]
    outs = {(dy, dx): (dy + 1) // 2 * 3 + dx + 1 for dy, dx, _ in lists}
    sample_lists(meta, lists, new_ref, gathered, outs)
    for dx in range(3):
        part_low[dx * 3 : dx * 3 + 3, :] = gathered[dx, 0:3, :]
        part_high[dx * 3 : dx * 3 + 3, :] = gathered[3 + dx, 0:3, :]


def sample_lists(meta, lists, field, out_ref, outs):
    _, size_x, size_y, depth = field.shape
    windows = depth // 128
    whole = size_y // 8 * 8
    rows_of = {-1: (0, 2), 0: (0, size_x), 1: (size_x - 1, 1)}
    cols_of = {-1: (0, 8), 0: (0, whole + 8), 1: (whole, 8)}

    def values_of(c, x, dy, at):
        if dy == -1:
            return [field[c, x, 0:8, at]]
        tail = field[c, x, whole:size_y, at]
        tail = jnp.concatenate([tail, jnp.zeros((whole + 8 - size_y, 128), F32)], axis=0)
        return [tail] if dy == 1 else [field[c, x, 0:whole, at], tail]

    def visit_step(visit, carry):
        window = jnp.bitwise_and(visit, windows - 1)
        at = pl.ds(pl.multiple_of(window * 128, 128), 128)

        def one(dy, dx, ref, step):
            index = (dy + 1) * 3 + dx + 1
            x0, rows = rows_of[dx]
            s0, cols = cols_of[dy]
            part, lanes, ahead, live = markers_of(meta, index, visit, step, ref, dx + 1)
            both = jnp.concatenate(split2(window_of(part, live, window, depth)), axis=1)
            right = jnp.concatenate([both, both], axis=0)
            table_x, table_y = plane_of(
                part, size_x * dx - 1 - x0, rows, size_y * dy - 1 - s0, cols
            )
            found = []
            for c in range(3):
                values = jnp.concatenate(
                    [v for r in range(rows) for v in values_of(c, x0 + r, dy, at)], axis=0
                )
                sums = nn(jnp.concatenate(split2(values), axis=1), right)
                sums = sums[:, 0:STEP] + sums[:, STEP : 2 * STEP]
                mixed = jnp.zeros((cols, STEP), F32)
                for r in range(rows):
                    mixed = mixed + table_x[r : r + 1] * sums[r * cols : (r + 1) * cols]
                total = jnp.sum(mixed * table_y, axis=0, keepdims=True)
                found.append(jnp.where(live, total, 0.0))
            found = jnp.concatenate([*found, jnp.zeros((5, STEP), F32)], axis=0)
            found = jnp.concatenate([found, jnp.zeros((8, 128), F32)], axis=1)
            out_ref[outs[dy, dx], :, lanes] += pltpu.roll(found, ahead, 1)

        run_lists(one, lists, meta, visit)
        return carry

    lax.fori_loop(0, windows + 1, visit_step, 0)


def sample_kernel(places, meta, mid_ref, field, out_ref):
    out_ref[...] = jnp.zeros(out_ref.shape, F32)
    lists = [(0, dx, mid_ref) for dx in places]
    sample_lists(meta, lists, field, out_ref, {(0, dx): i for i, dx in enumerate(places)})


def sample(meta, mid, field, places):
    return pl.pallas_call(
        functools.partial(sample_kernel, places),
        out_shape=jax.ShapeDtypeStruct((len(places), 8, mid.shape[2]), F32),
        in_specs=[smem(), vmem(), vmem()],
        out_specs=vmem(),
        compiler_params=params(),
        cost_estimate=cost(5 * 10**9, 5 * 10**6),
        name="sample",
    )(meta, mid, field)


def solve(sweeps, meta, spreads, velocity, viscosity, halos, lists):
    size_x, size_y, depth = viscosity.shape
    ext = size_x + 2 * HALO
    slots = lists[0].shape[2]
    partial = jax.ShapeDtypeStruct((9, slots), F32)
    return pl.pallas_call(
        functools.partial(solve_kernel, sweeps),
        out_shape=(jax.ShapeDtypeStruct(velocity.shape, F32), partial, partial),
        in_specs=[smem()] + [vmem()] * 13,
        out_specs=(vmem(),) * 3,
        scratch_shapes=[
            pltpu.VMEM((3, ext, YE, depth), F32),
            pltpu.VMEM((3, ext - 2, YE, depth), F32),
            pltpu.VMEM((3, ext - 2, YE, depth), F32),
            pltpu.VMEM((ext - 2, YE, depth), F32),
            pltpu.VMEM((6, 8, slots), F32),
        ],
        compiler_params=params(),
        cost_estimate=cost(10**10, 2 * 10**7),
        name="solve",
    )(meta, *spreads, velocity, viscosity, *halos, *lists)


def unsort_kernel(own_ref, sides_ref, low_ref, high_ref, rank_ref, out_ref):
    devices = out_ref.shape[0]
    slots = sides_ref.shape[1]
    total = own_ref[0, 0:3, :] + sides_ref[3:6, :] + low_ref[...] + high_ref[...]
    total = jnp.concatenate([total, jnp.zeros((5, slots), F32)], axis=0)
    flat = jnp.concatenate([rank_ref[k : k + 1, :] for k in range(CAP)], axis=1)
    block = 256
    sums = jnp.zeros((32, slots), F32)
    for b in range(slots // block):
        values = total[:, b * block : (b + 1) * block]
        parts = jnp.concatenate([*split3(values), jnp.zeros_like(values)], axis=0)
        sums = sums + nn(parts.astype(BF16), place_block(flat, b * block, block))
    rows = sums[0:8] + sums[8:16] + sums[16:24]
    turned = jnp.concatenate(
        [rows[:, k * devices : (k + 1) * devices] for k in range(CAP)], axis=0
    )
    out_ref[...] = turned.T


def unsort(own, sides, low, high, rank):
    devices = rank.shape[1]
    return pl.pallas_call(
        unsort_kernel,
        out_shape=jax.ShapeDtypeStruct((devices, CAP * 8), F32),
        in_specs=[vmem()] * 5,
        out_specs=vmem(),
        compiler_params=params(),
        cost_estimate=cost(10**9, 300_000),
        name="unsort",
    )(own, sides, low, high, rank)


def unpack_kernel(owner_ref, rank_ref, back_ref, out_ref):
    markers = owner_ref.shape[1]
    devices = back_ref.shape[0]
    onehot = (iota((devices, markers), 0) == owner_ref[...]).astype(F32).astype(BF16)
    rank = rank_ref[...]
    turned = back_ref[...].T
    picked = None
    for part in split3(turned):
        term = nn(part.astype(BF16), onehot)
        picked = term if picked is None else picked + term
    total = jnp.zeros((8, markers), F32)
    for k in range(CAP):
        total = total + jnp.where(rank == k, picked[k * 8 : (k + 1) * 8], 0.0)
    out_ref[...] = total[0:3]


def unpack(owner_row, rank, back):
    markers = owner_row.shape[1]
    return pl.pallas_call(
        unpack_kernel,
        out_shape=jax.ShapeDtypeStruct((3, markers), F32),
        in_specs=[vmem()] * 3,
        out_specs=vmem(),
        compiler_params=params(),
        cost_estimate=cost(10**8, 100_000),
        name="unpack",
    )(owner_row, rank, back)


def shift_up(x, axis):
    count = lax.axis_size(axis)
    return lax.ppermute(x, axis, [(i, (i + 1) % count) for i in range(count)])


def shift_down(x, axis):
    count = lax.axis_size(axis)
    return lax.ppermute(x, axis, [((i + 1) % count, i) for i in range(count)])


def shards(velocity, viscosity, cells, offsets, forces, owners):
    devices = lax.axis_size("gx") * lax.axis_size("gy")
    size_x, size_y, depth = viscosity.shape
    markers = owners.shape[0]
    owner_row = owners.reshape(1, markers)
    both = ("gx", "gy")

    outgoing, rank = pack(owner_row, cells, offsets, forces, devices)
    outgoing, face_source = lax.optimization_barrier((outgoing, viscosity))
    received = lax.all_to_all(outgoing, both, split_axis=0, concat_axis=0, tiled=True)
    x_up, x_down, y_up, y_down, x_up_late, x_down_late = faces(velocity, face_source)
    x_low = shift_up(x_up, "gx")
    x_high = shift_down(x_down, "gx")
    received, y_up, y_down = lax.optimization_barrier((received, y_up, y_down))
    y_low = shift_up(y_up, "gy")
    y_high = shift_down(y_down, "gy")
    markers_list, order = sort(received, depth)
    markers_list, x_low, x_high, y_low, y_high = lax.optimization_barrier(
        (markers_list, x_low, x_high, y_low, y_high)
    )
    list_low = shift_up(markers_list, "gx")
    list_high = shift_down(markers_list, "gx")
    x_up_late, x_down_late = late_faces(x_up_late, x_down_late, y_low, y_high, size_x)
    mid = jnp.stack([list_low, markers_list, list_high])
    mid, x_up_late, x_down_late = lax.optimization_barrier((mid, x_up_late, x_down_late))
    x_low_late = shift_up(x_up_late, "gx")
    x_high_late = shift_down(x_down_late, "gx")
    low = shift_up(mid, "gy")
    high = shift_down(mid, "gy")
    halos = (x_low, x_high, x_low_late, x_high_late, y_low, y_high)
    meta_mid = mid[:, 10, 0:64].astype(I32)
    meta_mid = jnp.pad(meta_mid, ((3, 3), (0, 0)))
    spread_own = spread_mid(meta_mid, mid, size_x, size_y, depth)
    low, high, spread_own = lax.optimization_barrier((low, high, spread_own))
    meta = jnp.concatenate([part[:, 10, 0:64] for part in (low, mid, high)], axis=0).astype(I32)
    spreads = (spread_own, *spread_side(meta, low, high, size_x, size_y, depth))
    halos, spreads = lax.optimization_barrier((halos, spreads))
    field, part_low, part_high = solve(
        3, meta, spreads, velocity, viscosity, halos, (low, high)
    )
    beside = sample(meta, mid, field, (-1, 1))
    sides = shift_down(part_low, "gy") + shift_up(part_high, "gy")
    to_low = sides[0:3] + beside[0, 0:3]
    to_high = sides[6:9] + beside[1, 0:3]
    to_low, to_high, field_own = lax.optimization_barrier((to_low, to_high, field))
    own = sample(meta, mid, field_own, (0,))
    back = unsort(own, sides, shift_down(to_low, "gx"), shift_up(to_high, "gx"), order)
    back = lax.all_to_all(back, both, split_axis=0, concat_axis=0, tiled=True)
    return (field, unpack(owner_row, rank, back))


def solution(mesh):
    in_specs = (
        P(None, "gx", "gy", None),
        P("gx", "gy", None),
        P(None, ("gx", "gy")),
        P(None, ("gx", "gy")),
        P(None, ("gx", "gy")),
        P(("gx", "gy"), None),
    )
    out_specs = (P(None, "gx", "gy", None), P(None, ("gx", "gy")))
    return jax.shard_map(shards, mesh=mesh, in_specs=in_specs, out_specs=out_specs, check_vma=False)
```

```python
import functools

import jax
import jax.numpy as jnp
from jax import lax
from jax.experimental import pallas as pl
from jax.experimental.pallas import tpu as pltpu
from jax.sharding import PartitionSpec as P

F32 = jnp.float32
BF16 = jnp.bfloat16
I32 = jnp.int32
LIMIT = 60 * 1024 * 1024
CAP = 16
HALO = 3
PAD = 8
YE = 40
VISITS = 16
STEP = 256
GROUP_MID = 3
GROUP_SIDE = 3


def split3(x):
    hi = x.astype(BF16).astype(F32)
    rest = x - hi
    mid = rest.astype(BF16).astype(F32)
    return hi, mid, rest - mid


def split2(x):
    hi = x.astype(BF16)
    return hi, (x - hi.astype(F32)).astype(BF16)


def nn(a, b):
    return lax.dot_general(a, b, (((1,), (0,)), ((), ())), preferred_element_type=F32)


def nt(a, b):
    return lax.dot_general(a, b, (((1,), (1,)), ((), ())), preferred_element_type=F32)


def tn(a, b):
    return lax.dot_general(a, b, (((0,), (0,)), ((), ())), preferred_element_type=F32)


def iota(shape, dim):
    return lax.broadcasted_iota(I32, shape, dim)


def vmem():
    return pl.BlockSpec(memory_space=pltpu.VMEM)


def smem():
    return pl.BlockSpec(memory_space=pltpu.SMEM)


def params():
    return pltpu.CompilerParams(vmem_limit_bytes=LIMIT)


def cost(flops, size):
    return pl.CostEstimate(flops=flops, bytes_accessed=size, transcendentals=0)


def pack_kernel(owner_ref, cells_ref, offsets_ref, forces_ref, out_ref, rank_ref):
    markers = owner_ref.shape[1]
    devices = out_ref.shape[0]
    owner = owner_ref[...]
    before = (iota((128, 128), 0) < iota((128, 128), 1)).astype(BF16)
    running = jnp.zeros((devices, 1), F32)
    ranks = []
    hots = []
    for g in range(markers // 128):
        hot = (iota((devices, 128), 0) == owner[:, g * 128 : (g + 1) * 128]).astype(F32)
        within = nn(hot.astype(BF16), before)
        ranks.append(jnp.sum(hot * (within + running), axis=0, keepdims=True))
        running = running + jnp.sum(hot, axis=1, keepdims=True)
        hots.append(hot.astype(BF16))
    rank = jnp.concatenate(ranks, axis=1).astype(I32)
    rank_ref[...] = rank
    onehot = jnp.concatenate(hots, axis=1)
    payload = jnp.concatenate(
        [
            cells_ref[...].astype(F32),
            offsets_ref[...],
            forces_ref[...],
            jnp.ones((1, markers), F32),
            jnp.zeros((6, markers), F32),
        ],
        axis=0,
    )
    parts = split3(payload)
    total = None
    for part in parts:
        rows = jnp.concatenate([jnp.where(rank == k, part, 0.0) for k in range(CAP)], axis=0)
        term = nt(onehot, rows.astype(BF16))
        total = term if total is None else total + term
    out_ref[...] = total


def pack(owner_row, cells, offsets, forces, devices):
    markers = owner_row.shape[1]
    return pl.pallas_call(
        pack_kernel,
        out_shape=(
            jax.ShapeDtypeStruct((devices, CAP * 16), F32),
            jax.ShapeDtypeStruct((1, markers), I32),
        ),
        in_specs=[vmem()] * 4,
        out_specs=(vmem(), vmem()),
        compiler_params=params(),
        cost_estimate=cost(4 * 10**8, 300_000),
        name="pack",
    )(owner_row, cells, offsets, forces)


def place_block(flat, start, count):
    return (flat == start + iota((count, flat.shape[1]), 0)).astype(F32).astype(BF16)


def sort_kernel(depth, rec_ref, list_ref, rank_ref, keys, pieces):
    devices = rec_ref.shape[0]
    slots = devices * CAP
    rec = rec_ref[...]
    flipped = rec.T
    empty = float(depth * 4096)

    def key_of(z, valid, index):
        low = jnp.where(z < 0.5, float(depth - 1), z - 1.0)
        return jnp.where(valid > 0.5, low * float(slots), empty) + index

    rows = []
    lane = iota((devices, 128), 1)
    for k in range(CAP):
        at = k * 16
        column = key_of(
            rec[:, at + 2 : at + 3],
            rec[:, at + 9 : at + 10],
            (iota((devices, 1), 0) + k * devices).astype(F32),
        )
        keys[k] = jnp.broadcast_to(column, (devices, devices))
        rows.append(
            key_of(
                flipped[at + 2 : at + 3, :],
                flipped[at + 9 : at + 10, :],
                (iota((1, devices), 1) + k * devices).astype(F32),
            )
        )
        half = rec[:, (k // 8) * 128 : (k // 8 + 1) * 128]
        turned = half if k % 8 == 0 else pltpu.roll(half, 128 - (k % 8) * 16, 1)
        hi, mid, lo = split3(turned)
        joined = jnp.where(
            lane < 16,
            hi,
            jnp.where(
                lane < 32, pltpu.roll(mid, 16, 1), jnp.where(lane < 48, pltpu.roll(lo, 32, 1), 0.0)
            ),
        )
        pieces[k * devices : (k + 1) * devices, :] = joined.astype(BF16)
    ranks = []
    for k in range(CAP):
        row = rows[k]

        def count(other, acc):
            return acc + jnp.where(keys[other] < row, 1.0, 0.0)

        acc = lax.fori_loop(0, CAP, count, jnp.zeros((devices, devices), F32))
        ranks.append(jnp.sum(acc, axis=0, keepdims=True).astype(I32))
    rank_ref[...] = jnp.concatenate(ranks, axis=0)
    flat = jnp.concatenate(ranks, axis=1)
    block = 256
    for b in range(slots // block):
        moved = nn(place_block(flat, b * block, block), pieces[...]).T
        rows = moved[0:16] + moved[16:32] + moved[32:48]
        z = rows[2:3]
        low = jnp.where(z < 0.5, float(depth - 1), z - 1.0)
        list_ref[:, b * block : (b + 1) * block] = jnp.where(
            iota((16, block), 0) == 2, low, rows
        )
    low = jnp.where(list_ref[9:10, :] > 0.5, list_ref[2:3, :], float(4 * depth))
    visit = (iota((VISITS, slots), 0) * 128).astype(F32)
    diagonal = iota((VISITS, 128), 0) == iota((VISITS, 128), 1)

    def count_below(bound):
        column = jnp.sum(jnp.where(low < bound, 1.0, 0.0), axis=1, keepdims=True)
        return jnp.sum(jnp.where(diagonal, column, 0.0), axis=0, keepdims=True)

    first = count_below(visit - 3.0)
    last = count_below(visit + 128.0)
    meta = jnp.where(iota((1, 128), 1) < VISITS, first, pltpu.roll(last, VISITS, 1))
    list_ref[10:11, 0:128] = meta


def sort(received, depth):
    devices = received.shape[0]
    slots = devices * CAP
    return pl.pallas_call(
        functools.partial(sort_kernel, depth),
        out_shape=(
            jax.ShapeDtypeStruct((16, slots), F32),
            jax.ShapeDtypeStruct((CAP, devices), I32),
        ),
        in_specs=[vmem()],
        out_specs=(vmem(), vmem()),
        scratch_shapes=[
            pltpu.VMEM((CAP, devices, devices), F32),
            pltpu.VMEM((slots, 128), BF16),
        ],
        compiler_params=params(),
        cost_estimate=cost(2 * 10**9, 300_000),
        name="sort",
    )(received)


def bump(frac):
    root = jnp.sqrt(1.0 + 4.0 * frac - 4.0 * frac * frac)
    return (
        (3.0 - 2.0 * frac - root) / 8.0,
        (3.0 - 2.0 * frac + root) / 8.0,
        (1.0 + 2.0 * frac + root) / 8.0,
        (1.0 + 2.0 * frac - root) / 8.0,
    )


def tent(first, weights, count, modulus=None):
    rows = iota((count, first.shape[1]), 0)
    table = 0.0
    for i in range(4):
        target = first + i
        if modulus is not None:
            target = jnp.bitwise_and(target, modulus - 1)
        table = jnp.where(rows == target, weights[i], table)
    return table


def markers_of(meta, index, visit, step, ref, at):
    slots = ref.shape[2]
    width = STEP + 128
    start = meta[index, visit] + STEP * step
    chunk = jnp.minimum(lax.shift_right_logical(start, 7), slots // 128 - width // 128)
    ahead = start - chunk * 128
    lanes = pl.ds(pl.multiple_of(chunk * 128, 128), width)
    part = pltpu.roll(ref[at, :, lanes], jnp.where(ahead == 0, 0, width - ahead), 1)[:, 0:STEP]
    live = iota((1, STEP), 1) < meta[index, VISITS + visit] - start
    return part, lanes, ahead, live


def window_of(part, live, window, depth):
    weights = [jnp.where(live, w, 0.0) for w in bump(part[5:6])]
    return tent(part[2:3].astype(I32) - window * 128, weights, 128, depth)


def plane_of(part, shift_x, rows_x, shift_y, rows_y):
    table_x = tent(part[0:1].astype(I32) + shift_x, bump(part[3:4]), -(-rows_x // 8) * 8)
    table_y = tent(part[1:2].astype(I32) + shift_y, bump(part[4:5]), rows_y)
    return table_x, table_y


def run_visits(one, lists, meta, windows, group):
    def length(dy, dx, visit):
        index = (dy + 1) * 3 + dx + 1
        return meta[index, VISITS + visit] - meta[index, visit]

    def turn(number, carry):
        most = 0
        for g in range(group):
            visit = number * group + g
            for dy, dx, ref in lists:
                one(dy, dx, ref, 0, visit)
                most = jnp.maximum(most, length(dy, dx, visit))

        @pl.when(most > STEP)
        def _():
            def again(visit, inner):
                for dy, dx, ref in lists:

                    def later(step, kept, dy=dy, dx=dx, ref=ref):
                        one(dy, dx, ref, step, visit)
                        return kept

                    steps = lax.shift_right_logical(length(dy, dx, visit) + STEP - 1, 8)
                    lax.fori_loop(1, steps, later, 0)
                return inner

            lax.fori_loop(number * group, (number + 1) * group, again, 0)

        return carry

    lax.fori_loop(0, (windows + 1) // group, turn, 0)


def spread_lists(size_x, size_y, meta, lists, outs, first_row, group):
    depth = next(iter(outs.values())).shape[3]
    windows = depth // 128
    rows_of = {-1: (0, 5), 0: (2, size_x + 3), 1: (size_x + 2, 4)}

    def clear(e, carry):
        for out_ref in outs.values():
            for c in range(3):
                out_ref[c, e] = jnp.zeros(out_ref.shape[2:], F32)
        return carry

    lax.fori_loop(0, size_x + 2 * HALO, clear, 0)

    def one(dy, dx, ref, step, visit):
            window = jnp.bitwise_and(visit, windows - 1)
            at = pl.ds(pl.multiple_of(window * 128, 128), 128)
            out_ref = outs[dy]
            index = (dy + 1) * 3 + dx + 1
            e0, rows = rows_of[dx]
            s0, cols, base = first_row[dy]
            part, _, _, live = markers_of(meta, index, visit, step, ref, dx + 1)
            both = jnp.concatenate(split2(window_of(part, live, window, depth).T), axis=1)
            right = jnp.concatenate([both, both], axis=0)
            table_x, table_y = plane_of(
                part, HALO - 1 + size_x * dx - e0, rows, PAD - 1 + size_y * dy - s0, cols
            )
            for c in range(3):
                pushed = table_y * part[6 + c : 7 + c]
                planar = jnp.concatenate(
                    [table_x[r : r + 1] * pushed for r in range(rows)], axis=0
                )
                sums = nn(jnp.concatenate(split2(planar), axis=1), right)
                sums = sums[:, 0:128] + sums[:, 128:256]
                for r in range(rows):
                    out_ref[c, e0 + r, base : base + cols, at] += sums[r * cols : (r + 1) * cols]

    run_visits(one, lists, meta, windows, group)


ROWS_MID = {0: (PAD - 1, 32, PAD - 1)}
ROWS_SIDE = {-1: (PAD - 3, 8, 0), 1: (32, 8, 0)}


def spread_mid_kernel(size_x, size_y, meta, mid_ref, out_ref):
    lists = [(0, dx, mid_ref) for dx in (0, -1, 1)]
    spread_lists(size_x, size_y, meta, lists, {0: out_ref}, ROWS_MID, GROUP_MID)


def spread_side_kernel(size_x, size_y, meta, low_ref, high_ref, out_low, out_high):
    lists = [(dy, dx, ref) for dy, ref in ((-1, low_ref), (1, high_ref)) for dx in (0, -1, 1)]
    outs = {-1: out_low, 1: out_high}
    spread_lists(size_x, size_y, meta, lists, outs, ROWS_SIDE, GROUP_SIDE)


def spread_mid(meta, mid, size_x, size_y, depth):
    return pl.pallas_call(
        functools.partial(spread_mid_kernel, size_x, size_y),
        out_shape=jax.ShapeDtypeStruct((3, size_x + 2 * HALO, YE, depth), F32),
        in_specs=[smem(), vmem()],
        out_specs=vmem(),
        compiler_params=params(),
        cost_estimate=cost(10**10, 10**7),
        name="spread_mid",
    )(meta, mid)


def spread_side(meta, low, high, size_x, size_y, depth):
    shape = jax.ShapeDtypeStruct((3, size_x + 2 * HALO, 8, depth), F32)
    return pl.pallas_call(
        functools.partial(spread_side_kernel, size_x, size_y),
        out_shape=(shape, shape),
        in_specs=[smem(), vmem(), vmem()],
        out_specs=(vmem(), vmem()),
        compiler_params=params(),
        cost_estimate=cost(10**10, 10**7),
        name="spread_side",
    )(meta, low, high)


def faces_kernel(vel_ref, visc_ref, x_up, x_down, y_up, y_down, x_up_late, x_down_late):
    size_x, size_y = visc_ref.shape[0], visc_ref.shape[1]
    for r in range(X_FIRST, X_LAYERS):
        up, down = (x_up, x_down) if r < X_EARLY else (x_up_late, x_down_late)
        at = r - X_FIRST if r < X_EARLY else r - X_EARLY
        rows = slice(at * size_y, (at + 1) * size_y)
        c, l = r // HALO, r % HALO
        if c < 3:
            up[rows, :] = vel_ref[c, size_x - HALO + l]
            down[rows, :] = vel_ref[c, l]
        else:
            up[rows, :] = visc_ref[size_x - HALO + 1 + l]
            down[rows, :] = visc_ref[l]
    for x in range(size_x):
        for c in range(3):
            r = (c * size_x + x) * HALO
            y_up[r : r + HALO, :] = vel_ref[c, x, size_y - HALO : size_y, :]
            y_down[r : r + HALO, :] = vel_ref[c, x, 0:HALO, :]
        r = 3 * size_x * HALO + x * (HALO - 1)
        y_up[r : r + HALO - 1, :] = visc_ref[x, size_y - HALO + 1 : size_y, :]
        y_down[r : r + HALO - 1, :] = visc_ref[x, 0 : HALO - 1, :]


def layer_of(first, early, late, r, size_y):
    if r < X_FIRST:
        return first[r]
    ref, at = (early, r - X_FIRST) if r < X_EARLY else (late, r - X_EARLY)
    return ref[at * size_y : (at + 1) * size_y, :]


X_LAYERS = 4 * HALO - 1
X_FIRST = 2
X_EARLY = 5


def face_rows(size_x, size_y):
    rows_y = 3 * size_x * HALO + size_x * (HALO - 1)
    rows = ((X_EARLY - X_FIRST) * size_y, rows_y, (X_LAYERS - X_EARLY) * size_y)
    return tuple(-(-number // 8) * 8 for number in rows)


def faces(velocity, viscosity):
    size_x, size_y, depth = viscosity.shape
    shapes = [jax.ShapeDtypeStruct((rows, depth), F32) for rows in face_rows(size_x, size_y)]
    return pl.pallas_call(
        faces_kernel,
        out_shape=[shape for shape in shapes for _ in range(2)],
        in_specs=[vmem(), vmem()],
        out_specs=[vmem()] * 6,
        compiler_params=params(),
        cost_estimate=cost(10**6, 10**7),
        name="faces",
    )(velocity, viscosity)


def corner_plan(up):
    plan, at = [], 0
    for r in range(X_LAYERS):
        c, l = r // HALO, r % HALO
        reach = HALO if c < 3 else HALO - 1
        away = reach - l if up else l + 1
        if reach > away:
            plan.append((r, reach - away, at))
            at += 2 * (reach - away)
    return plan, at


def late_kernel(size_x, up_ref, down_ref, y_low, y_high, up, down):
    thick = up_ref.shape[0]
    up[0:thick, :] = up_ref[...]
    down[0:thick, :] = down_ref[...]
    base = 3 * size_x * HALO
    thin = HALO - 1
    for out, is_up in ((up, True), (down, False)):
        for r, count, first in corner_plan(is_up)[0]:
            c, l = r // HALO, r % HALO
            x = l if not is_up else size_x - HALO + l + (1 if c == 3 else 0)
            deep, row = (HALO, (c * size_x + x) * HALO) if c < 3 else (thin, base + x * thin)
            at = thick + first
            out[at : at + count, :] = y_low[row + deep - count : row + deep, :]
            at = at + count
            out[at : at + count, :] = y_high[row : row + count, :]


def late_faces(up, down, y_low, y_high, size_x):
    thick = up.shape[0]
    rows = thick + -(-corner_plan(True)[1] // 8) * 8
    shape = jax.ShapeDtypeStruct((rows, up.shape[1]), F32)
    return pl.pallas_call(
        functools.partial(late_kernel, size_x),
        out_shape=(shape, shape),
        in_specs=[vmem()] * 4,
        out_specs=(vmem(), vmem()),
        compiler_params=params(),
        cost_estimate=cost(10**6, 4 * 10**6),
        name="late_faces",
    )(up, down, y_low, y_high)


def solve_kernel(
    sweeps,
    meta,
    spread_ref,
    side_low,
    side_high,
    vel_ref,
    visc_ref,
    x_low_first,
    x_high_first,
    x_low,
    x_high,
    x_low_late,
    x_high_late,
    y_low,
    y_high,
    low_ref,
    high_ref,
    new_ref,
    part_low,
    part_high,
    rhs,
    scaled,
    field,
    ratio,
    gathered,
):
    size_x, size_y, depth = visc_ref.shape
    ext = size_x + 2 * HALO
    own = slice(PAD, PAD + size_y)
    below = slice(PAD - HALO, PAD)
    above = slice(PAD + size_y, PAD + size_y + HALO)
    tiles = [slice(s, s + 8) for s in range(0, YE, 8)]
    thick = -(-(X_LAYERS - X_EARLY) * size_y // 8) * 8

    def clear(e, carry):
        for c in range(3):
            rhs[c, e, tiles[0]] = jnp.zeros((8, depth), F32)
            rhs[c, e, tiles[4]] = jnp.zeros((8, depth), F32)
        return carry

    lax.fori_loop(0, ext, clear, 0)

    def clear_ratio(e, carry):
        ratio[e, tiles[0]] = jnp.zeros((8, depth), F32)
        ratio[e, tiles[4]] = jnp.zeros((8, depth), F32)
        return carry

    lax.fori_loop(0, ext - 2, clear_ratio, 0)

    base = 3 * size_x * HALO
    thin = HALO - 1
    for x in range(size_x):
        e = x + HALO - 1
        ratio[e, own, :] = visc_ref[x]
        ratio[e, PAD - thin : PAD, :] = y_low[base + x * thin : base + (x + 1) * thin, :]
        ratio[e, PAD + size_y : PAD + size_y + thin, :] = y_high[
            base + x * thin : base + (x + 1) * thin, :
        ]
        for c in range(3):
            r = (c * size_x + x) * HALO
            rhs[c, x + HALO, own, :] = vel_ref[c, x]
            rhs[c, x + HALO, below, :] = y_low[r : r + HALO, :]
            rhs[c, x + HALO, above, :] = y_high[r : r + HALO, :]
    for side, start, early, late in (
        (0, x_low_first, x_low, x_low_late),
        (1, x_high_first, x_high, x_high_late),
    ):
        for r in range(X_LAYERS):
            c, l = r // HALO, r % HALO
            if c < 3:
                target = rhs.at[c, l if side == 0 else size_x + HALO + l]
            else:
                target = ratio.at[l if side == 0 else size_x + HALO - 1 + l]
            target[own, :] = layer_of(start, early, late, r, size_y)
        for r, count, first in corner_plan(side == 0)[0]:
            c, l = r // HALO, r % HALO
            if c < 3:
                target = rhs.at[c, l if side == 0 else size_x + HALO + l]
            else:
                target = ratio.at[l if side == 0 else size_x + HALO - 1 + l]
            at = thick + first
            target[PAD - count : PAD, :] = late[at : at + count, :]
            at = at + count
            target[PAD + size_y : PAD + size_y + count, :] = late[at : at + count, :]

    rows8 = iota((8, depth), 0)

    def total(c, e, s):
        value = rhs[c, e, tiles[s], :] + spread_ref[c, e, tiles[s], :]
        if s < 2:
            turned = pltpu.roll(side_low[c, e], PAD - 3, 0)
            keep = rows8 >= PAD - 3 if s == 0 else rows8 < PAD - 3
            value = value + jnp.where(keep, turned, 0.0)
        if s == 4:
            value = value + side_high[c, e]
        return value

    for e in (0, ext - 1):
        for c in range(3):
            for s in range(5):
                rhs[c, e, tiles[s], :] = total(c, e, s)

    def scale(e, carry):
        for s in range(5):
            nu = ratio[e - 1, tiles[s], :]
            inverse = 1.0 / (1.0 + 6.0 * nu)
            ratio[e - 1, tiles[s], :] = nu * inverse
            for c in range(3):
                value = total(c, e, s)
                rhs[c, e, tiles[s], :] = value
                scaled[c, e - 1, tiles[s], :] = value * inverse
        return carry

    lax.fori_loop(1, ext - 1, scale, 0)

    def sweep(source, offset, target, target_offset, first, last, write):
        def row(e, carry):
            for s in range(1 if write else 0, 5):
                factor = ratio[e - 1, tiles[s], :]
                for c in range(3):
                    here = source[c, e - offset, tiles[s], :]
                    beside = source[c, e + 1 - offset, tiles[s], :]
                    beside = beside + source[c, e - 1 - offset, tiles[s], :]
                    if s < 4:
                        beside = beside + source[c, e - offset, s * 8 + 1 : s * 8 + 9, :]
                    else:
                        beside = beside + pltpu.roll(here, 7, 0)
                    if s > 0:
                        beside = beside + source[c, e - offset, s * 8 - 1 : s * 8 + 7, :]
                    else:
                        beside = beside + pltpu.roll(here, 1, 0)
                    beside = beside + pltpu.roll(here, depth - 1, 1) + pltpu.roll(here, 1, 1)
                    value = scaled[c, e - 1, tiles[s], :] + factor * beside
                    if not write:
                        target[c, e - target_offset, tiles[s], :] = value
                    elif s == 4:
                        target[c, e - target_offset, 24:size_y, :] = value[0 : size_y - 24]
                    else:
                        target[c, e - target_offset, (s - 1) * 8 : s * 8, :] = value
            return carry

        lax.fori_loop(first, last, row, 0)

    sweep(rhs, 0, field, 1, 1, ext - 1, False)
    sweep(field, 1, rhs, 0, 2, ext - 2, False)
    sweep(rhs, 0, new_ref, HALO, 3, ext - 3, True)

    gathered[...] = jnp.zeros(gathered.shape, F32)
    lists = [(dy, dx, ref) for dy, ref in ((-1, low_ref), (1, high_ref)) for dx in (0, -1, 1)]
    outs = {(dy, dx): (dy + 1) // 2 * 3 + dx + 1 for dy, dx, _ in lists}
    sample_lists(meta, lists, new_ref, gathered, outs, GROUP_SIDE)
    for dx in range(3):
        part_low[dx * 3 : dx * 3 + 3, :] = gathered[dx, 0:3, :]
        part_high[dx * 3 : dx * 3 + 3, :] = gathered[3 + dx, 0:3, :]


def sample_lists(meta, lists, field, out_ref, outs, group):
    _, size_x, size_y, depth = field.shape
    windows = depth // 128
    whole = size_y // 8 * 8
    rows_of = {-1: (0, 2), 0: (0, size_x), 1: (size_x - 1, 1)}
    cols_of = {-1: (0, 8), 0: (0, whole + 8), 1: (whole, 8)}

    def values_of(c, x, dy, at):
        if dy == -1:
            return [field[c, x, 0:8, at]]
        tail = field[c, x, whole:size_y, at]
        tail = jnp.concatenate([tail, jnp.zeros((whole + 8 - size_y, 128), F32)], axis=0)
        return [tail] if dy == 1 else [field[c, x, 0:whole, at], tail]

    def one(dy, dx, ref, step, visit):
            window = jnp.bitwise_and(visit, windows - 1)
            at = pl.ds(pl.multiple_of(window * 128, 128), 128)
            index = (dy + 1) * 3 + dx + 1
            x0, rows = rows_of[dx]
            s0, cols = cols_of[dy]
            part, lanes, ahead, live = markers_of(meta, index, visit, step, ref, dx + 1)
            both = jnp.concatenate(split2(window_of(part, live, window, depth)), axis=1)
            right = jnp.concatenate([both, both], axis=0)
            table_x, table_y = plane_of(
                part, size_x * dx - 1 - x0, rows, size_y * dy - 1 - s0, cols
            )
            found = []
            for c in range(3):
                values = jnp.concatenate(
                    [v for r in range(rows) for v in values_of(c, x0 + r, dy, at)], axis=0
                )
                sums = nn(jnp.concatenate(split2(values), axis=1), right)
                sums = sums[:, 0:STEP] + sums[:, STEP : 2 * STEP]
                mixed = jnp.zeros((cols, STEP), F32)
                for r in range(rows):
                    mixed = mixed + table_x[r : r + 1] * sums[r * cols : (r + 1) * cols]
                total = jnp.sum(mixed * table_y, axis=0, keepdims=True)
                found.append(jnp.where(live, total, 0.0))
            found = jnp.concatenate([*found, jnp.zeros((5, STEP), F32)], axis=0)
            found = jnp.concatenate([found, jnp.zeros((8, 128), F32)], axis=1)
            out_ref[outs[dy, dx], :, lanes] += pltpu.roll(found, ahead, 1)

    run_visits(one, lists, meta, windows, group)


def sample_kernel(places, meta, mid_ref, field, out_ref):
    out_ref[...] = jnp.zeros(out_ref.shape, F32)
    lists = [(0, dx, mid_ref) for dx in places]
    sample_lists(meta, lists, field, out_ref, {(0, dx): i for i, dx in enumerate(places)}, 3)


def sample(meta, mid, field, places):
    return pl.pallas_call(
        functools.partial(sample_kernel, places),
        out_shape=jax.ShapeDtypeStruct((len(places), 8, mid.shape[2]), F32),
        in_specs=[smem(), vmem(), vmem()],
        out_specs=vmem(),
        compiler_params=params(),
        cost_estimate=cost(5 * 10**9, 5 * 10**6),
        name="sample",
    )(meta, mid, field)


def solve(sweeps, meta, spreads, velocity, viscosity, halos, lists):
    size_x, size_y, depth = viscosity.shape
    ext = size_x + 2 * HALO
    slots = lists[0].shape[2]
    partial = jax.ShapeDtypeStruct((9, slots), F32)
    return pl.pallas_call(
        functools.partial(solve_kernel, sweeps),
        out_shape=(jax.ShapeDtypeStruct(velocity.shape, F32), partial, partial),
        in_specs=[smem()] + [vmem()] * 15,
        out_specs=(vmem(),) * 3,
        scratch_shapes=[
            pltpu.VMEM((3, ext, YE, depth), F32),
            pltpu.VMEM((3, ext - 2, YE, depth), F32),
            pltpu.VMEM((3, ext - 2, YE, depth), F32),
            pltpu.VMEM((ext - 2, YE, depth), F32),
            pltpu.VMEM((6, 8, slots), F32),
        ],
        compiler_params=params(),
        cost_estimate=cost(10**10, 2 * 10**7),
        name="solve",
    )(meta, *spreads, velocity, viscosity, *halos, *lists)


def unsort_kernel(own_ref, sides_ref, low_ref, high_ref, rank_ref, out_ref):
    devices = out_ref.shape[0]
    slots = sides_ref.shape[1]
    total = own_ref[0, 0:3, :] + sides_ref[3:6, :] + low_ref[...] + high_ref[...]
    total = jnp.concatenate([total, jnp.zeros((5, slots), F32)], axis=0)
    flat = jnp.concatenate([rank_ref[k : k + 1, :] for k in range(CAP)], axis=1)
    block = 256
    sums = jnp.zeros((32, slots), F32)
    for b in range(slots // block):
        values = total[:, b * block : (b + 1) * block]
        parts = jnp.concatenate([*split3(values), jnp.zeros_like(values)], axis=0)
        sums = sums + nn(parts.astype(BF16), place_block(flat, b * block, block))
    rows = sums[0:8] + sums[8:16] + sums[16:24]
    turned = jnp.concatenate(
        [rows[:, k * devices : (k + 1) * devices] for k in range(CAP)], axis=0
    )
    out_ref[...] = turned.T


def unsort(own, sides, low, high, rank):
    devices = rank.shape[1]
    return pl.pallas_call(
        unsort_kernel,
        out_shape=jax.ShapeDtypeStruct((devices, CAP * 8), F32),
        in_specs=[vmem()] * 5,
        out_specs=vmem(),
        compiler_params=params(),
        cost_estimate=cost(10**9, 300_000),
        name="unsort",
    )(own, sides, low, high, rank)


def unpack_kernel(owner_ref, rank_ref, back_ref, out_ref):
    markers = owner_ref.shape[1]
    devices = back_ref.shape[0]
    onehot = (iota((devices, markers), 0) == owner_ref[...]).astype(F32).astype(BF16)
    rank = rank_ref[...]
    turned = back_ref[...].T
    picked = None
    for part in split3(turned):
        term = nn(part.astype(BF16), onehot)
        picked = term if picked is None else picked + term
    total = jnp.zeros((8, markers), F32)
    for k in range(CAP):
        total = total + jnp.where(rank == k, picked[k * 8 : (k + 1) * 8], 0.0)
    out_ref[...] = total[0:3]


def unpack(owner_row, rank, back):
    markers = owner_row.shape[1]
    return pl.pallas_call(
        unpack_kernel,
        out_shape=jax.ShapeDtypeStruct((3, markers), F32),
        in_specs=[vmem()] * 3,
        out_specs=vmem(),
        compiler_params=params(),
        cost_estimate=cost(10**8, 100_000),
        name="unpack",
    )(owner_row, rank, back)


def shift_up(x, axis):
    count = lax.axis_size(axis)
    return lax.ppermute(x, axis, [(i, (i + 1) % count) for i in range(count)])


def shift_down(x, axis):
    count = lax.axis_size(axis)
    return lax.ppermute(x, axis, [((i + 1) % count, i) for i in range(count)])


def shards(velocity, viscosity, cells, offsets, forces, owners):
    devices = lax.axis_size("gx") * lax.axis_size("gy")
    size_x, size_y, depth = viscosity.shape
    markers = owners.shape[0]
    owner_row = owners.reshape(1, markers)
    both = ("gx", "gy")

    x_low_first = shift_up(velocity[0, size_x - HALO : size_x - HALO + X_FIRST], "gx")
    x_high_first = shift_down(velocity[0, 0:X_FIRST], "gx")
    outgoing, rank = pack(owner_row, cells, offsets, forces, devices)
    outgoing, face_source = lax.optimization_barrier((outgoing, viscosity))
    received = lax.all_to_all(outgoing, both, split_axis=0, concat_axis=0, tiled=True)
    x_up, x_down, y_up, y_down, x_up_late, x_down_late = faces(velocity, face_source)
    received, x_low_first, x_high_first, x_up, x_down, y_up, y_down = lax.optimization_barrier(
        (received, x_low_first, x_high_first, x_up, x_down, y_up, y_down)
    )
    x_low = shift_up(x_up, "gx")
    x_high = shift_down(x_down, "gx")
    y_low = shift_up(y_up, "gy")
    y_high = shift_down(y_down, "gy")
    markers_list, order = sort(received, depth)
    markers_list, x_low, x_high, y_low, y_high = lax.optimization_barrier(
        (markers_list, x_low, x_high, y_low, y_high)
    )
    list_low = shift_up(markers_list, "gx")
    list_high = shift_down(markers_list, "gx")
    x_up_late, x_down_late = late_faces(x_up_late, x_down_late, y_low, y_high, size_x)
    mid = jnp.stack([list_low, markers_list, list_high])
    mid, x_up_late, x_down_late = lax.optimization_barrier((mid, x_up_late, x_down_late))
    x_low_late = shift_up(x_up_late, "gx")
    x_high_late = shift_down(x_down_late, "gx")
    low = shift_up(mid, "gy")
    high = shift_down(mid, "gy")
    halos = (x_low_first, x_high_first, x_low, x_high, x_low_late, x_high_late, y_low, y_high)
    meta_mid = mid[:, 10, 0:64].astype(I32)
    meta_mid = jnp.pad(meta_mid, ((3, 3), (0, 0)))
    spread_own = spread_mid(meta_mid, mid, size_x, size_y, depth)
    low, high, spread_own = lax.optimization_barrier((low, high, spread_own))
    meta = jnp.concatenate([part[:, 10, 0:64] for part in (low, mid, high)], axis=0).astype(I32)
    spreads = (spread_own, *spread_side(meta, low, high, size_x, size_y, depth))
    halos, spreads = lax.optimization_barrier((halos, spreads))
    field, part_low, part_high = solve(
        3, meta, spreads, velocity, viscosity, halos, (low, high)
    )
    beside = sample(meta, mid, field, (-1, 1))
    sides = shift_down(part_low, "gy") + shift_up(part_high, "gy")
    to_low = sides[0:3] + beside[0, 0:3]
    to_high = sides[6:9] + beside[1, 0:3]
    to_low, to_high, field_own = lax.optimization_barrier((to_low, to_high, field))
    own = sample(meta, mid, field_own, (0,))
    back = unsort(own, sides, shift_down(to_low, "gx"), shift_up(to_high, "gx"), order)
    back = lax.all_to_all(back, both, split_axis=0, concat_axis=0, tiled=True)
    return (field, unpack(owner_row, rank, back))


def solution(mesh):
    in_specs = (
        P(None, "gx", "gy", None),
        P("gx", "gy", None),
        P(None, ("gx", "gy")),
        P(None, ("gx", "gy")),
        P(None, ("gx", "gy")),
        P(("gx", "gy"), None),
    )
    out_specs = (P(None, "gx", "gy", None), P(None, ("gx", "gy")))
    return jax.shard_map(shards, mesh=mesh, in_specs=in_specs, out_specs=out_specs, check_vma=False)
```

```python
import functools

import jax
import jax.numpy as jnp
from jax import lax
from jax.experimental import pallas as pl
from jax.experimental.pallas import tpu as pltpu
from jax.sharding import PartitionSpec as P

F32 = jnp.float32
BF16 = jnp.bfloat16
I32 = jnp.int32
LIMIT = 60 * 1024 * 1024
CAP = 16
HALO = 3
PAD = 8
YE = 40
VISITS = 16
STEP = 256
GROUP_MID = 3
GROUP_SIDE = 3


def split3(x):
    hi = x.astype(BF16).astype(F32)
    rest = x - hi
    mid = rest.astype(BF16).astype(F32)
    return hi, mid, rest - mid


def split2(x):
    hi = x.astype(BF16)
    return hi, (x - hi.astype(F32)).astype(BF16)


def nn(a, b):
    return lax.dot_general(a, b, (((1,), (0,)), ((), ())), preferred_element_type=F32)


def nt(a, b):
    return lax.dot_general(a, b, (((1,), (1,)), ((), ())), preferred_element_type=F32)


def tn(a, b):
    return lax.dot_general(a, b, (((0,), (0,)), ((), ())), preferred_element_type=F32)


def iota(shape, dim):
    return lax.broadcasted_iota(I32, shape, dim)


def vmem():
    return pl.BlockSpec(memory_space=pltpu.VMEM)


def smem():
    return pl.BlockSpec(memory_space=pltpu.SMEM)


def params():
    return pltpu.CompilerParams(vmem_limit_bytes=LIMIT)


def cost(flops, size):
    return pl.CostEstimate(flops=flops, bytes_accessed=size, transcendentals=0)


def pack_kernel(owner_ref, cells_ref, offsets_ref, forces_ref, out_ref, rank_ref):
    markers = owner_ref.shape[1]
    devices = out_ref.shape[0]
    owner = owner_ref[...]
    before = (iota((128, 128), 0) < iota((128, 128), 1)).astype(BF16)
    running = jnp.zeros((devices, 1), F32)
    ranks = []
    hots = []
    for g in range(markers // 128):
        hot = (iota((devices, 128), 0) == owner[:, g * 128 : (g + 1) * 128]).astype(F32)
        within = nn(hot.astype(BF16), before)
        ranks.append(jnp.sum(hot * (within + running), axis=0, keepdims=True))
        running = running + jnp.sum(hot, axis=1, keepdims=True)
        hots.append(hot.astype(BF16))
    rank = jnp.concatenate(ranks, axis=1).astype(I32)
    rank_ref[...] = rank
    onehot = jnp.concatenate(hots, axis=1)
    payload = jnp.concatenate(
        [
            cells_ref[...].astype(F32),
            offsets_ref[...],
            forces_ref[...],
            jnp.ones((1, markers), F32),
            jnp.zeros((6, markers), F32),
        ],
        axis=0,
    )
    parts = split3(payload)
    total = None
    for part in parts:
        rows = jnp.concatenate([jnp.where(rank == k, part, 0.0) for k in range(CAP)], axis=0)
        term = nt(onehot, rows.astype(BF16))
        total = term if total is None else total + term
    out_ref[...] = total


def pack(owner_row, cells, offsets, forces, devices):
    markers = owner_row.shape[1]
    return pl.pallas_call(
        pack_kernel,
        out_shape=(
            jax.ShapeDtypeStruct((devices, CAP * 16), F32),
            jax.ShapeDtypeStruct((1, markers), I32),
        ),
        in_specs=[vmem()] * 4,
        out_specs=(vmem(), vmem()),
        compiler_params=params(),
        cost_estimate=cost(4 * 10**8, 300_000),
        name="pack",
    )(owner_row, cells, offsets, forces)


def place_block(flat, start, count):
    return (flat == start + iota((count, flat.shape[1]), 0)).astype(F32).astype(BF16)


def sort_kernel(depth, rec_ref, list_ref, rank_ref, keys, pieces):
    devices = rec_ref.shape[0]
    slots = devices * CAP
    rec = rec_ref[...]
    flipped = rec.T
    empty = float(depth * 4096)

    def key_of(z, valid, index):
        low = jnp.where(z < 0.5, float(depth - 1), z - 1.0)
        return jnp.where(valid > 0.5, low * float(slots), empty) + index

    rows = []
    lane = iota((devices, 128), 1)
    for k in range(CAP):
        at = k * 16
        column = key_of(
            rec[:, at + 2 : at + 3],
            rec[:, at + 9 : at + 10],
            (iota((devices, 1), 0) + k * devices).astype(F32),
        )
        keys[k] = jnp.broadcast_to(column, (devices, devices))
        rows.append(
            key_of(
                flipped[at + 2 : at + 3, :],
                flipped[at + 9 : at + 10, :],
                (iota((1, devices), 1) + k * devices).astype(F32),
            )
        )
        half = rec[:, (k // 8) * 128 : (k // 8 + 1) * 128]
        turned = half if k % 8 == 0 else pltpu.roll(half, 128 - (k % 8) * 16, 1)
        hi, mid, lo = split3(turned)
        joined = jnp.where(
            lane < 16,
            hi,
            jnp.where(
                lane < 32, pltpu.roll(mid, 16, 1), jnp.where(lane < 48, pltpu.roll(lo, 32, 1), 0.0)
            ),
        )
        pieces[k * devices : (k + 1) * devices, :] = joined.astype(BF16)
    ranks = []
    for k in range(CAP):
        row = rows[k]

        def count(other, acc):
            return acc + jnp.where(keys[other] < row, 1.0, 0.0)

        acc = lax.fori_loop(0, CAP, count, jnp.zeros((devices, devices), F32))
        ranks.append(jnp.sum(acc, axis=0, keepdims=True).astype(I32))
    rank_ref[...] = jnp.concatenate(ranks, axis=0)
    flat = jnp.concatenate(ranks, axis=1)
    block = 256
    for b in range(slots // block):
        moved = nn(place_block(flat, b * block, block), pieces[...]).T
        rows = moved[0:16] + moved[16:32] + moved[32:48]
        z = rows[2:3]
        low = jnp.where(z < 0.5, float(depth - 1), z - 1.0)
        list_ref[:, b * block : (b + 1) * block] = jnp.where(
            iota((16, block), 0) == 2, low, rows
        )
    low = jnp.where(list_ref[9:10, :] > 0.5, list_ref[2:3, :], float(4 * depth))
    visit = (iota((VISITS, slots), 0) * 128).astype(F32)
    diagonal = iota((VISITS, 128), 0) == iota((VISITS, 128), 1)

    def count_below(bound):
        column = jnp.sum(jnp.where(low < bound, 1.0, 0.0), axis=1, keepdims=True)
        return jnp.sum(jnp.where(diagonal, column, 0.0), axis=0, keepdims=True)

    first = count_below(visit - 3.0)
    last = count_below(visit + 128.0)
    meta = jnp.where(iota((1, 128), 1) < VISITS, first, pltpu.roll(last, VISITS, 1))
    list_ref[10:11, 0:128] = meta


def sort(received, depth):
    devices = received.shape[0]
    slots = devices * CAP
    return pl.pallas_call(
        functools.partial(sort_kernel, depth),
        out_shape=(
            jax.ShapeDtypeStruct((16, slots), F32),
            jax.ShapeDtypeStruct((CAP, devices), I32),
        ),
        in_specs=[vmem()],
        out_specs=(vmem(), vmem()),
        scratch_shapes=[
            pltpu.VMEM((CAP, devices, devices), F32),
            pltpu.VMEM((slots, 128), BF16),
        ],
        compiler_params=params(),
        cost_estimate=cost(2 * 10**9, 300_000),
        name="sort",
    )(received)


def bump(frac):
    root = jnp.sqrt(1.0 + 4.0 * frac - 4.0 * frac * frac)
    return (
        (3.0 - 2.0 * frac - root) / 8.0,
        (3.0 - 2.0 * frac + root) / 8.0,
        (1.0 + 2.0 * frac + root) / 8.0,
        (1.0 + 2.0 * frac - root) / 8.0,
    )


def tent(first, weights, count, modulus=None):
    rows = iota((count, first.shape[1]), 0)
    table = 0.0
    for i in range(4):
        target = first + i
        if modulus is not None:
            target = jnp.bitwise_and(target, modulus - 1)
        table = jnp.where(rows == target, weights[i], table)
    return table


def markers_of(meta, index, visit, step, ref, at):
    slots = ref.shape[2]
    width = STEP + 128
    start = meta[index, visit] + STEP * step
    chunk = jnp.minimum(lax.shift_right_logical(start, 7), slots // 128 - width // 128)
    ahead = start - chunk * 128
    lanes = pl.ds(pl.multiple_of(chunk * 128, 128), width)
    part = pltpu.roll(ref[at, :, lanes], jnp.where(ahead == 0, 0, width - ahead), 1)[:, 0:STEP]
    live = iota((1, STEP), 1) < meta[index, VISITS + visit] - start
    return part, lanes, ahead, live


def window_of(part, live, window, depth):
    weights = [jnp.where(live, w, 0.0) for w in bump(part[5:6])]
    return tent(part[2:3].astype(I32) - window * 128, weights, 128, depth)


def plane_of(part, shift_x, rows_x, shift_y, rows_y):
    table_x = tent(part[0:1].astype(I32) + shift_x, bump(part[3:4]), -(-rows_x // 8) * 8)
    table_y = tent(part[1:2].astype(I32) + shift_y, bump(part[4:5]), rows_y)
    return table_x, table_y


def run_visits(one, lists, meta, windows, group):
    def length(dy, dx, visit):
        index = (dy + 1) * 3 + dx + 1
        return meta[index, VISITS + visit] - meta[index, visit]

    def turn(number, carry):
        most = 0
        for g in range(group):
            visit = number * group + g
            for dy, dx, ref in lists:
                one(dy, dx, ref, 0, visit)
                most = jnp.maximum(most, length(dy, dx, visit))

        @pl.when(most > STEP)
        def _():
            def again(visit, inner):
                for dy, dx, ref in lists:

                    def later(step, kept, dy=dy, dx=dx, ref=ref):
                        one(dy, dx, ref, step, visit)
                        return kept

                    steps = lax.shift_right_logical(length(dy, dx, visit) + STEP - 1, 8)
                    lax.fori_loop(1, steps, later, 0)
                return inner

            lax.fori_loop(number * group, (number + 1) * group, again, 0)

        return carry

    lax.fori_loop(0, (windows + 1) // group, turn, 0)


def spread_lists(size_x, size_y, meta, lists, outs, first_row, group):
    depth = next(iter(outs.values())).shape[3]
    windows = depth // 128
    rows_of = {-1: (0, 5), 0: (2, size_x + 3), 1: (size_x + 2, 4)}

    def clear(e, carry):
        for out_ref in outs.values():
            for c in range(3):
                out_ref[c, e] = jnp.zeros(out_ref.shape[2:], F32)
        return carry

    lax.fori_loop(0, size_x + 2 * HALO, clear, 0)

    def one(dy, dx, ref, step, visit):
            window = jnp.bitwise_and(visit, windows - 1)
            at = pl.ds(pl.multiple_of(window * 128, 128), 128)
            out_ref = outs[dy]
            index = (dy + 1) * 3 + dx + 1
            e0, rows = rows_of[dx]
            s0, cols, base = first_row[dy]
            part, _, _, live = markers_of(meta, index, visit, step, ref, dx + 1)
            both = jnp.concatenate(split2(window_of(part, live, window, depth).T), axis=1)
            right = jnp.concatenate([both, both], axis=0)
            table_x, table_y = plane_of(
                part, HALO - 1 + size_x * dx - e0, rows, PAD - 1 + size_y * dy - s0, cols
            )
            for c in range(3):
                pushed = table_y * part[6 + c : 7 + c]
                planar = jnp.concatenate(
                    [table_x[r : r + 1] * pushed for r in range(rows)], axis=0
                )
                sums = nn(jnp.concatenate(split2(planar), axis=1), right)
                sums = sums[:, 0:128] + sums[:, 128:256]
                for r in range(rows):
                    out_ref[c, e0 + r, base : base + cols, at] += sums[r * cols : (r + 1) * cols]

    run_visits(one, lists, meta, windows, group)


ROWS_MID = {0: (PAD - 1, 32, PAD - 1)}
ROWS_SIDE = {-1: (PAD - 3, 8, 0), 1: (32, 8, 0)}


def spread_mid_kernel(size_x, size_y, meta, mid_ref, out_ref):
    lists = [(0, dx, mid_ref) for dx in (0, -1, 1)]
    spread_lists(size_x, size_y, meta, lists, {0: out_ref}, ROWS_MID, GROUP_MID)


def spread_side_kernel(size_x, size_y, meta, low_ref, high_ref, out_low, out_high):
    lists = [(dy, dx, ref) for dy, ref in ((-1, low_ref), (1, high_ref)) for dx in (0, -1, 1)]
    outs = {-1: out_low, 1: out_high}
    spread_lists(size_x, size_y, meta, lists, outs, ROWS_SIDE, GROUP_SIDE)


def spread_mid(meta, mid, size_x, size_y, depth):
    return pl.pallas_call(
        functools.partial(spread_mid_kernel, size_x, size_y),
        out_shape=jax.ShapeDtypeStruct((3, size_x + 2 * HALO, YE, depth), F32),
        in_specs=[smem(), vmem()],
        out_specs=vmem(),
        compiler_params=params(),
        cost_estimate=cost(10**10, 10**7),
        name="spread_mid",
    )(meta, mid)


def spread_side(meta, low, high, size_x, size_y, depth):
    shape = jax.ShapeDtypeStruct((3, size_x + 2 * HALO, 8, depth), F32)
    return pl.pallas_call(
        functools.partial(spread_side_kernel, size_x, size_y),
        out_shape=(shape, shape),
        in_specs=[smem(), vmem(), vmem()],
        out_specs=(vmem(), vmem()),
        compiler_params=params(),
        cost_estimate=cost(10**10, 10**7),
        name="spread_side",
    )(meta, low, high)


def faces_kernel(vel_ref, visc_ref, x_up, x_down, y_up, y_down, x_up_late, x_down_late):
    size_x, size_y = visc_ref.shape[0], visc_ref.shape[1]
    for r in range(X_FIRST, X_LAYERS):
        up, down = (x_up, x_down) if r < X_EARLY else (x_up_late, x_down_late)
        at = r - X_FIRST if r < X_EARLY else r - X_EARLY
        rows = slice(at * size_y, (at + 1) * size_y)
        c, l = r // HALO, r % HALO
        if c < 3:
            up[rows, :] = vel_ref[c, size_x - HALO + l]
            down[rows, :] = vel_ref[c, l]
        else:
            up[rows, :] = visc_ref[size_x - HALO + 1 + l]
            down[rows, :] = visc_ref[l]
    for x in range(size_x):
        for c in range(3):
            r = (c * size_x + x) * HALO
            y_up[r : r + HALO, :] = vel_ref[c, x, size_y - HALO : size_y, :]
            y_down[r : r + HALO, :] = vel_ref[c, x, 0:HALO, :]
        r = 3 * size_x * HALO + x * (HALO - 1)
        y_up[r : r + HALO - 1, :] = visc_ref[x, size_y - HALO + 1 : size_y, :]
        y_down[r : r + HALO - 1, :] = visc_ref[x, 0 : HALO - 1, :]


def layer_of(first, early, late, r, size_y):
    if r < X_FIRST:
        return first[r]
    ref, at = (early, r - X_FIRST) if r < X_EARLY else (late, r - X_EARLY)
    return ref[at * size_y : (at + 1) * size_y, :]


X_LAYERS = 4 * HALO - 1
X_FIRST = 2
X_EARLY = 4


def face_rows(size_x, size_y):
    rows_y = 3 * size_x * HALO + size_x * (HALO - 1)
    rows = ((X_EARLY - X_FIRST) * size_y, rows_y, (X_LAYERS - X_EARLY) * size_y)
    return tuple(-(-number // 8) * 8 for number in rows)


def faces(velocity, viscosity):
    size_x, size_y, depth = viscosity.shape
    shapes = [jax.ShapeDtypeStruct((rows, depth), F32) for rows in face_rows(size_x, size_y)]
    return pl.pallas_call(
        faces_kernel,
        out_shape=[shape for shape in shapes for _ in range(2)],
        in_specs=[vmem(), vmem()],
        out_specs=[vmem()] * 6,
        compiler_params=params(),
        cost_estimate=cost(10**6, 10**7),
        name="faces",
    )(velocity, viscosity)


def corner_plan(up):
    plan, at = [], 0
    for r in range(X_LAYERS):
        c, l = r // HALO, r % HALO
        reach = HALO if c < 3 else HALO - 1
        away = reach - l if up else l + 1
        if reach > away:
            plan.append((r, reach - away, at))
            at += 2 * (reach - away)
    return plan, at


def late_kernel(size_x, up_ref, down_ref, y_low, y_high, up, down):
    thick = up_ref.shape[0]
    up[0:thick, :] = up_ref[...]
    down[0:thick, :] = down_ref[...]
    base = 3 * size_x * HALO
    thin = HALO - 1
    for out, is_up in ((up, True), (down, False)):
        for r, count, first in corner_plan(is_up)[0]:
            c, l = r // HALO, r % HALO
            x = l if not is_up else size_x - HALO + l + (1 if c == 3 else 0)
            deep, row = (HALO, (c * size_x + x) * HALO) if c < 3 else (thin, base + x * thin)
            at = thick + first
            out[at : at + count, :] = y_low[row + deep - count : row + deep, :]
            at = at + count
            out[at : at + count, :] = y_high[row : row + count, :]


def late_faces(up, down, y_low, y_high, size_x):
    thick = up.shape[0]
    rows = thick + -(-corner_plan(True)[1] // 8) * 8
    shape = jax.ShapeDtypeStruct((rows, up.shape[1]), F32)
    return pl.pallas_call(
        functools.partial(late_kernel, size_x),
        out_shape=(shape, shape),
        in_specs=[vmem()] * 4,
        out_specs=(vmem(), vmem()),
        compiler_params=params(),
        cost_estimate=cost(10**6, 4 * 10**6),
        name="late_faces",
    )(up, down, y_low, y_high)


def solve_kernel(
    sweeps,
    meta,
    spread_ref,
    side_low,
    side_high,
    vel_ref,
    visc_ref,
    x_low_first,
    x_high_first,
    x_low,
    x_high,
    x_low_late,
    x_high_late,
    y_low,
    y_high,
    low_ref,
    high_ref,
    new_ref,
    part_low,
    part_high,
    rhs,
    scaled,
    field,
    ratio,
    gathered,
):
    size_x, size_y, depth = visc_ref.shape
    ext = size_x + 2 * HALO
    own = slice(PAD, PAD + size_y)
    below = slice(PAD - HALO, PAD)
    above = slice(PAD + size_y, PAD + size_y + HALO)
    tiles = [slice(s, s + 8) for s in range(0, YE, 8)]
    thick = -(-(X_LAYERS - X_EARLY) * size_y // 8) * 8

    def clear(e, carry):
        for c in range(3):
            rhs[c, e, tiles[0]] = jnp.zeros((8, depth), F32)
            rhs[c, e, tiles[4]] = jnp.zeros((8, depth), F32)
        return carry

    lax.fori_loop(0, ext, clear, 0)

    def clear_ratio(e, carry):
        ratio[e, tiles[0]] = jnp.zeros((8, depth), F32)
        ratio[e, tiles[4]] = jnp.zeros((8, depth), F32)
        return carry

    lax.fori_loop(0, ext - 2, clear_ratio, 0)

    base = 3 * size_x * HALO
    thin = HALO - 1
    for x in range(size_x):
        e = x + HALO - 1
        ratio[e, own, :] = visc_ref[x]
        ratio[e, PAD - thin : PAD, :] = y_low[base + x * thin : base + (x + 1) * thin, :]
        ratio[e, PAD + size_y : PAD + size_y + thin, :] = y_high[
            base + x * thin : base + (x + 1) * thin, :
        ]
        for c in range(3):
            r = (c * size_x + x) * HALO
            rhs[c, x + HALO, own, :] = vel_ref[c, x]
            rhs[c, x + HALO, below, :] = y_low[r : r + HALO, :]
            rhs[c, x + HALO, above, :] = y_high[r : r + HALO, :]
    for side, start, early, late in (
        (0, x_low_first, x_low, x_low_late),
        (1, x_high_first, x_high, x_high_late),
    ):
        for r in range(X_LAYERS):
            c, l = r // HALO, r % HALO
            if c < 3:
                target = rhs.at[c, l if side == 0 else size_x + HALO + l]
            else:
                target = ratio.at[l if side == 0 else size_x + HALO - 1 + l]
            target[own, :] = layer_of(start, early, late, r, size_y)
        for r, count, first in corner_plan(side == 0)[0]:
            c, l = r // HALO, r % HALO
            if c < 3:
                target = rhs.at[c, l if side == 0 else size_x + HALO + l]
            else:
                target = ratio.at[l if side == 0 else size_x + HALO - 1 + l]
            at = thick + first
            target[PAD - count : PAD, :] = late[at : at + count, :]
            at = at + count
            target[PAD + size_y : PAD + size_y + count, :] = late[at : at + count, :]

    rows8 = iota((8, depth), 0)

    def total(c, e, s):
        value = rhs[c, e, tiles[s], :] + spread_ref[c, e, tiles[s], :]
        if s < 2:
            turned = pltpu.roll(side_low[c, e], PAD - 3, 0)
            keep = rows8 >= PAD - 3 if s == 0 else rows8 < PAD - 3
            value = value + jnp.where(keep, turned, 0.0)
        if s == 4:
            value = value + side_high[c, e]
        return value

    for e in (0, ext - 1):
        for c in range(3):
            for s in range(5):
                rhs[c, e, tiles[s], :] = total(c, e, s)

    def scale(e, carry):
        for s in range(5):
            nu = ratio[e - 1, tiles[s], :]
            inverse = 1.0 / (1.0 + 6.0 * nu)
            ratio[e - 1, tiles[s], :] = nu * inverse
            for c in range(3):
                value = total(c, e, s)
                rhs[c, e, tiles[s], :] = value
                scaled[c, e - 1, tiles[s], :] = value * inverse
        return carry

    lax.fori_loop(1, ext - 1, scale, 0)

    def sweep(source, offset, target, target_offset, first, last, write):
        def row(e, carry):
            for s in range(1 if write else 0, 5):
                factor = ratio[e - 1, tiles[s], :]
                for c in range(3):
                    here = source[c, e - offset, tiles[s], :]
                    beside = source[c, e + 1 - offset, tiles[s], :]
                    beside = beside + source[c, e - 1 - offset, tiles[s], :]
                    if s < 4:
                        beside = beside + source[c, e - offset, s * 8 + 1 : s * 8 + 9, :]
                    else:
                        beside = beside + pltpu.roll(here, 7, 0)
                    if s > 0:
                        beside = beside + source[c, e - offset, s * 8 - 1 : s * 8 + 7, :]
                    else:
                        beside = beside + pltpu.roll(here, 1, 0)
                    beside = beside + pltpu.roll(here, depth - 1, 1) + pltpu.roll(here, 1, 1)
                    value = scaled[c, e - 1, tiles[s], :] + factor * beside
                    if not write:
                        target[c, e - target_offset, tiles[s], :] = value
                    elif s == 4:
                        target[c, e - target_offset, 24:size_y, :] = value[0 : size_y - 24]
                    else:
                        target[c, e - target_offset, (s - 1) * 8 : s * 8, :] = value
            return carry

        lax.fori_loop(first, last, row, 0)

    sweep(rhs, 0, field, 1, 1, ext - 1, False)
    sweep(field, 1, rhs, 0, 2, ext - 2, False)
    sweep(rhs, 0, new_ref, HALO, 3, ext - 3, True)

    gathered[...] = jnp.zeros(gathered.shape, F32)
    lists = [(dy, dx, ref) for dy, ref in ((-1, low_ref), (1, high_ref)) for dx in (0, -1, 1)]
    outs = {(dy, dx): (dy + 1) // 2 * 3 + dx + 1 for dy, dx, _ in lists}
    sample_lists(meta, lists, new_ref, gathered, outs, GROUP_SIDE)
    for dx in range(3):
        part_low[dx * 3 : dx * 3 + 3, :] = gathered[dx, 0:3, :]
        part_high[dx * 3 : dx * 3 + 3, :] = gathered[3 + dx, 0:3, :]


def sample_lists(meta, lists, field, out_ref, outs, group):
    _, size_x, size_y, depth = field.shape
    windows = depth // 128
    whole = size_y // 8 * 8
    rows_of = {-1: (0, 2), 0: (0, size_x), 1: (size_x - 1, 1)}
    cols_of = {-1: (0, 8), 0: (0, whole + 8), 1: (whole, 8)}

    def values_of(c, x, dy, at):
        if dy == -1:
            return [field[c, x, 0:8, at]]
        tail = field[c, x, whole:size_y, at]
        tail = jnp.concatenate([tail, jnp.zeros((whole + 8 - size_y, 128), F32)], axis=0)
        return [tail] if dy == 1 else [field[c, x, 0:whole, at], tail]

    def one(dy, dx, ref, step, visit):
            window = jnp.bitwise_and(visit, windows - 1)
            at = pl.ds(pl.multiple_of(window * 128, 128), 128)
            index = (dy + 1) * 3 + dx + 1
            x0, rows = rows_of[dx]
            s0, cols = cols_of[dy]
            part, lanes, ahead, live = markers_of(meta, index, visit, step, ref, dx + 1)
            both = jnp.concatenate(split2(window_of(part, live, window, depth)), axis=1)
            right = jnp.concatenate([both, both], axis=0)
            table_x, table_y = plane_of(
                part, size_x * dx - 1 - x0, rows, size_y * dy - 1 - s0, cols
            )
            found = []
            for c in range(3):
                values = jnp.concatenate(
                    [v for r in range(rows) for v in values_of(c, x0 + r, dy, at)], axis=0
                )
                sums = nn(jnp.concatenate(split2(values), axis=1), right)
                sums = sums[:, 0:STEP] + sums[:, STEP : 2 * STEP]
                mixed = jnp.zeros((cols, STEP), F32)
                for r in range(rows):
                    mixed = mixed + table_x[r : r + 1] * sums[r * cols : (r + 1) * cols]
                total = jnp.sum(mixed * table_y, axis=0, keepdims=True)
                found.append(jnp.where(live, total, 0.0))
            found = jnp.concatenate([*found, jnp.zeros((5, STEP), F32)], axis=0)
            found = jnp.concatenate([found, jnp.zeros((8, 128), F32)], axis=1)
            out_ref[outs[dy, dx], :, lanes] += pltpu.roll(found, ahead, 1)

    run_visits(one, lists, meta, windows, group)


def sample_kernel(places, meta, mid_ref, field, out_ref):
    out_ref[...] = jnp.zeros(out_ref.shape, F32)
    lists = [(0, dx, mid_ref) for dx in places]
    sample_lists(meta, lists, field, out_ref, {(0, dx): i for i, dx in enumerate(places)}, 3)


def sample(meta, mid, field, places):
    return pl.pallas_call(
        functools.partial(sample_kernel, places),
        out_shape=jax.ShapeDtypeStruct((len(places), 8, mid.shape[2]), F32),
        in_specs=[smem(), vmem(), vmem()],
        out_specs=vmem(),
        compiler_params=params(),
        cost_estimate=cost(5 * 10**9, 5 * 10**6),
        name="sample",
    )(meta, mid, field)


def solve(sweeps, meta, spreads, velocity, viscosity, halos, lists):
    size_x, size_y, depth = viscosity.shape
    ext = size_x + 2 * HALO
    slots = lists[0].shape[2]
    partial = jax.ShapeDtypeStruct((9, slots), F32)
    return pl.pallas_call(
        functools.partial(solve_kernel, sweeps),
        out_shape=(jax.ShapeDtypeStruct(velocity.shape, F32), partial, partial),
        in_specs=[smem()] + [vmem()] * 15,
        out_specs=(vmem(),) * 3,
        scratch_shapes=[
            pltpu.VMEM((3, ext, YE, depth), F32),
            pltpu.VMEM((3, ext - 2, YE, depth), F32),
            pltpu.VMEM((3, ext - 2, YE, depth), F32),
            pltpu.VMEM((ext - 2, YE, depth), F32),
            pltpu.VMEM((6, 8, slots), F32),
        ],
        compiler_params=params(),
        cost_estimate=cost(10**10, 2 * 10**7),
        name="solve",
    )(meta, *spreads, velocity, viscosity, *halos, *lists)


def unsort_kernel(own_ref, sides_ref, low_ref, high_ref, rank_ref, out_ref):
    devices = out_ref.shape[0]
    slots = sides_ref.shape[1]
    total = own_ref[0, 0:3, :] + sides_ref[3:6, :] + low_ref[...] + high_ref[...]
    total = jnp.concatenate([total, jnp.zeros((5, slots), F32)], axis=0)
    flat = jnp.concatenate([rank_ref[k : k + 1, :] for k in range(CAP)], axis=1)
    block = 256
    sums = jnp.zeros((32, slots), F32)
    for b in range(slots // block):
        values = total[:, b * block : (b + 1) * block]
        parts = jnp.concatenate([*split3(values), jnp.zeros_like(values)], axis=0)
        sums = sums + nn(parts.astype(BF16), place_block(flat, b * block, block))
    rows = sums[0:8] + sums[8:16] + sums[16:24]
    turned = jnp.concatenate(
        [rows[:, k * devices : (k + 1) * devices] for k in range(CAP)], axis=0
    )
    out_ref[...] = turned.T


def unsort(own, sides, low, high, rank):
    devices = rank.shape[1]
    return pl.pallas_call(
        unsort_kernel,
        out_shape=jax.ShapeDtypeStruct((devices, CAP * 8), F32),
        in_specs=[vmem()] * 5,
        out_specs=vmem(),
        compiler_params=params(),
        cost_estimate=cost(10**9, 300_000),
        name="unsort",
    )(own, sides, low, high, rank)


def unpack_kernel(owner_ref, rank_ref, back_ref, out_ref):
    markers = owner_ref.shape[1]
    devices = back_ref.shape[0]
    onehot = (iota((devices, markers), 0) == owner_ref[...]).astype(F32).astype(BF16)
    rank = rank_ref[...]
    turned = back_ref[...].T
    picked = None
    for part in split3(turned):
        term = nn(part.astype(BF16), onehot)
        picked = term if picked is None else picked + term
    total = jnp.zeros((8, markers), F32)
    for k in range(CAP):
        total = total + jnp.where(rank == k, picked[k * 8 : (k + 1) * 8], 0.0)
    out_ref[...] = total[0:3]


def unpack(owner_row, rank, back):
    markers = owner_row.shape[1]
    return pl.pallas_call(
        unpack_kernel,
        out_shape=jax.ShapeDtypeStruct((3, markers), F32),
        in_specs=[vmem()] * 3,
        out_specs=vmem(),
        compiler_params=params(),
        cost_estimate=cost(10**8, 100_000),
        name="unpack",
    )(owner_row, rank, back)


def shift_up(x, axis):
    count = lax.axis_size(axis)
    return lax.ppermute(x, axis, [(i, (i + 1) % count) for i in range(count)])


def shift_down(x, axis):
    count = lax.axis_size(axis)
    return lax.ppermute(x, axis, [((i + 1) % count, i) for i in range(count)])


def shards(velocity, viscosity, cells, offsets, forces, owners):
    devices = lax.axis_size("gx") * lax.axis_size("gy")
    size_x, size_y, depth = viscosity.shape
    markers = owners.shape[0]
    owner_row = owners.reshape(1, markers)
    both = ("gx", "gy")

    x_low_first = shift_up(velocity[0, size_x - HALO : size_x - HALO + X_FIRST], "gx")
    x_high_first = shift_down(velocity[0, 0:X_FIRST], "gx")
    outgoing, rank = pack(owner_row, cells, offsets, forces, devices)
    outgoing, face_source = lax.optimization_barrier((outgoing, viscosity))
    received = lax.all_to_all(outgoing, both, split_axis=0, concat_axis=0, tiled=True)
    x_up, x_down, y_up, y_down, x_up_late, x_down_late = faces(velocity, face_source)
    received, x_low_first, x_high_first, x_up, x_down, y_up, y_down = lax.optimization_barrier(
        (received, x_low_first, x_high_first, x_up, x_down, y_up, y_down)
    )
    x_low = shift_up(x_up, "gx")
    x_high = shift_down(x_down, "gx")
    y_low = shift_up(y_up, "gy")
    y_high = shift_down(y_down, "gy")
    markers_list, order = sort(received, depth)
    markers_list, x_low, x_high, y_low, y_high = lax.optimization_barrier(
        (markers_list, x_low, x_high, y_low, y_high)
    )
    list_low = shift_up(markers_list, "gx")
    list_high = shift_down(markers_list, "gx")
    x_up_late, x_down_late = late_faces(x_up_late, x_down_late, y_low, y_high, size_x)
    mid = jnp.stack([list_low, markers_list, list_high])
    x_low_late = shift_up(x_up_late, "gx")
    x_high_late = shift_down(x_down_late, "gx")
    low = shift_up(mid, "gy")
    high = shift_down(mid, "gy")
    halos = (x_low_first, x_high_first, x_low, x_high, x_low_late, x_high_late, y_low, y_high)
    meta_mid = mid[:, 10, 0:64].astype(I32)
    meta_mid = jnp.pad(meta_mid, ((3, 3), (0, 0)))
    spread_own = spread_mid(meta_mid, mid, size_x, size_y, depth)
    low, high, spread_own = lax.optimization_barrier((low, high, spread_own))
    meta = jnp.concatenate([part[:, 10, 0:64] for part in (low, mid, high)], axis=0).astype(I32)
    spreads = (spread_own, *spread_side(meta, low, high, size_x, size_y, depth))
    halos, spreads = lax.optimization_barrier((halos, spreads))
    field, part_low, part_high = solve(
        3, meta, spreads, velocity, viscosity, halos, (low, high)
    )
    beside = sample(meta, mid, field, (-1, 1))
    sides = shift_down(part_low, "gy") + shift_up(part_high, "gy")
    to_low = sides[0:3] + beside[0, 0:3]
    to_high = sides[6:9] + beside[1, 0:3]
    to_low, to_high, field_own = lax.optimization_barrier((to_low, to_high, field))
    own = sample(meta, mid, field_own, (0,))
    back = unsort(own, sides, shift_down(to_low, "gx"), shift_up(to_high, "gx"), order)
    back = lax.all_to_all(back, both, split_axis=0, concat_axis=0, tiled=True)
    return (field, unpack(owner_row, rank, back))


def solution(mesh):
    in_specs = (
        P(None, "gx", "gy", None),
        P("gx", "gy", None),
        P(None, ("gx", "gy")),
        P(None, ("gx", "gy")),
        P(None, ("gx", "gy")),
        P(("gx", "gy"), None),
    )
    out_specs = (P(None, "gx", "gy", None), P(None, ("gx", "gy")))
    return jax.shard_map(shards, mesh=mesh, in_specs=in_specs, out_specs=out_specs, check_vma=False)
```

```python
import functools

import jax
import jax.numpy as jnp
from jax import lax
from jax.experimental import pallas as pl
from jax.experimental.pallas import tpu as pltpu
from jax.sharding import PartitionSpec as P

F32 = jnp.float32
BF16 = jnp.bfloat16
I32 = jnp.int32
LIMIT = 60 * 1024 * 1024
CAP = 16
HALO = 3
PAD = 8
YE = 40
VISITS = 16
STEP = 256
GROUP_MID = 3
GROUP_SIDE = 3


def split3(x):
    hi = x.astype(BF16).astype(F32)
    rest = x - hi
    mid = rest.astype(BF16).astype(F32)
    return hi, mid, rest - mid


def split2(x):
    hi = x.astype(BF16)
    return hi, (x - hi.astype(F32)).astype(BF16)


def nn(a, b):
    return lax.dot_general(a, b, (((1,), (0,)), ((), ())), preferred_element_type=F32)


def nt(a, b):
    return lax.dot_general(a, b, (((1,), (1,)), ((), ())), preferred_element_type=F32)


def tn(a, b):
    return lax.dot_general(a, b, (((0,), (0,)), ((), ())), preferred_element_type=F32)


def iota(shape, dim):
    return lax.broadcasted_iota(I32, shape, dim)


def vmem():
    return pl.BlockSpec(memory_space=pltpu.VMEM)


def smem():
    return pl.BlockSpec(memory_space=pltpu.SMEM)


def params():
    return pltpu.CompilerParams(vmem_limit_bytes=LIMIT)


def cost(flops, size):
    return pl.CostEstimate(flops=flops, bytes_accessed=size, transcendentals=0)


def pack_kernel(owner_ref, cells_ref, offsets_ref, forces_ref, out_ref, rank_ref):
    markers = owner_ref.shape[1]
    devices = out_ref.shape[0]
    owner = owner_ref[...]
    before = (iota((128, 128), 0) < iota((128, 128), 1)).astype(BF16)
    running = jnp.zeros((devices, 1), F32)
    ranks = []
    hots = []
    for g in range(markers // 128):
        hot = (iota((devices, 128), 0) == owner[:, g * 128 : (g + 1) * 128]).astype(F32)
        within = nn(hot.astype(BF16), before)
        ranks.append(jnp.sum(hot * (within + running), axis=0, keepdims=True))
        running = running + jnp.sum(hot, axis=1, keepdims=True)
        hots.append(hot.astype(BF16))
    rank = jnp.concatenate(ranks, axis=1).astype(I32)
    rank_ref[...] = rank
    onehot = jnp.concatenate(hots, axis=1)
    payload = jnp.concatenate(
        [
            cells_ref[...].astype(F32),
            offsets_ref[...],
            forces_ref[...],
            jnp.ones((1, markers), F32),
            jnp.zeros((6, markers), F32),
        ],
        axis=0,
    )
    parts = split3(payload)
    total = None
    for part in parts:
        rows = jnp.concatenate([jnp.where(rank == k, part, 0.0) for k in range(CAP)], axis=0)
        term = nt(onehot, rows.astype(BF16))
        total = term if total is None else total + term
    out_ref[...] = total


def pack(owner_row, cells, offsets, forces, devices):
    markers = owner_row.shape[1]
    return pl.pallas_call(
        pack_kernel,
        out_shape=(
            jax.ShapeDtypeStruct((devices, CAP * 16), F32),
            jax.ShapeDtypeStruct((1, markers), I32),
        ),
        in_specs=[vmem()] * 4,
        out_specs=(vmem(), vmem()),
        compiler_params=params(),
        cost_estimate=cost(4 * 10**8, 300_000),
        name="pack",
    )(owner_row, cells, offsets, forces)


def place_block(flat, start, count):
    return (flat == start + iota((count, flat.shape[1]), 0)).astype(F32).astype(BF16)


def sort_kernel(depth, rec_ref, list_ref, rank_ref, keys, pieces):
    devices = rec_ref.shape[0]
    slots = devices * CAP
    rec = rec_ref[...]
    flipped = rec.T
    empty = float(depth * 4096)

    def key_of(z, valid, index):
        low = jnp.where(z < 0.5, float(depth - 1), z - 1.0)
        return jnp.where(valid > 0.5, low * float(slots), empty) + index

    rows = []
    lane = iota((devices, 128), 1)
    for k in range(CAP):
        at = k * 16
        column = key_of(
            rec[:, at + 2 : at + 3],
            rec[:, at + 9 : at + 10],
            (iota((devices, 1), 0) + k * devices).astype(F32),
        )
        keys[k] = jnp.broadcast_to(column, (devices, devices))
        rows.append(
            key_of(
                flipped[at + 2 : at + 3, :],
                flipped[at + 9 : at + 10, :],
                (iota((1, devices), 1) + k * devices).astype(F32),
            )
        )
        half = rec[:, (k // 8) * 128 : (k // 8 + 1) * 128]
        turned = half if k % 8 == 0 else pltpu.roll(half, 128 - (k % 8) * 16, 1)
        hi, mid, lo = split3(turned)
        joined = jnp.where(
            lane < 16,
            hi,
            jnp.where(
                lane < 32, pltpu.roll(mid, 16, 1), jnp.where(lane < 48, pltpu.roll(lo, 32, 1), 0.0)
            ),
        )
        pieces[k * devices : (k + 1) * devices, :] = joined.astype(BF16)
    ranks = []
    for k in range(CAP):
        row = rows[k]

        def count(other, acc):
            return acc + jnp.where(keys[other] < row, 1.0, 0.0)

        acc = lax.fori_loop(0, CAP, count, jnp.zeros((devices, devices), F32))
        ranks.append(jnp.sum(acc, axis=0, keepdims=True).astype(I32))
    rank_ref[...] = jnp.concatenate(ranks, axis=0)
    flat = jnp.concatenate(ranks, axis=1)
    block = 256
    for b in range(slots // block):
        moved = nn(place_block(flat, b * block, block), pieces[...]).T
        rows = moved[0:16] + moved[16:32] + moved[32:48]
        z = rows[2:3]
        low = jnp.where(z < 0.5, float(depth - 1), z - 1.0)
        list_ref[:, b * block : (b + 1) * block] = jnp.where(
            iota((16, block), 0) == 2, low, rows
        )
    low = jnp.where(list_ref[9:10, :] > 0.5, list_ref[2:3, :], float(4 * depth))
    visit = (iota((VISITS, slots), 0) * 128).astype(F32)
    diagonal = iota((VISITS, 128), 0) == iota((VISITS, 128), 1)

    def count_below(bound):
        column = jnp.sum(jnp.where(low < bound, 1.0, 0.0), axis=1, keepdims=True)
        return jnp.sum(jnp.where(diagonal, column, 0.0), axis=0, keepdims=True)

    first = count_below(visit - 3.0)
    last = count_below(visit + 128.0)
    meta = jnp.where(iota((1, 128), 1) < VISITS, first, pltpu.roll(last, VISITS, 1))
    list_ref[10:11, 0:128] = meta


def sort(received, depth):
    devices = received.shape[0]
    slots = devices * CAP
    return pl.pallas_call(
        functools.partial(sort_kernel, depth),
        out_shape=(
            jax.ShapeDtypeStruct((16, slots), F32),
            jax.ShapeDtypeStruct((CAP, devices), I32),
        ),
        in_specs=[vmem()],
        out_specs=(vmem(), vmem()),
        scratch_shapes=[
            pltpu.VMEM((CAP, devices, devices), F32),
            pltpu.VMEM((slots, 128), BF16),
        ],
        compiler_params=params(),
        cost_estimate=cost(2 * 10**9, 300_000),
        name="sort",
    )(received)


def bump(frac):
    root = jnp.sqrt(1.0 + 4.0 * frac - 4.0 * frac * frac)
    return (
        (3.0 - 2.0 * frac - root) / 8.0,
        (3.0 - 2.0 * frac + root) / 8.0,
        (1.0 + 2.0 * frac + root) / 8.0,
        (1.0 + 2.0 * frac - root) / 8.0,
    )


def tent(first, weights, count, modulus=None):
    rows = iota((count, first.shape[1]), 0)
    table = 0.0
    for i in range(4):
        target = first + i
        if modulus is not None:
            target = jnp.bitwise_and(target, modulus - 1)
        table = jnp.where(rows == target, weights[i], table)
    return table


def markers_of(meta, index, visit, step, ref, at):
    slots = ref.shape[2]
    width = STEP + 128
    start = meta[index, visit] + STEP * step
    chunk = jnp.minimum(lax.shift_right_logical(start, 7), slots // 128 - width // 128)
    ahead = start - chunk * 128
    lanes = pl.ds(pl.multiple_of(chunk * 128, 128), width)
    part = pltpu.roll(ref[at, :, lanes], jnp.where(ahead == 0, 0, width - ahead), 1)[:, 0:STEP]
    live = iota((1, STEP), 1) < meta[index, VISITS + visit] - start
    return part, lanes, ahead, live


def window_of(part, live, window, depth):
    weights = [jnp.where(live, w, 0.0) for w in bump(part[5:6])]
    return tent(part[2:3].astype(I32) - window * 128, weights, 128, depth)


def plane_of(part, shift_x, rows_x, shift_y, rows_y):
    table_x = tent(part[0:1].astype(I32) + shift_x, bump(part[3:4]), -(-rows_x // 8) * 8)
    table_y = tent(part[1:2].astype(I32) + shift_y, bump(part[4:5]), rows_y)
    return table_x, table_y


def run_visits(one, lists, meta, windows, group):
    def length(dy, dx, visit):
        index = (dy + 1) * 3 + dx + 1
        return meta[index, VISITS + visit] - meta[index, visit]

    def turn(number, carry):
        most = 0
        for g in range(group):
            visit = number * group + g
            for dy, dx, ref in lists:
                one(dy, dx, ref, 0, visit)
                most = jnp.maximum(most, length(dy, dx, visit))

        @pl.when(most > STEP)
        def _():
            def again(visit, inner):
                for dy, dx, ref in lists:

                    def later(step, kept, dy=dy, dx=dx, ref=ref):
                        one(dy, dx, ref, step, visit)
                        return kept

                    steps = lax.shift_right_logical(length(dy, dx, visit) + STEP - 1, 8)
                    lax.fori_loop(1, steps, later, 0)
                return inner

            lax.fori_loop(number * group, (number + 1) * group, again, 0)

        return carry

    lax.fori_loop(0, (windows + 1) // group, turn, 0)


def spread_lists(size_x, size_y, meta, lists, outs, first_row, group):
    depth = next(iter(outs.values())).shape[3]
    windows = depth // 128
    rows_of = {-1: (0, 5), 0: (2, size_x + 3), 1: (size_x + 2, 4)}

    def clear(e, carry):
        for out_ref in outs.values():
            for c in range(3):
                out_ref[c, e] = jnp.zeros(out_ref.shape[2:], F32)
        return carry

    lax.fori_loop(0, size_x + 2 * HALO, clear, 0)

    def one(dy, dx, ref, step, visit):
            window = jnp.bitwise_and(visit, windows - 1)
            at = pl.ds(pl.multiple_of(window * 128, 128), 128)
            out_ref = outs[dy]
            index = (dy + 1) * 3 + dx + 1
            e0, rows = rows_of[dx]
            s0, cols, base = first_row[dy]
            part, _, _, live = markers_of(meta, index, visit, step, ref, dx + 1)
            both = jnp.concatenate(split2(window_of(part, live, window, depth).T), axis=1)
            right = jnp.concatenate([both, both], axis=0)
            table_x, table_y = plane_of(
                part, HALO - 1 + size_x * dx - e0, rows, PAD - 1 + size_y * dy - s0, cols
            )
            for c in range(3):
                pushed = table_y * part[6 + c : 7 + c]
                planar = jnp.concatenate(
                    [table_x[r : r + 1] * pushed for r in range(rows)], axis=0
                )
                sums = nn(jnp.concatenate(split2(planar), axis=1), right)
                sums = sums[:, 0:128] + sums[:, 128:256]
                for r in range(rows):
                    out_ref[c, e0 + r, base : base + cols, at] += sums[r * cols : (r + 1) * cols]

    run_visits(one, lists, meta, windows, group)


ROWS_MID = {0: (PAD - 1, 32, PAD - 1)}
ROWS_SIDE = {-1: (PAD - 3, 8, 0), 1: (32, 8, 0)}


def spread_mid_kernel(size_x, size_y, meta, mid_ref, out_ref):
    lists = [(0, dx, mid_ref) for dx in (0, -1, 1)]
    spread_lists(size_x, size_y, meta, lists, {0: out_ref}, ROWS_MID, GROUP_MID)


def spread_side_kernel(size_x, size_y, meta, low_ref, high_ref, out_low, out_high):
    lists = [(dy, dx, ref) for dy, ref in ((-1, low_ref), (1, high_ref)) for dx in (0, -1, 1)]
    outs = {-1: out_low, 1: out_high}
    spread_lists(size_x, size_y, meta, lists, outs, ROWS_SIDE, GROUP_SIDE)


def spread_mid(meta, mid, size_x, size_y, depth):
    return pl.pallas_call(
        functools.partial(spread_mid_kernel, size_x, size_y),
        out_shape=jax.ShapeDtypeStruct((3, size_x + 2 * HALO, YE, depth), F32),
        in_specs=[smem(), vmem()],
        out_specs=vmem(),
        compiler_params=params(),
        cost_estimate=cost(10**10, 10**7),
        name="spread_mid",
    )(meta, mid)


def spread_side(meta, low, high, size_x, size_y, depth):
    shape = jax.ShapeDtypeStruct((3, size_x + 2 * HALO, 8, depth), F32)
    return pl.pallas_call(
        functools.partial(spread_side_kernel, size_x, size_y),
        out_shape=(shape, shape),
        in_specs=[smem(), vmem(), vmem()],
        out_specs=(vmem(), vmem()),
        compiler_params=params(),
        cost_estimate=cost(10**10, 10**7),
        name="spread_side",
    )(meta, low, high)


def faces_kernel(vel_ref, visc_ref, x_up, x_down, y_up, y_down, x_up_late, x_down_late):
    size_x, size_y = visc_ref.shape[0], visc_ref.shape[1]
    for r in range(X_FIRST, X_LAYERS):
        up, down = (x_up, x_down) if r < X_EARLY else (x_up_late, x_down_late)
        at = r - X_FIRST if r < X_EARLY else r - X_EARLY
        rows = slice(at * size_y, (at + 1) * size_y)
        c, l = r // HALO, r % HALO
        if c < 3:
            up[rows, :] = vel_ref[c, size_x - HALO + l]
            down[rows, :] = vel_ref[c, l]
        else:
            up[rows, :] = visc_ref[size_x - HALO + 1 + l]
            down[rows, :] = visc_ref[l]
    for x in range(size_x):
        for c in range(3):
            r = (c * size_x + x) * HALO
            y_up[r : r + HALO, :] = vel_ref[c, x, size_y - HALO : size_y, :]
            y_down[r : r + HALO, :] = vel_ref[c, x, 0:HALO, :]
        r = 3 * size_x * HALO + x * (HALO - 1)
        y_up[r : r + HALO - 1, :] = visc_ref[x, size_y - HALO + 1 : size_y, :]
        y_down[r : r + HALO - 1, :] = visc_ref[x, 0 : HALO - 1, :]


def layer_of(first, early, late, r, size_y):
    if r < X_FIRST:
        return first[r]
    ref, at = (early, r - X_FIRST) if r < X_EARLY else (late, r - X_EARLY)
    return ref[at * size_y : (at + 1) * size_y, :]


X_LAYERS = 4 * HALO - 1
X_FIRST = 3
X_EARLY = 5


def face_rows(size_x, size_y):
    rows_y = 3 * size_x * HALO + size_x * (HALO - 1)
    rows = ((X_EARLY - X_FIRST) * size_y, rows_y, (X_LAYERS - X_EARLY) * size_y)
    return tuple(-(-number // 8) * 8 for number in rows)


def faces(velocity, viscosity):
    size_x, size_y, depth = viscosity.shape
    shapes = [jax.ShapeDtypeStruct((rows, depth), F32) for rows in face_rows(size_x, size_y)]
    return pl.pallas_call(
        faces_kernel,
        out_shape=[shape for shape in shapes for _ in range(2)],
        in_specs=[vmem(), vmem()],
        out_specs=[vmem()] * 6,
        compiler_params=params(),
        cost_estimate=cost(10**6, 10**7),
        name="faces",
    )(velocity, viscosity)


def corner_plan(up):
    plan, at = [], 0
    for r in range(X_LAYERS):
        c, l = r // HALO, r % HALO
        reach = HALO if c < 3 else HALO - 1
        away = reach - l if up else l + 1
        if reach > away:
            plan.append((r, reach - away, at))
            at += 2 * (reach - away)
    return plan, at


def late_kernel(size_x, up_ref, down_ref, y_low, y_high, up, down):
    thick = up_ref.shape[0]
    up[0:thick, :] = up_ref[...]
    down[0:thick, :] = down_ref[...]
    base = 3 * size_x * HALO
    thin = HALO - 1
    for out, is_up in ((up, True), (down, False)):
        for r, count, first in corner_plan(is_up)[0]:
            c, l = r // HALO, r % HALO
            x = l if not is_up else size_x - HALO + l + (1 if c == 3 else 0)
            deep, row = (HALO, (c * size_x + x) * HALO) if c < 3 else (thin, base + x * thin)
            at = thick + first
            out[at : at + count, :] = y_low[row + deep - count : row + deep, :]
            at = at + count
            out[at : at + count, :] = y_high[row : row + count, :]


def late_faces(up, down, y_low, y_high, size_x):
    thick = up.shape[0]
    rows = thick + -(-corner_plan(True)[1] // 8) * 8
    shape = jax.ShapeDtypeStruct((rows, up.shape[1]), F32)
    return pl.pallas_call(
        functools.partial(late_kernel, size_x),
        out_shape=(shape, shape),
        in_specs=[vmem()] * 4,
        out_specs=(vmem(), vmem()),
        compiler_params=params(),
        cost_estimate=cost(10**6, 4 * 10**6),
        name="late_faces",
    )(up, down, y_low, y_high)


def solve_kernel(
    sweeps,
    meta,
    spread_ref,
    side_low,
    side_high,
    vel_ref,
    visc_ref,
    x_low_first,
    x_high_first,
    x_low,
    x_high,
    x_low_late,
    x_high_late,
    y_low,
    y_high,
    low_ref,
    high_ref,
    new_ref,
    part_low,
    part_high,
    rhs,
    scaled,
    field,
    ratio,
    gathered,
):
    size_x, size_y, depth = visc_ref.shape
    ext = size_x + 2 * HALO
    own = slice(PAD, PAD + size_y)
    below = slice(PAD - HALO, PAD)
    above = slice(PAD + size_y, PAD + size_y + HALO)
    tiles = [slice(s, s + 8) for s in range(0, YE, 8)]
    thick = -(-(X_LAYERS - X_EARLY) * size_y // 8) * 8

    def clear(e, carry):
        for c in range(3):
            rhs[c, e, tiles[0]] = jnp.zeros((8, depth), F32)
            rhs[c, e, tiles[4]] = jnp.zeros((8, depth), F32)
        return carry

    lax.fori_loop(0, ext, clear, 0)

    def clear_ratio(e, carry):
        ratio[e, tiles[0]] = jnp.zeros((8, depth), F32)
        ratio[e, tiles[4]] = jnp.zeros((8, depth), F32)
        return carry

    lax.fori_loop(0, ext - 2, clear_ratio, 0)

    base = 3 * size_x * HALO
    thin = HALO - 1
    for x in range(size_x):
        e = x + HALO - 1
        ratio[e, own, :] = visc_ref[x]
        ratio[e, PAD - thin : PAD, :] = y_low[base + x * thin : base + (x + 1) * thin, :]
        ratio[e, PAD + size_y : PAD + size_y + thin, :] = y_high[
            base + x * thin : base + (x + 1) * thin, :
        ]
        for c in range(3):
            r = (c * size_x + x) * HALO
            rhs[c, x + HALO, own, :] = vel_ref[c, x]
            rhs[c, x + HALO, below, :] = y_low[r : r + HALO, :]
            rhs[c, x + HALO, above, :] = y_high[r : r + HALO, :]
    for side, start, early, late in (
        (0, x_low_first, x_low, x_low_late),
        (1, x_high_first, x_high, x_high_late),
    ):
        for r in range(X_LAYERS):
            c, l = r // HALO, r % HALO
            if c < 3:
                target = rhs.at[c, l if side == 0 else size_x + HALO + l]
            else:
                target = ratio.at[l if side == 0 else size_x + HALO - 1 + l]
            target[own, :] = layer_of(start, early, late, r, size_y)
        for r, count, first in corner_plan(side == 0)[0]:
            c, l = r // HALO, r % HALO
            if c < 3:
                target = rhs.at[c, l if side == 0 else size_x + HALO + l]
            else:
                target = ratio.at[l if side == 0 else size_x + HALO - 1 + l]
            at = thick + first
            target[PAD - count : PAD, :] = late[at : at + count, :]
            at = at + count
            target[PAD + size_y : PAD + size_y + count, :] = late[at : at + count, :]

    rows8 = iota((8, depth), 0)

    def total(c, e, s):
        value = rhs[c, e, tiles[s], :] + spread_ref[c, e, tiles[s], :]
        if s < 2:
            turned = pltpu.roll(side_low[c, e], PAD - 3, 0)
            keep = rows8 >= PAD - 3 if s == 0 else rows8 < PAD - 3
            value = value + jnp.where(keep, turned, 0.0)
        if s == 4:
            value = value + side_high[c, e]
        return value

    for e in (0, ext - 1):
        for c in range(3):
            for s in range(5):
                rhs[c, e, tiles[s], :] = total(c, e, s)

    def scale(e, carry):
        for s in range(5):
            nu = ratio[e - 1, tiles[s], :]
            inverse = 1.0 / (1.0 + 6.0 * nu)
            ratio[e - 1, tiles[s], :] = nu * inverse
            for c in range(3):
                value = total(c, e, s)
                rhs[c, e, tiles[s], :] = value
                scaled[c, e - 1, tiles[s], :] = value * inverse
        return carry

    lax.fori_loop(1, ext - 1, scale, 0)

    def sweep(source, offset, target, target_offset, first, last, write):
        def row(e, carry):
            for s in range(1 if write else 0, 5):
                factor = ratio[e - 1, tiles[s], :]
                for c in range(3):
                    here = source[c, e - offset, tiles[s], :]
                    beside = source[c, e + 1 - offset, tiles[s], :]
                    beside = beside + source[c, e - 1 - offset, tiles[s], :]
                    if s < 4:
                        beside = beside + source[c, e - offset, s * 8 + 1 : s * 8 + 9, :]
                    else:
                        beside = beside + pltpu.roll(here, 7, 0)
                    if s > 0:
                        beside = beside + source[c, e - offset, s * 8 - 1 : s * 8 + 7, :]
                    else:
                        beside = beside + pltpu.roll(here, 1, 0)
                    beside = beside + pltpu.roll(here, depth - 1, 1) + pltpu.roll(here, 1, 1)
                    value = scaled[c, e - 1, tiles[s], :] + factor * beside
                    if not write:
                        target[c, e - target_offset, tiles[s], :] = value
                    elif s == 4:
                        target[c, e - target_offset, 24:size_y, :] = value[0 : size_y - 24]
                    else:
                        target[c, e - target_offset, (s - 1) * 8 : s * 8, :] = value
            return carry

        lax.fori_loop(first, last, row, 0)

    sweep(rhs, 0, field, 1, 1, ext - 1, False)
    sweep(field, 1, rhs, 0, 2, ext - 2, False)
    sweep(rhs, 0, new_ref, HALO, 3, ext - 3, True)

    gathered[...] = jnp.zeros(gathered.shape, F32)
    lists = [(dy, dx, ref) for dy, ref in ((-1, low_ref), (1, high_ref)) for dx in (0, -1, 1)]
    outs = {(dy, dx): (dy + 1) // 2 * 3 + dx + 1 for dy, dx, _ in lists}
    sample_lists(meta, lists, new_ref, gathered, outs, GROUP_SIDE)
    for dx in range(3):
        part_low[dx * 3 : dx * 3 + 3, :] = gathered[dx, 0:3, :]
        part_high[dx * 3 : dx * 3 + 3, :] = gathered[3 + dx, 0:3, :]


def sample_lists(meta, lists, field, out_ref, outs, group):
    _, size_x, size_y, depth = field.shape
    windows = depth // 128
    whole = size_y // 8 * 8
    rows_of = {-1: (0, 2), 0: (0, size_x), 1: (size_x - 1, 1)}
    cols_of = {-1: (0, 8), 0: (0, whole + 8), 1: (whole, 8)}

    def values_of(c, x, dy, at):
        if dy == -1:
            return [field[c, x, 0:8, at]]
        tail = field[c, x, whole:size_y, at]
        tail = jnp.concatenate([tail, jnp.zeros((whole + 8 - size_y, 128), F32)], axis=0)
        return [tail] if dy == 1 else [field[c, x, 0:whole, at], tail]

    def one(dy, dx, ref, step, visit):
            window = jnp.bitwise_and(visit, windows - 1)
            at = pl.ds(pl.multiple_of(window * 128, 128), 128)
            index = (dy + 1) * 3 + dx + 1
            x0, rows = rows_of[dx]
            s0, cols = cols_of[dy]
            part, lanes, ahead, live = markers_of(meta, index, visit, step, ref, dx + 1)
            both = jnp.concatenate(split2(window_of(part, live, window, depth)), axis=1)
            right = jnp.concatenate([both, both], axis=0)
            table_x, table_y = plane_of(
                part, size_x * dx - 1 - x0, rows, size_y * dy - 1 - s0, cols
            )
            found = []
            for c in range(3):
                values = jnp.concatenate(
                    [v for r in range(rows) for v in values_of(c, x0 + r, dy, at)], axis=0
                )
                sums = nn(jnp.concatenate(split2(values), axis=1), right)
                sums = sums[:, 0:STEP] + sums[:, STEP : 2 * STEP]
                mixed = jnp.zeros((cols, STEP), F32)
                for r in range(rows):
                    mixed = mixed + table_x[r : r + 1] * sums[r * cols : (r + 1) * cols]
                total = jnp.sum(mixed * table_y, axis=0, keepdims=True)
                found.append(jnp.where(live, total, 0.0))
            found = jnp.concatenate([*found, jnp.zeros((5, STEP), F32)], axis=0)
            found = jnp.concatenate([found, jnp.zeros((8, 128), F32)], axis=1)
            out_ref[outs[dy, dx], :, lanes] += pltpu.roll(found, ahead, 1)

    run_visits(one, lists, meta, windows, group)


def sample_kernel(places, meta, mid_ref, field, out_ref):
    out_ref[...] = jnp.zeros(out_ref.shape, F32)
    lists = [(0, dx, mid_ref) for dx in places]
    sample_lists(meta, lists, field, out_ref, {(0, dx): i for i, dx in enumerate(places)}, 3)


def sample(meta, mid, field, places):
    return pl.pallas_call(
        functools.partial(sample_kernel, places),
        out_shape=jax.ShapeDtypeStruct((len(places), 8, mid.shape[2]), F32),
        in_specs=[smem(), vmem(), vmem()],
        out_specs=vmem(),
        compiler_params=params(),
        cost_estimate=cost(5 * 10**9, 5 * 10**6),
        name="sample",
    )(meta, mid, field)


def solve(sweeps, meta, spreads, velocity, viscosity, halos, lists):
    size_x, size_y, depth = viscosity.shape
    ext = size_x + 2 * HALO
    slots = lists[0].shape[2]
    partial = jax.ShapeDtypeStruct((9, slots), F32)
    return pl.pallas_call(
        functools.partial(solve_kernel, sweeps),
        out_shape=(jax.ShapeDtypeStruct(velocity.shape, F32), partial, partial),
        in_specs=[smem()] + [vmem()] * 15,
        out_specs=(vmem(),) * 3,
        scratch_shapes=[
            pltpu.VMEM((3, ext, YE, depth), F32),
            pltpu.VMEM((3, ext - 2, YE, depth), F32),
            pltpu.VMEM((3, ext - 2, YE, depth), F32),
            pltpu.VMEM((ext - 2, YE, depth), F32),
            pltpu.VMEM((6, 8, slots), F32),
        ],
        compiler_params=params(),
        cost_estimate=cost(10**10, 2 * 10**7),
        name="solve",
    )(meta, *spreads, velocity, viscosity, *halos, *lists)


def unsort_kernel(own_ref, sides_ref, low_ref, high_ref, rank_ref, out_ref):
    devices = out_ref.shape[0]
    slots = sides_ref.shape[1]
    total = own_ref[0, 0:3, :] + sides_ref[3:6, :] + low_ref[...] + high_ref[...]
    total = jnp.concatenate([total, jnp.zeros((5, slots), F32)], axis=0)
    flat = jnp.concatenate([rank_ref[k : k + 1, :] for k in range(CAP)], axis=1)
    block = 256
    sums = jnp.zeros((32, slots), F32)
    for b in range(slots // block):
        values = total[:, b * block : (b + 1) * block]
        parts = jnp.concatenate([*split3(values), jnp.zeros_like(values)], axis=0)
        sums = sums + nn(parts.astype(BF16), place_block(flat, b * block, block))
    rows = sums[0:8] + sums[8:16] + sums[16:24]
    turned = jnp.concatenate(
        [rows[:, k * devices : (k + 1) * devices] for k in range(CAP)], axis=0
    )
    out_ref[...] = turned.T


def unsort(own, sides, low, high, rank):
    devices = rank.shape[1]
    return pl.pallas_call(
        unsort_kernel,
        out_shape=jax.ShapeDtypeStruct((devices, CAP * 8), F32),
        in_specs=[vmem()] * 5,
        out_specs=vmem(),
        compiler_params=params(),
        cost_estimate=cost(10**9, 300_000),
        name="unsort",
    )(own, sides, low, high, rank)


def unpack_kernel(owner_ref, rank_ref, back_ref, out_ref):
    markers = owner_ref.shape[1]
    devices = back_ref.shape[0]
    onehot = (iota((devices, markers), 0) == owner_ref[...]).astype(F32).astype(BF16)
    rank = rank_ref[...]
    turned = back_ref[...].T
    picked = None
    for part in split3(turned):
        term = nn(part.astype(BF16), onehot)
        picked = term if picked is None else picked + term
    total = jnp.zeros((8, markers), F32)
    for k in range(CAP):
        total = total + jnp.where(rank == k, picked[k * 8 : (k + 1) * 8], 0.0)
    out_ref[...] = total[0:3]


def unpack(owner_row, rank, back):
    markers = owner_row.shape[1]
    return pl.pallas_call(
        unpack_kernel,
        out_shape=jax.ShapeDtypeStruct((3, markers), F32),
        in_specs=[vmem()] * 3,
        out_specs=vmem(),
        compiler_params=params(),
        cost_estimate=cost(10**8, 100_000),
        name="unpack",
    )(owner_row, rank, back)


def shift_up(x, axis):
    count = lax.axis_size(axis)
    return lax.ppermute(x, axis, [(i, (i + 1) % count) for i in range(count)])


def shift_down(x, axis):
    count = lax.axis_size(axis)
    return lax.ppermute(x, axis, [((i + 1) % count, i) for i in range(count)])


def shards(velocity, viscosity, cells, offsets, forces, owners):
    devices = lax.axis_size("gx") * lax.axis_size("gy")
    size_x, size_y, depth = viscosity.shape
    markers = owners.shape[0]
    owner_row = owners.reshape(1, markers)
    both = ("gx", "gy")

    x_low_first = shift_up(velocity[0, size_x - HALO : size_x - HALO + X_FIRST], "gx")
    x_high_first = shift_down(velocity[0, 0:X_FIRST], "gx")
    outgoing, rank = pack(owner_row, cells, offsets, forces, devices)
    outgoing, face_source = lax.optimization_barrier((outgoing, viscosity))
    received = lax.all_to_all(outgoing, both, split_axis=0, concat_axis=0, tiled=True)
    x_up, x_down, y_up, y_down, x_up_late, x_down_late = faces(velocity, face_source)
    received, x_low_first, x_high_first, x_up, x_down, y_up, y_down = lax.optimization_barrier(
        (received, x_low_first, x_high_first, x_up, x_down, y_up, y_down)
    )
    x_low = shift_up(x_up, "gx")
    x_high = shift_down(x_down, "gx")
    y_low = shift_up(y_up, "gy")
    y_high = shift_down(y_down, "gy")
    markers_list, order = sort(received, depth)
    markers_list, x_low, x_high, y_low, y_high = lax.optimization_barrier(
        (markers_list, x_low, x_high, y_low, y_high)
    )
    list_low = shift_up(markers_list, "gx")
    list_high = shift_down(markers_list, "gx")
    x_up_late, x_down_late = late_faces(x_up_late, x_down_late, y_low, y_high, size_x)
    mid = jnp.stack([list_low, markers_list, list_high])
    mid, x_up_late, x_down_late = lax.optimization_barrier((mid, x_up_late, x_down_late))
    x_low_late = shift_up(x_up_late, "gx")
    x_high_late = shift_down(x_down_late, "gx")
    low = shift_up(mid, "gy")
    high = shift_down(mid, "gy")
    halos = (x_low_first, x_high_first, x_low, x_high, x_low_late, x_high_late, y_low, y_high)
    meta_mid = mid[:, 10, 0:64].astype(I32)
    meta_mid = jnp.pad(meta_mid, ((3, 3), (0, 0)))
    spread_own = spread_mid(meta_mid, mid, size_x, size_y, depth)
    low, high, spread_own = lax.optimization_barrier((low, high, spread_own))
    meta = jnp.concatenate([part[:, 10, 0:64] for part in (low, mid, high)], axis=0).astype(I32)
    spreads = (spread_own, *spread_side(meta, low, high, size_x, size_y, depth))
    halos, spreads = lax.optimization_barrier((halos, spreads))
    field, part_low, part_high = solve(
        3, meta, spreads, velocity, viscosity, halos, (low, high)
    )
    beside = sample(meta, mid, field, (-1, 1))
    sides = shift_down(part_low, "gy") + shift_up(part_high, "gy")
    to_low = sides[0:3] + beside[0, 0:3]
    to_high = sides[6:9] + beside[1, 0:3]
    to_low, to_high, field_own = lax.optimization_barrier((to_low, to_high, field))
    own = sample(meta, mid, field_own, (0,))
    back = unsort(own, sides, shift_down(to_low, "gx"), shift_up(to_high, "gx"), order)
    back = lax.all_to_all(back, both, split_axis=0, concat_axis=0, tiled=True)
    return (field, unpack(owner_row, rank, back))


def solution(mesh):
    in_specs = (
        P(None, "gx", "gy", None),
        P("gx", "gy", None),
        P(None, ("gx", "gy")),
        P(None, ("gx", "gy")),
        P(None, ("gx", "gy")),
        P(("gx", "gy"), None),
    )
    out_specs = (P(None, "gx", "gy", None), P(None, ("gx", "gy")))
    return jax.shard_map(shards, mesh=mesh, in_specs=in_specs, out_specs=out_specs, check_vma=False)
```
